256 devices in a mesh: bx: 16 (over z, y_lo), by: 4 (over x), view: 4 (over y_hi, core).
Axes of the slice: x: 4, y: 4 (y_hi: 2, y_lo: 2; y = y_hi * 2 + y_lo), z: 8, core: 2. Of those that a mesh axis runs over, the one named last changes fastest.
Arguments:
- estimate: float32 [512, 128, 128], P('bx', 'by'), may hold values from 0.5 to 2
- views_raw: float32 [4, 512, 128, 128], P('view', 'bx', 'by'), as said below
- psf_taps: float32 [4, 3, 31], P('view'), may hold values from 0.05 to 1
- offsets: int32 [4, 16, 4, 3], P('view', 'bx', 'by'), may hold values from -8 to 8
- view_weights: int32 [4, 16, 4], P(None, 'bx', 'by'), may hold values from 1 to 8
Outputs:
- estimate_next: float32 [512, 128, 128], P('bx', 'by')
The draws below stay inside these ranges and needn't reach their ends.
Inputs may be any that keep to these rules, and one draw needn't show every extreme that they name: `views_raw`: every entry is positive.
All inputs are finite; a program needn't handle non-finite values.
Results may differ from the reference program's by a relative error of at most 0.0003.
Values sent between devices are 32-bit elements; how exact they have to be, the bound alone decides.
A program may use at most 128 MiB of HBM per device.

```python
import math
import jax
import jax.numpy as jnp
from jax import lax

CX = 32
CY = 32
CZ = 128
ITERS = 2
TAPS = 31
SHIFT = 8
VIEWS = 4
BLOCKS_X = 16
BLOCKS_Y = 4
NX = 512
NY = 128
NZ = 128


def draw_views_raw(key, part):
    key = jax.random.fold_in(key, 11)
    noise_key, view_key = jax.random.split(key)
    noise = jnp.exp(jax.random.uniform(noise_key, (VIEWS, NX, NY, NZ), jnp.float32, -1.2, 1.2))
    view_scale = jnp.exp(jax.random.uniform(view_key, (VIEWS, 1, 1, 1), jnp.float32, -0.7, 0.7))
    strength = 0.5
    coords = jnp.arange(NX, dtype=jnp.float32)[None, :, None, None]
    region = jnp.exp(strength * jnp.sin(18.85 * coords / NX))
    return noise * view_scale * region


def touch_ends(drawn, rng, low, high):
    spot = [jax.random.randint(jax.random.fold_in(rng, axis), (), 0, length) for axis, length in enumerate(drawn.shape)]
    widest = drawn.shape.index(max(drawn.shape))
    neighbour = spot[:widest] + [(spot[widest] + 1) % drawn.shape[widest]] + spot[widest + 1:]
    return drawn.at[tuple(spot)].set(low).at[tuple(neighbour)].set(high)


def levels(key, dims, shards, smallest, top_value):
    def one(dim, shards_of):
        heights = jax.random.uniform(jax.random.fold_in(jax.random.fold_in(key, 6), dim), (shards_of,), jnp.float32, smallest / len(shards), top_value / len(shards))
        return jnp.repeat(jnp.exp(heights), dims[dim] // shards_of).reshape((-1,) + (1,) * (len(dims) - dim - 1))

    gain = one(*shards[0])
    for cut in shards[1:]:
        gain = gain * one(*cut)
    return gain


def setup_inputs(seed: int = 0) -> dict:
    arg_keys = jax.random.split(jax.random.key(seed), 6)
    estimate = jnp.clip(jnp.exp(math.log(2.0) - 1.3862944 * jax.random.uniform(arg_keys[0], (NX, NY, NZ), jnp.float32) ** levels(arg_keys[0], (NX, NY, NZ), ((0, 16), (1, 4)), -0.2, 0.2)), 0.5, 2.0)
    views_raw = draw_views_raw(jax.random.fold_in(arg_keys[5], 71), 0)
    psf_taps = jnp.clip(jnp.exp(math.log(1.0) - 2.9957323 * jax.random.uniform(arg_keys[2], (VIEWS, 3, TAPS), jnp.float32) ** levels(arg_keys[2], (VIEWS, 3, TAPS), ((0, 4),), -0.2, 0.2)), 0.05, 1.0)
    offsets = touch_ends(jax.random.randint(arg_keys[3], (VIEWS, BLOCKS_X, BLOCKS_Y, 3), -SHIFT, SHIFT + 1), jax.random.fold_in(arg_keys[3], 1), -SHIFT, SHIFT).astype(jnp.int32)
    view_weights = touch_ends(jax.random.randint(arg_keys[4], (VIEWS, BLOCKS_X, BLOCKS_Y), 1, 9), jax.random.fold_in(arg_keys[4], 1), 1, 8).astype(jnp.int32)
    return {"estimate": estimate, "views_raw": views_raw, "psf_taps": psf_taps, "offsets": offsets, "view_weights": view_weights}


def band(kernel_row, length):
    half = (TAPS - 1) // 2
    distance = jnp.arange(length, dtype=jnp.int32)[:, None] - jnp.arange(length, dtype=jnp.int32)[None, :] + half
    matrix = jnp.zeros((length, length), kernel_row.dtype)
    for position in range(TAPS):
        matrix = matrix + jnp.where(distance == position, kernel_row[position], jnp.zeros((), kernel_row.dtype))
    return matrix


def blur(field, kernel):
    along_x = jnp.einsum("abc,ai->ibc", field, band(kernel[0], NX), precision=lax.Precision.HIGHEST)
    along_y = jnp.einsum("abc,bi->aic", along_x, band(kernel[1], NY), precision=lax.Precision.HIGHEST)
    return jnp.einsum("abc,ci->abi", along_y, band(kernel[2], NZ), precision=lax.Precision.HIGHEST)


def align(recorded, shifts):
    padded = jnp.pad(recorded, SHIFT)
    block_rows = jnp.arange(BLOCKS_X, dtype=jnp.int32)
    block_cols = jnp.arange(BLOCKS_Y, dtype=jnp.int32)

    def one_block(block_row, block_col):
        offset = shifts[block_row, block_col].astype(jnp.int32)
        start_x = (block_row * CX + SHIFT + offset[0]).astype(jnp.int32)
        start_y = (block_col * CY + SHIFT + offset[1]).astype(jnp.int32)
        start_z = (SHIFT + offset[2]).astype(jnp.int32)
        piece = lax.dynamic_slice(padded, (start_x, start_y, start_z), (CX, CY, CZ))
        global_x = block_row * CX + offset[0] + jnp.arange(CX, dtype=jnp.int32)
        global_y = block_col * CY + offset[1] + jnp.arange(CY, dtype=jnp.int32)
        global_z = offset[2] + jnp.arange(CZ, dtype=jnp.int32)
        inside = (((global_x >= 0) & (global_x < NX))[:, None, None]
                  & ((global_y >= 0) & (global_y < NY))[None, :, None]
                  & ((global_z >= 0) & (global_z < NZ))[None, None, :])
        return piece, inside

    pieces, insides = jax.vmap(lambda row: jax.vmap(lambda col: one_block(row, col))(block_cols))(block_rows)
    pieces = pieces.transpose(0, 2, 1, 3, 4).reshape(NX, NY, NZ)
    insides = insides.transpose(0, 2, 1, 3, 4).reshape(NX, NY, NZ)
    return pieces, insides


def reference(estimate, views_raw, psf_taps, offsets, view_weights):
    kernels = psf_taps / jnp.sum(psf_taps, axis=-1, keepdims=True)
    aligned_list = []
    inside_list = []
    for view_index in range(VIEWS):
        aligned, inside = align(views_raw[view_index], offsets[view_index])
        aligned_list.append(aligned)
        inside_list.append(inside)
    weights = view_weights.astype(jnp.float32)
    spread = jnp.repeat(jnp.repeat(weights, CX, axis=1), CY, axis=2)[..., None]
    weight_total = jnp.sum(spread, axis=0)
    current = estimate
    for iteration in range(ITERS):
        log_sum = jnp.zeros((NX, NY, NZ), jnp.float32)
        for view_index in range(VIEWS):
            blurred = blur(current, kernels[view_index])
            ratio = jnp.where(inside_list[view_index], aligned_list[view_index] / blurred, 1.0)
            back = blur(ratio, kernels[view_index][:, ::-1])
            log_sum = log_sum + spread[view_index] * jnp.log(back)
        current = current * jnp.exp(log_sum / weight_total)
    return current
```

```python
import functools

import jax
import jax.numpy as jnp
from jax import lax
from jax.experimental import pallas as pl
from jax.experimental.pallas import tpu as pltpu
from jax.sharding import PartitionSpec as P

ITERS = 2
TAPS = 31
HALF = 15
SHIFT = 8
CX, CY, CZ = 32, 32, 128
PADY = 16
WIDE_X = CX + 2 * HALF
WIDE_Y = CY + 2 * PADY
STEP = 8
STEPS = CX // STEP
N_SEMS = 64
MESH = pl.DeviceIdType.MESH


def split(value):
    high = value.astype(jnp.bfloat16)
    low = (value - high.astype(jnp.float32)).astype(jnp.bfloat16)
    return high, low


def kernel(
    sizes,
    est, view, psf, off, wts,
    out,
    xf, yf, yb, xb, logs, parts, wide, own_aligned, aligned, own_params, params,
    taps, band_y, band_z,
    send_sem, recv_sem,
):
    nz, nx = sizes
    bx, by, vw = lax.axis_index("bx"), lax.axis_index("by"), lax.axis_index("view")
    zc, y_lo = lax.div(bx, 2), lax.rem(bx, 2)
    y_hi, core = lax.div(vw, 2), lax.rem(vw, 2)
    y = 2 * y_hi + y_lo
    other = 1 - core
    stays = y_lo == core

    def dev(zc_, x_, y_, core_):
        return (zc_ * 2 + lax.rem(y_, 2), x_, lax.div(y_, 2) * 2 + core_)

    x_left = dev(lax.rem(zc + nz - other, nz), by, y, other)
    x_right = dev(lax.rem(zc + core, nz), by, y, other)
    y_left = (bx, lax.rem(by + nx - 1, nx), vw)
    y_right = (bx, lax.rem(by + 1, nx), vw)
    ring = [None] + [dev(zc, by, lax.rem(y + d, 4), core) for d in (1, 2, 3)]
    ring_other = [dev(zc, by, lax.rem(y + d, 4), other) for d in (0, 1, 2, 3)]
    partner = dev(zc, by, 2 * y_hi + 1 - y_lo, other)
    raw_left = (lax.rem(bx + 2 * nz - 1, 2 * nz), by, vw)
    raw_right = (lax.rem(bx + 1, 2 * nz), by, vw)
    raw_far = (
        lax.rem(bx + 2 * nz + jnp.where(y_lo == 0, -1, 1), 2 * nz), by, vw)
    far_x = dev(jnp.where(core == 0, lax.rem(zc + nz - 1, nz), lax.rem(zc + 1, nz)), by, y, other)

    barrier = pltpu.get_barrier_semaphore()
    peers = ring[1:] + ring_other + [far_x, y_left, y_right, raw_far]
    for peer in peers:
        pl.semaphore_signal(barrier, inc=1, device_id=peer, device_id_type=MESH)
    pl.semaphore_wait(barrier, len(peers))

    used = [0]
    sent = []

    def new_sem(count=1):
        first = used[0]
        used[0] += count
        return first

    def remote(src, dst, sem, device):
        return pltpu.make_async_remote_copy(
            src_ref=src, dst_ref=dst, send_sem=send_sem.at[sem], recv_sem=recv_sem.at[sem],
            device_id=device, device_id_type=MESH)

    def go(src, dst, device):
        copy = remote(src, dst, new_sem(), device)
        copy.start()
        sent.append(copy)
        return copy

    first = xf[0]
    half = CX // 2
    est_sems = new_sem(2)
    est_copies = [
        remote(est.at[pl.ds(0, half)], first.at[pl.ds(HALF, half)], est_sems, ring_other[3]),
        remote(est.at[pl.ds(half, half)], first.at[pl.ds(HALF + half, half)], est_sems + 1,
               ring_other[1]),
    ]
    params_copy = remote(own_params, params, new_sem(), partner)

    own_params[...] = jnp.zeros((8, 128), jnp.float32)
    row = psf[0]
    own_params[0:3, 0:TAPS] = row / jnp.sum(row, axis=-1, keepdims=True)
    for v in range(4):
        own_params[4 + v : 5 + v, :] = jnp.full((1, 128), wts[v, 0, 0].astype(jnp.float32))

    @pl.when(jnp.logical_not(stays))
    def _():
        params_copy.start()
        for copy in est_copies:
            copy.start()

    @pl.when(stays)
    def _():
        params[...] = own_params[...]
        first[HALF : HALF + CX] = est[...]

    wide[SHIFT : SHIFT + CX, SHIFT : SHIFT + CY, :] = view[0]
    rows = pl.ds(SHIFT, CY)
    raw_x = [
        go(view.at[0, pl.ds(0, SHIFT)], wide.at[pl.ds(SHIFT + CX, SHIFT), rows], raw_left),
        go(view.at[0, pl.ds(CX - SHIFT, SHIFT)], wide.at[pl.ds(0, SHIFT), rows], raw_right),
    ]

    @pl.when(jnp.logical_not(stays))
    def _():
        params_copy.wait()
        for copy in est_copies:
            copy.wait()

    def send_x(field):
        return [
            go(field.at[pl.ds(HALF, HALF)], field.at[pl.ds(HALF + CX, HALF)], x_left),
            go(field.at[pl.ds(CX, HALF)], field.at[pl.ds(0, HALF)], x_right),
        ]

    def wait_x(field, copies):
        for copy in copies:
            copy.wait_recv()

        @pl.when((zc == 0) & (core == 0))
        def _():
            field[0:HALF] = jnp.zeros((HALF, CY, CZ), jnp.float32)

        @pl.when((zc == nz - 1) & (core == 1))
        def _():
            field[HALF + CX :] = jnp.zeros((HALF, CY, CZ), jnp.float32)

    def send_y(field, step):
        planes = pl.ds(step * STEP, STEP)
        return [
            go(field.at[planes, pl.ds(PADY, PADY)], field.at[planes, pl.ds(PADY + CY, PADY)], y_left),
            go(field.at[planes, pl.ds(CY, PADY)], field.at[planes, pl.ds(0, PADY)], y_right),
        ]

    x_copies = send_x(first)

    for t in range(TAPS):
        taps[t] = jnp.broadcast_to(params[0:1, t : t + 1], (8, CZ))

    r = lax.broadcasted_iota(jnp.int32, (CY, 4 * WIDE_Y), 0)
    c = lax.broadcasted_iota(jnp.int32, (CY, 4 * WIDE_Y), 1)
    group, c = lax.div(c, WIDE_Y), lax.rem(c, WIDE_Y)
    distance = c - r - 1
    outside = ((by == 0) & (c < PADY)) | ((by == nx - 1) & (c >= PADY + CY))
    forward = jnp.zeros((CY, 4 * WIDE_Y), jnp.float32)
    backward = forward
    for t in range(TAPS):
        tap = params[1:2, t : t + 1]
        forward = jnp.where(distance == t, tap, forward)
        backward = jnp.where(distance == TAPS - 1 - t, tap, backward)
    for k, band in enumerate((forward, backward)):
        high, low = split(jnp.where(outside, 0.0, band))
        band_y[k] = jnp.where(group < 2, high.astype(jnp.float32), low.astype(jnp.float32)).astype(
            jnp.bfloat16)
    r = lax.broadcasted_iota(jnp.int32, (CZ, CZ), 0)
    c = lax.broadcasted_iota(jnp.int32, (CZ, CZ), 1)
    distance = r - c + HALF
    forward = jnp.zeros((CZ, CZ), jnp.float32)
    backward = forward
    for t in range(TAPS):
        tap = params[2:3, t : t + 1]
        forward = jnp.where(distance == t, tap, forward)
        backward = jnp.where(distance == TAPS - 1 - t, tap, backward)
    for k, band in enumerate((forward, backward)):
        high, low = split(band)
        for part in range(2):
            band_z[k, part * CZ : (part + 1) * CZ, 0:CZ] = high
            band_z[k, part * CZ : (part + 1) * CZ, CZ : 2 * CZ] = low

    for copy in raw_x:
        copy.wait_recv()
    raw_y = [
        go(wide.at[:, pl.ds(SHIFT, SHIFT)], wide.at[:, pl.ds(SHIFT + CY, SHIFT)], y_left),
        go(wide.at[:, pl.ds(CY, SHIFT)], wide.at[:, pl.ds(0, SHIFT)], y_right),
    ]

    def conv_x(field, start, tile, flip):
        weights = [taps[TAPS - 1 - t if flip else t] for t in range(TAPS)]
        sums = [None] * STEP
        for a in range(STEP + TAPS - 1):
            value = field[start + a, pl.ds(tile, 8), :]
            for i in range(STEP):
                if 0 <= a - i < TAPS:
                    term = weights[a - i] * value
                    sums[i] = term if sums[i] is None else sums[i] + term
        return sums

    def conv_y(field, step, k):
        blocks = []
        for p in range(0, STEP, 2):
            pair = jnp.concatenate([field[step * STEP + p], field[step * STEP + p + 1]], axis=1)
            high, low = split(pair)
            stacked = jnp.concatenate([high, low, high, low], axis=0)
            both = jnp.dot(band_y[k], stacked, preferred_element_type=jnp.float32)
            blocks += [both[:, :CZ], both[:, CZ:]]
        return jnp.concatenate(blocks, axis=0)

    def conv_z(value, k):
        both = jnp.concatenate(split(value), axis=1)
        summed = jnp.dot(both, band_z[k], preferred_element_type=jnp.float32)
        return summed[:, :CZ] + summed[:, CZ:]

    def align():
        for copy in raw_y:
            copy.wait_recv()
        ox, oy, oz = off[0, 0, 0, 0], off[0, 0, 0, 1], off[0, 0, 0, 2]
        gy = by * CY + oy + lax.broadcasted_iota(jnp.int32, (CY, CZ), 0)
        gz = oz + lax.broadcasted_iota(jnp.int32, (CY, CZ), 1)
        inside = (gy >= 0) & (gy < nx * CY) & (gz >= 0) & (gz < CZ)
        turn = lax.rem(CZ - oz, CZ)

        def plane(p, carry):
            value = wide[SHIFT + ox + p, pl.ds(SHIFT + oy, CY), :]
            value = pltpu.roll(value, turn, 1)
            gx = bx * CX + ox + p
            ok = inside & (gx >= 0) & (gx < 2 * nz * CX)
            own_aligned[p] = jnp.where(ok, value, -1.0)
            return carry

        lax.fori_loop(0, CX, plane, 0)

        @pl.when(jnp.logical_not(stays))
        def _():
            aligned_copy.start()

        @pl.when(stays)
        def _():
            aligned[...] = own_aligned[...]

    aligned_copy = remote(own_aligned, aligned, new_sem(), partner)

    def wait_aligned():
        @pl.when(jnp.logical_not(stays))
        def _():
            aligned_copy.wait()

    total = params[4:5, :] + params[5:6, :] + params[6:7, :] + params[7:8, :]
    own_weight = params[pl.ds(4 + y, 1), :]

    for iteration in range(ITERS):
        field = xf[iteration]
        wait_x(field, x_copies)
        ahead, back = yf[iteration], yb[iteration]
        ahead_copies, back_copies = [], []
        for step in range(STEPS):

            def tile(j, carry, step=step, field=field, ahead=ahead):
                sums = conv_x(field, step * STEP, 8 * j, False)
                for i in range(STEP):
                    ahead[step * STEP + i, pl.ds(pl.multiple_of(PADY + 8 * j, 8), 8), :] = sums[i]
                return carry

            lax.fori_loop(0, CY // 8, tile, 0)
            ahead_copies.append(send_y(ahead, step))
        if iteration == 0:
            align()
            wait_aligned()
        for step in range(STEPS):
            for copy in ahead_copies[step]:
                copy.wait_recv()
            blurred = conv_z(conv_y(ahead, step, 0), 0)
            recorded = aligned[step * STEP : (step + 1) * STEP].reshape(STEP * CY, CZ)
            ratio = jnp.where(recorded >= 0.0, recorded / blurred, 1.0)
            back[step * STEP : (step + 1) * STEP, PADY : PADY + CY, :] = conv_z(ratio, 1).reshape(
                STEP, CY, CZ)
            back_copies.append(send_y(back, step))
        field_back = xb[iteration]
        x_copies = []
        for step in range(STEPS):
            for copy in back_copies[step]:
                copy.wait_recv()
            field_back[HALF + step * STEP : HALF + (step + 1) * STEP] = conv_y(back, step, 1).reshape(
                STEP, CY, CZ)
        x_copies = send_x(field_back)
        wait_x(field_back, x_copies)
        slots = parts[iteration]
        mine = logs[iteration]
        sum_copies = []
        for d in (2, 1, 3, 0):
            start = lax.rem(y + d, 4) * STEP

            def tile_back(j, carry, start=start, field=field_back, d=d, slots=slots, mine=mine):
                sums = conv_x(field, start, 8 * j, True)
                for i in range(STEP):
                    mine[d * STEP + i, pl.ds(pl.multiple_of(8 * j, 8), 8), :] = own_weight * jnp.log(
                        sums[i])
                return carry

            lax.fori_loop(0, CY // 8, tile_back, 0)
            if d:
                sum_copies.append(go(mine.at[pl.ds(d * STEP, STEP)], slots.at[d], ring[d]))
        for copy in sum_copies:
            copy.wait_recv()
        log_sum = mine[0:STEP] + slots[1] + slots[2] + slots[3]
        updated = field[pl.ds(HALF + y * STEP, STEP)] * jnp.exp(log_sum / total[None])
        if iteration + 1 < ITERS:
            following = xf[iteration + 1]
            shard = following.at[pl.ds(HALF + y * STEP, STEP)]
            shard[...] = updated
            copies = [go(shard, shard, ring[d]) for d in (2, 1, 3)]
            for copy in copies:
                copy.wait_recv()
            x_copies = send_x(following)
        else:
            own = out.at[pl.ds(y * STEP, STEP)]
            base = new_sem(4)
            shard = logs[iteration].at[pl.ds(0, STEP)]
            shard[...] = updated
            results = []
            for n in range(4):
                to_y, to_core = core + 2 * (n // 2), n % 2
                me = (to_y == y) & (to_core == core)
                result = pltpu.make_async_remote_copy(
                    src_ref=shard, dst_ref=own, send_sem=send_sem.at[base + n],
                    recv_sem=recv_sem.at[base + y], device_id=dev(zc, by, to_y, to_core),
                    device_id_type=MESH)
                results.append((me, result))

                @pl.when(jnp.logical_not(me))
                def _(result=result):
                    result.start()

            @pl.when(stays)
            def _():
                own[...] = updated

            for n in range(4):
                at = out.at[pl.ds(n * STEP, STEP)]

                @pl.when(jnp.logical_not(stays & (y == n)))
                def _(at=at, n=n):
                    remote(at, at, base + n, partner).wait_recv()

            for me, result in results:

                @pl.when(jnp.logical_not(me))
                def _(result=result):
                    result.wait_send()

    for copy in sent:
        copy.wait_send()


def solution(mesh):
    nz, nx = mesh.shape["bx"] // 2, mesh.shape["by"]
    f32 = jnp.float32

    def shards(estimate, views_raw, psf_taps, offsets, view_weights):
        x_field = pltpu.VMEM((WIDE_X, CY, CZ), f32)
        y_field = pltpu.VMEM((CX, WIDE_Y, CZ), f32)
        block = pltpu.VMEM((CX, CY, CZ), f32)
        vmem = pl.BlockSpec(memory_space=pltpu.VMEM)
        smem = pl.BlockSpec(memory_space=pltpu.SMEM)
        return pl.pallas_call(
            functools.partial(kernel, (nz, nx)),
            out_shape=jax.ShapeDtypeStruct((CX, CY, CZ), f32),
            in_specs=[vmem, vmem, vmem, smem, smem],
            out_specs=vmem,
            scratch_shapes=[
                [x_field] * ITERS,
                [y_field] * ITERS,
                [y_field] * ITERS,
                [x_field] * ITERS,
                [block] * ITERS,
                [pltpu.VMEM((4, STEP, CY, CZ), f32)] * ITERS,
                pltpu.VMEM((CX + 2 * SHIFT, CY + 2 * SHIFT, CZ), f32),
                block,
                block,
                pltpu.VMEM((8, 128), f32),
                pltpu.VMEM((8, 128), f32),
                pltpu.VMEM((TAPS, 8, CZ), f32),
                pltpu.VMEM((2, CY, 4 * WIDE_Y), jnp.bfloat16),
                pltpu.VMEM((2, 2 * CZ, 2 * CZ), jnp.bfloat16),
                pltpu.SemaphoreType.DMA((N_SEMS,)),
                pltpu.SemaphoreType.DMA((N_SEMS,)),
            ],
            compiler_params=pltpu.CompilerParams(
                collective_id=0, has_side_effects=True, vmem_limit_bytes=40 * 1024 * 1024
            ),
            cost_estimate=pl.CostEstimate(flops=10**9, bytes_accessed=2 * 10**6, transcendentals=10**6),
        )(estimate, views_raw, psf_taps, offsets, view_weights)

    return jax.shard_map(
        shards,
        mesh=mesh,
        in_specs=(
            P("bx", "by", None),
            P("view", "bx", "by", None),
            P("view", None, None),
            P("view", "bx", "by", None),
            P(None, "bx", "by"),
        ),
        out_specs=P("bx", "by", None),
        check_vma=False,
    )
```

```python
import functools

import jax
import jax.numpy as jnp
from jax import lax
from jax.experimental import pallas as pl
from jax.experimental.pallas import tpu as pltpu
from jax.sharding import PartitionSpec as P

ITERS = 2
TAPS = 31
HALF = 15
SHIFT = 8
VIEWS = 4
CX, CY, CZ = 32, 32, 128
PX, PY = 16, 16
WIDE_X = PX + 2 * HALF
WIDE_Y = 3 * PY
N_SEMS = 96
MESH = pl.DeviceIdType.MESH


def split(value):
    high = value.astype(jnp.bfloat16)
    low = (value - high.astype(jnp.float32)).astype(jnp.bfloat16)
    return high, low


def kernel(
    sizes,
    est, view, psf, off, wts,
    out,
    xf, yf, xb, yb, summed, result, wide, own_aligned, aligned, own_params, params,
    taps, band_y, band_z,
    send_sem, recv_sem, local_sem,
):
    nz, nx = sizes
    bx, by, vw = lax.axis_index("bx"), lax.axis_index("by"), lax.axis_index("view")
    zc, y_lo = lax.div(bx, 2), lax.rem(bx, 2)
    y_hi, core = lax.div(vw, 2), lax.rem(vw, 2)
    y = 2 * y_hi + y_lo
    other = 1 - core
    pos = jnp.where(lax.rem(zc, 2) == 0, y, 3 - y)
    side, part = lax.div(pos, 2), lax.rem(pos, 2)
    stays = side == y_lo

    def dev(zc_, x_, y_, core_):
        return (zc_ * 2 + lax.rem(y_, 2), x_, lax.div(y_, 2) * 2 + core_)

    def chip_at(zc_, pos_):
        return jnp.where(lax.rem(zc_, 2) == 0, pos_, 3 - pos_)

    def along_x(step):
        place = lax.rem(4 * zc + pos + 4 * nz + step, 4 * nz)
        zc_, pos_ = lax.div(place, 4), lax.rem(place, 4)
        return dev(zc_, by, chip_at(zc_, pos_), core)

    def along_y(step):
        place = lax.rem(2 * by + core + 2 * nx + step, 2 * nx)
        return dev(zc, lax.div(place, 2), y, lax.rem(place, 2))

    x_left, x_right = along_x(-1), along_x(1)
    y_left, y_right = along_y(-1), along_y(1)
    first_x, last_x = (zc == 0) & (pos == 0), (zc == nz - 1) & (pos == 3)
    first_y, last_y = (by == 0) & (core == 0), (by == nx - 1) & (core == 1)

    def raw(step_x, step_y):
        return (lax.rem(bx + 2 * nz + step_x, 2 * nz), lax.rem(by + nx + step_y, nx), vw)

    far_y = dev(zc, lax.rem(by + nx + jnp.where(core == 0, -1, 1), nx), y, other)
    raw_far = raw(jnp.where(y_lo == 0, -1, 1), 0)
    barrier = pltpu.get_barrier_semaphore()
    peers = [dev(zc, by, lax.rem(y + d, 4), core) for d in (1, 2, 3)]
    peers += [dev(zc, by, lax.rem(y + d, 4), other) for d in (0, 1, 2, 3)]
    peers += [dev(lax.rem(zc + nz + d, nz), by, y, core) for d in (-1, 1)]
    peers += [far_y, raw_far, raw(0, -1), raw(0, 1)]
    peers += [raw(i, j) for i in (-1, 1) for j in (-1, 1)]
    for peer in peers:
        pl.semaphore_signal(barrier, inc=1, device_id=peer, device_id_type=MESH)

    used = [0]
    sent = []

    def new_sem(count=1):
        first = used[0]
        used[0] += count
        return first

    def remote(src, dst, sem, device, at=None):
        return pltpu.make_async_remote_copy(
            src_ref=src, dst_ref=dst, send_sem=send_sem.at[sem],
            recv_sem=recv_sem.at[sem if at is None else at],
            device_id=device, device_id_type=MESH)

    def go(src, dst, device):
        copy = remote(src, dst, new_sem(), device)
        copy.start()
        sent.append(copy)
        return copy

    def piece(n):
        return pl.ds(n * PX, PX)

    def spread(source_at, target, own_store):
        base = new_sem(4)
        copies = []
        for r in range(4):
            y_, core_ = chip_at(zc, 2 * y_lo + r // 2), r % 2
            me = (y_ == y) & (core_ == core)
            copy = remote(source_at(r), target(vw), base + r, dev(zc, by, y_, core_), base + vw)
            copies.append((me, copy))

        def start():
            for me, copy in copies:
                pl.when(jnp.logical_not(me))(copy.start)

            @pl.when(stays)
            def _():
                own_store()

        def wait(s):
            @pl.when(jnp.logical_not(stays & (vw == s)))
            def _():
                remote(target(s), target(s), base + s, x_left).wait_recv()

        def finish():
            for me, copy in copies:
                pl.when(jnp.logical_not(me))(copy.wait_send)

        return start, wait, finish

    local_view = pltpu.make_async_copy(
        view.at[0], wide.at[pl.ds(SHIFT, CX), pl.ds(SHIFT, CY)], local_sem.at[0])
    local_view.start()
    own_block = xf.at[0, pl.ds(HALF, PX)]
    local_est = pltpu.make_async_copy(
        est.at[piece(part), piece(core)], own_block, local_sem.at[1])
    pl.when(stays)(local_est.start)
    pair = jnp.where(y_lo == 0, lax.rem(y + 3, 4), lax.rem(y + 1, 4))
    pair_part = lax.rem(jnp.where(lax.rem(zc, 2) == 0, pair, 3 - pair), 2)
    est_copy = remote(
        est.at[piece(pair_part), piece(core)], own_block, new_sem(), dev(zc, by, pair, core))

    own_params[...] = jnp.zeros((8, 128), jnp.float32)
    row = psf[0]
    own_params[0:3, 0:TAPS] = row / jnp.sum(row, axis=-1, keepdims=True)
    for v in range(VIEWS):
        own_params[4 + v : 5 + v, :] = jnp.full((1, 128), wts[v, 0, 0].astype(jnp.float32))

    def store_params():
        params[vw] = own_params[...]

    params_start, params_wait, params_finish = spread(
        lambda r: own_params, lambda s: params.at[s], store_params)

    pl.semaphore_wait(barrier, len(peers))
    pl.when(jnp.logical_not(stays))(est_copy.start)
    params_start()
    raw_copies = []
    low, high, middle = pl.ds(0, SHIFT), pl.ds(CX - SHIFT, SHIFT), pl.ds(0, CX)
    to_low, to_high, to_middle = pl.ds(0, SHIFT), pl.ds(SHIFT + CX, SHIFT), pl.ds(SHIFT, CX)
    moves = {-1: (low, to_high), 0: (middle, to_middle), 1: (high, to_low)}
    for i, j in ((-1, 0), (1, 0), (0, -1), (0, 1), (-1, -1), (-1, 1), (1, -1), (1, 1)):
        raw_copies.append(go(
            view.at[0, moves[i][0], moves[j][0]], wide.at[moves[i][1], moves[j][1]], raw(i, j)))

    def send_x(field):
        return [
            go(field.at[pl.ds(HALF, HALF)], field.at[pl.ds(HALF + PX, HALF)], x_left),
            go(field.at[pl.ds(PX, HALF)], field.at[pl.ds(0, HALF)], x_right),
        ]

    def wait_x(field, copies):
        for copy in copies:
            copy.wait_recv()

        @pl.when(first_x)
        def _():
            field[0:HALF] = jnp.zeros((HALF, PY, CZ), jnp.float32)

        @pl.when(last_x)
        def _():
            field[HALF + PX : WIDE_X] = jnp.zeros((HALF, PY, CZ), jnp.float32)

    def send_y(field):
        own = field.at[:, pl.ds(PY, PY)]
        return [
            go(own, field.at[:, pl.ds(2 * PY, PY)], y_left),
            go(own, field.at[:, pl.ds(0, PY)], y_right),
        ]

    pl.when(stays)(local_est.wait)
    pl.when(jnp.logical_not(stays))(est_copy.wait)
    x_copies = send_x(xf.at[0])

    for s in range(VIEWS):
        params_wait(s)

    def build(v, carry):
        for t in range(TAPS):
            taps[v, t] = jnp.broadcast_to(params[v, 0:1, t : t + 1], (8, CZ))
        r = lax.broadcasted_iota(jnp.int32, (PY, 4 * WIDE_Y), 0)
        c = lax.broadcasted_iota(jnp.int32, (PY, 4 * WIDE_Y), 1)
        group, c = lax.div(c, WIDE_Y), lax.rem(c, WIDE_Y)
        distance = c - r - 1
        outside = (first_y & (c < PY)) | (last_y & (c >= 2 * PY))
        forward = jnp.zeros((PY, 4 * WIDE_Y), jnp.float32)
        backward = forward
        for t in range(TAPS):
            tap = params[v, 1:2, t : t + 1]
            forward = jnp.where(distance == t, tap, forward)
            backward = jnp.where(distance == TAPS - 1 - t, tap, backward)
        for k, band in enumerate((forward, backward)):
            upper, lower = split(jnp.where(outside, 0.0, band))
            band_y[k, v] = jnp.where(
                group < 2, upper.astype(jnp.float32), lower.astype(jnp.float32)).astype(jnp.bfloat16)
        r = lax.broadcasted_iota(jnp.int32, (CZ, CZ), 0)
        c = lax.broadcasted_iota(jnp.int32, (CZ, CZ), 1)
        distance = r - c + HALF
        forward = jnp.zeros((CZ, CZ), jnp.float32)
        backward = forward
        for t in range(TAPS):
            tap = params[v, 2:3, t : t + 1]
            forward = jnp.where(distance == t, tap, forward)
            backward = jnp.where(distance == TAPS - 1 - t, tap, backward)
        for k, band in enumerate((forward, backward)):
            upper, lower = split(band)
            for n in range(2):
                band_z[k, v, n * CZ : (n + 1) * CZ, 0:CZ] = upper
                band_z[k, v, n * CZ : (n + 1) * CZ, CZ : 2 * CZ] = lower
        return carry

    lax.fori_loop(0, VIEWS, build, 0)

    def conv_x(field, v, flip, target):
        def tile(j, carry):
            weights = [taps[v, TAPS - 1 - t if flip else t] for t in range(TAPS)]
            sums = [None] * PX
            for a in range(WIDE_X):
                value = field[a, pl.ds(pl.multiple_of(8 * j, 8), 8), :]
                for i in range(PX):
                    if 0 <= a - i < TAPS:
                        term = weights[a - i] * value
                        sums[i] = term if sums[i] is None else sums[i] + term
            for i in range(PX):
                target[i, pl.ds(pl.multiple_of(PY + 8 * j, 8), 8), :] = sums[i]
            return carry

        lax.fori_loop(0, PY // 8, tile, 0)

    def conv_y(field, v, k):
        blocks = []
        for p in range(0, PX, 2):
            both = jnp.concatenate([field[p], field[p + 1]], axis=1)
            upper, lower = split(both)
            stacked = jnp.concatenate([upper, lower, upper, lower], axis=0)
            both = jnp.dot(band_y[k, v], stacked, preferred_element_type=jnp.float32)
            blocks += [both[:, :CZ], both[:, CZ:]]
        return jnp.concatenate(blocks, axis=0)

    def conv_z(value, v, k):
        both = jnp.concatenate(split(value), axis=1)
        both = jnp.dot(both, band_z[k, v], preferred_element_type=jnp.float32)
        return both[:, :CZ] + both[:, CZ:]

    def store_aligned():
        aligned[vw] = own_aligned[piece(part), piece(core), :]

    aligned_start, aligned_wait, aligned_finish = spread(
        lambda r: own_aligned.at[piece(r // 2), piece(r % 2)], lambda s: aligned.at[s], store_aligned)

    def align():
        local_view.wait()
        for copy in raw_copies:
            copy.wait_recv()
        ox, oy, oz = off[0, 0, 0, 0], off[0, 0, 0, 1], off[0, 0, 0, 2]
        gy = by * CY + oy + lax.broadcasted_iota(jnp.int32, (CY, CZ), 0)
        gz = oz + lax.broadcasted_iota(jnp.int32, (CY, CZ), 1)
        inside = (gy >= 0) & (gy < nx * CY) & (gz >= 0) & (gz < CZ)
        turn = lax.rem(CZ - oz, CZ)

        def plane(p, carry):
            value = wide[SHIFT + ox + p, pl.ds(SHIFT + oy, CY), :]
            value = pltpu.roll(value, turn, 1)
            gx = bx * CX + ox + p
            ok = inside & (gx >= 0) & (gx < 2 * nz * CX)
            own_aligned[p] = jnp.where(ok, value, -1.0)
            return carry

        lax.fori_loop(0, CX, plane, 0)
        aligned_start()

    weights = params[0, 4:8, :]
    total = jnp.sum(weights, axis=0, keepdims=True)

    for iteration in range(ITERS):
        field = xf.at[iteration]
        if iteration == 0:
            align()
        wait_x(field, x_copies)
        y_copies = []
        for v in range(VIEWS):
            conv_x(field, v, False, yf.at[iteration, v])
            y_copies.append(send_y(yf.at[iteration, v]))
        xb_copies, yb_copies = [], []
        for v in range(VIEWS):
            for copy in y_copies[v]:
                copy.wait_recv()
            blurred = conv_z(conv_y(yf.at[iteration, v], v, 0), v, 0)
            if iteration == 0:
                aligned_wait(v)
            recorded = aligned[v].reshape(PX * PY, CZ)
            ratio = jnp.where(recorded >= 0.0, recorded / blurred, 1.0)
            back = xb.at[iteration, v]
            back[HALF : HALF + PX] = conv_z(ratio, v, 1).reshape(PX, PY, CZ)
            xb_copies.append(send_x(back))
        for v in range(VIEWS):
            wait_x(xb.at[iteration, v], xb_copies[v])
            conv_x(xb.at[iteration, v], v, True, yb.at[iteration, v])
            yb_copies.append(send_y(yb.at[iteration, v]))
        for v in range(VIEWS):
            for copy in yb_copies[v]:
                copy.wait_recv()
            term = params[0, 4 + v : 5 + v, :] * jnp.log(conv_y(yb.at[iteration, v], v, 1))
            summed[...] = term if v == 0 else summed[...] + term
        update = jnp.exp(summed[...] / total).reshape(PX, PY, CZ)
        updated = field[HALF : HALF + PX] * update
        if iteration + 1 < ITERS:
            xf[iteration + 1, HALF : HALF + PX] = updated
            x_copies = send_x(xf.at[iteration + 1])
        else:
            result[...] = updated
            base = new_sem(4)
            copies = []
            own_target = out.at[piece(part), piece(core)]
            for n in range(4):
                y_, core_ = side + 2 * (n // 2), n % 2
                me = (y_ == y) & (core_ == core)
                copy = remote(result, own_target, base + n, dev(zc, by, y_, core_), base + 2 * part + core)
                copies.append((me, copy))
                pl.when(jnp.logical_not(me))(copy.start)

            @pl.when(stays)
            def _():
                own_target[...] = updated

            for s in range(4):
                target = out.at[piece(s // 2), piece(s % 2)]
                mine = stays & (part == s // 2) & (core == s % 2)

                @pl.when(jnp.logical_not(mine))
                def _(target=target, s=s):
                    remote(target, target, base + s, x_left).wait_recv()

            for me, copy in copies:
                pl.when(jnp.logical_not(me))(copy.wait_send)

    params_finish()
    aligned_finish()
    for copy in sent:
        copy.wait_send()


def solution(mesh):
    nz, nx = mesh.shape["bx"] // 2, mesh.shape["by"]
    f32, bf16 = jnp.float32, jnp.bfloat16

    def shards(estimate, views_raw, psf_taps, offsets, view_weights):
        vmem = pl.BlockSpec(memory_space=pltpu.VMEM)
        smem = pl.BlockSpec(memory_space=pltpu.SMEM)
        hbm = pl.BlockSpec(memory_space=pl.ANY)
        return pl.pallas_call(
            functools.partial(kernel, (nz, nx)),
            out_shape=jax.ShapeDtypeStruct((CX, CY, CZ), f32),
            in_specs=[hbm, hbm, vmem, smem, smem],
            out_specs=vmem,
            scratch_shapes=[
                pltpu.VMEM((ITERS, WIDE_X, PY, CZ), f32),
                pltpu.VMEM((ITERS, VIEWS, PX, WIDE_Y, CZ), f32),
                pltpu.VMEM((ITERS, VIEWS, WIDE_X, PY, CZ), f32),
                pltpu.VMEM((ITERS, VIEWS, PX, WIDE_Y, CZ), f32),
                pltpu.VMEM((PX * PY, CZ), f32),
                pltpu.VMEM((PX, PY, CZ), f32),
                pltpu.VMEM((CX + 2 * SHIFT, CY + 2 * SHIFT, CZ), f32),
                pltpu.VMEM((CX, CY, CZ), f32),
                pltpu.VMEM((VIEWS, PX, PY, CZ), f32),
                pltpu.VMEM((8, 128), f32),
                pltpu.VMEM((VIEWS, 8, 128), f32),
                pltpu.VMEM((VIEWS, TAPS, 8, CZ), f32),
                pltpu.VMEM((2, VIEWS, PY, 4 * WIDE_Y), bf16),
                pltpu.VMEM((2, VIEWS, 2 * CZ, 2 * CZ), bf16),
                pltpu.SemaphoreType.DMA((N_SEMS,)),
                pltpu.SemaphoreType.DMA((N_SEMS,)),
                pltpu.SemaphoreType.DMA((2,)),
            ],
            compiler_params=pltpu.CompilerParams(
                collective_id=0, has_side_effects=True, vmem_limit_bytes=56 * 1024 * 1024
            ),
            cost_estimate=pl.CostEstimate(flops=10**9, bytes_accessed=2 * 10**6, transcendentals=10**6),
        )(estimate, views_raw, psf_taps, offsets, view_weights)

    return jax.shard_map(
        shards,
        mesh=mesh,
        in_specs=(
            P("bx", "by", None),
            P("view", "bx", "by", None),
            P("view", None, None),
            P("view", "bx", "by", None),
            P(None, "bx", "by"),
        ),
        out_specs=P("bx", "by", None),
        check_vma=False,
    )
```

```python
import functools

import jax
import jax.numpy as jnp
from jax import lax
from jax.experimental import pallas as pl
from jax.experimental.pallas import tpu as pltpu
from jax.sharding import PartitionSpec as P

ITERS = 2
TAPS = 31
HALF = 15
SHIFT = 8
VIEWS = 4
CX, CY, CZ = 32, 32, 128
PX, PY = 16, 16
WIDE_X = PX + 2 * HALF
WIDE_Y = 3 * PY
N_SEMS = 128
MESH = pl.DeviceIdType.MESH


def split(value):
    high = value.astype(jnp.bfloat16)
    low = (value - high.astype(jnp.float32)).astype(jnp.bfloat16)
    return high, low


def kernel(
    sizes,
    est, view, psf_hbm, off_hbm, wts_hbm,
    out,
    raw_x, raw_y, x_wide, y_wide, value, summed, result, psf, off, wts, wide, own_aligned, aligned, own_params, params,
    taps, band_y, band_z,
    send_sem, recv_sem, local_sem,
):
    nz, nx = sizes
    bx, by, vw = lax.axis_index("bx"), lax.axis_index("by"), lax.axis_index("view")
    zc, y_lo = lax.div(bx, 2), lax.rem(bx, 2)
    y_hi, core = lax.div(vw, 2), lax.rem(vw, 2)
    y = 2 * y_hi + y_lo
    other = 1 - core
    pos = jnp.where(lax.rem(zc, 2) == 0, y, 3 - y)
    side, part = lax.div(pos, 2), lax.rem(pos, 2)
    stays = side == y_lo

    def dev(zc_, x_, y_, core_):
        return (zc_ * 2 + lax.rem(y_, 2), x_, lax.div(y_, 2) * 2 + core_)

    def chip_at(zc_, pos_):
        return jnp.where(lax.rem(zc_, 2) == 0, pos_, 3 - pos_)

    def along_x(step):
        place = lax.rem(4 * zc + pos + 4 * nz + step, 4 * nz)
        zc_, pos_ = lax.div(place, 4), lax.rem(place, 4)
        return dev(zc_, by, chip_at(zc_, pos_), core)

    def along_y(step):
        place = lax.rem(2 * by + core + 2 * nx + step, 2 * nx)
        return dev(zc, lax.div(place, 2), y, lax.rem(place, 2))

    x_left, x_right = along_x(-1), along_x(1)
    y_left, y_right = along_y(-1), along_y(1)
    first_x, last_x = (zc == 0) & (pos == 0), (zc == nz - 1) & (pos == 3)
    first_y, last_y = (by == 0) & (core == 0), (by == nx - 1) & (core == 1)

    def raw(step_x, step_y):
        return (lax.rem(bx + 2 * nz + step_x, 2 * nz), lax.rem(by + nx + step_y, nx), vw)

    far_y = dev(zc, lax.rem(by + nx + jnp.where(core == 0, -1, 1), nx), y, other)
    raw_far = raw(jnp.where(y_lo == 0, -1, 1), 0)
    barrier = pltpu.get_barrier_semaphore()
    peers = [dev(zc, by, lax.rem(y + d, 4), core) for d in (1, 2, 3)]
    peers += [dev(zc, by, lax.rem(y + d, 4), other) for d in (0, 1, 2, 3)]
    peers += [dev(lax.rem(zc + nz + d, nz), by, y, core) for d in (-1, 1)]
    peers += [far_y, raw_far, raw(0, -1), raw(0, 1)]
    peers += [raw(i, j) for i in (-1, 1) for j in (-1, 1)]
    for peer in peers:
        pl.semaphore_signal(barrier, inc=1, device_id=peer, device_id_type=MESH)

    used = [0]
    sent = []

    def new_sem(count=1):
        first = used[0]
        used[0] += count
        return first

    def remote(src, dst, sem, device, at=None):
        return pltpu.make_async_remote_copy(
            src_ref=src, dst_ref=dst, send_sem=send_sem.at[sem],
            recv_sem=recv_sem.at[sem if at is None else at],
            device_id=device, device_id_type=MESH)

    def go(src, dst, device):
        copy = remote(src, dst, new_sem(), device)
        copy.start()
        sent.append(copy)
        return copy

    def piece(n):
        return pl.ds(n * PX, PX)

    def spread(source_at, target, own_store):
        base = new_sem(4)
        copies = []
        for r in range(4):
            y_, core_ = chip_at(zc, 2 * y_lo + r // 2), r % 2
            me = (y_ == y) & (core_ == core)
            copy = remote(source_at(r), target(vw), base + r, dev(zc, by, y_, core_), base + vw)
            copies.append((me, copy))

        def start():
            for me, copy in copies:
                pl.when(jnp.logical_not(me))(copy.start)

            @pl.when(stays)
            def _():
                own_store()

        def wait(s):
            @pl.when(jnp.logical_not(stays & (vw == s)))
            def _():
                remote(target(s), target(s), base + s, x_left).wait_recv()

        def finish():
            for me, copy in copies:
                pl.when(jnp.logical_not(me))(copy.wait_send)

        return start, wait, finish

    local_view = pltpu.make_async_copy(
        view.at[0], wide.at[pl.ds(SHIFT, CX), pl.ds(SHIFT, CY)], local_sem.at[0])
    local_view.start()
    small = [
        pltpu.make_async_copy(src, dst, local_sem.at[2 + n])
        for n, (src, dst) in enumerate(((psf_hbm, psf), (wts_hbm, wts), (off_hbm, off)))
    ]
    for copy in small:
        copy.start()
    own_block = raw_x.at[0, pl.ds(HALF, PX)]
    local_est = pltpu.make_async_copy(
        est.at[piece(part), piece(core)], own_block, local_sem.at[1])
    pl.when(stays)(local_est.start)
    pair = jnp.where(y_lo == 0, lax.rem(y + 3, 4), lax.rem(y + 1, 4))
    pair_part = lax.rem(jnp.where(lax.rem(zc, 2) == 0, pair, 3 - pair), 2)
    est_copy = remote(
        est.at[piece(pair_part), piece(core)], own_block, new_sem(), dev(zc, by, pair, core))

    own_params[...] = jnp.zeros((8, 128), jnp.float32)
    for copy in small:
        copy.wait()
    row = psf[:, 0, :]
    own_params[0:3, 0:TAPS] = row / jnp.sum(row, axis=-1, keepdims=True)
    for v in range(VIEWS):
        own_params[4 + v : 5 + v, :] = jnp.full((1, 128), wts[0, 0, v].astype(jnp.float32))

    def store_params():
        params[vw] = own_params[...]

    params_start, params_wait, params_finish = spread(
        lambda r: own_params, lambda s: params.at[s], store_params)

    pl.semaphore_wait(barrier, len(peers))
    pl.when(jnp.logical_not(stays))(est_copy.start)
    params_start()
    raw_copies = []
    low, high, middle = pl.ds(0, SHIFT), pl.ds(CX - SHIFT, SHIFT), pl.ds(0, CX)
    to_low, to_high, to_middle = pl.ds(0, SHIFT), pl.ds(SHIFT + CX, SHIFT), pl.ds(SHIFT, CX)
    moves = {-1: (low, to_high), 0: (middle, to_middle), 1: (high, to_low)}
    for i, j in ((-1, 0), (1, 0), (0, -1), (0, 1), (-1, -1), (-1, 1), (1, -1), (1, 1)):
        raw_copies.append(go(
            view.at[0, moves[i][0], moves[j][0]], wide.at[moves[i][1], moves[j][1]], raw(i, j)))

    def send_x(field):
        return [
            go(field.at[pl.ds(HALF, HALF)], field.at[pl.ds(HALF + PX, HALF)], x_left),
            go(field.at[pl.ds(PX, HALF)], field.at[pl.ds(0, HALF)], x_right),
        ]

    def wait_x(field, copies):
        for copy in copies:
            copy.wait_recv()

        @pl.when(first_x)
        def _():
            field[0:HALF] = jnp.zeros((HALF, PY, CZ), jnp.float32)

        @pl.when(last_x)
        def _():
            field[HALF + PX : WIDE_X] = jnp.zeros((HALF, PY, CZ), jnp.float32)

    def send_y(field):
        own = field.at[:, pl.ds(PY, PY)]
        return [
            go(own, field.at[:, pl.ds(2 * PY, PY)], y_left),
            go(own, field.at[:, pl.ds(0, PY)], y_right),
        ]

    pl.when(stays)(local_est.wait)
    pl.when(jnp.logical_not(stays))(est_copy.wait)

    def send_current(iteration):
        raw_y[iteration, :, PY : 2 * PY, :] = raw_x[iteration, HALF : HALF + PX]
        return send_y(raw_y.at[iteration]), send_x(raw_x.at[iteration])

    current_copies = send_current(0)

    for s in range(VIEWS):
        params_wait(s)

    def build(v, carry):
        for t in range(TAPS):
            taps[v, t] = jnp.broadcast_to(params[v, 0:1, t : t + 1], (8, CZ))
        r = lax.broadcasted_iota(jnp.int32, (PY, 4 * WIDE_Y), 0)
        c = lax.broadcasted_iota(jnp.int32, (PY, 4 * WIDE_Y), 1)
        group, c = lax.div(c, WIDE_Y), lax.rem(c, WIDE_Y)
        distance = c - r - 1
        outside = (first_y & (c < PY)) | (last_y & (c >= 2 * PY))
        forward = jnp.zeros((PY, 4 * WIDE_Y), jnp.float32)
        backward = forward
        for t in range(TAPS):
            tap = params[v, 1:2, t : t + 1]
            forward = jnp.where(distance == t, tap, forward)
            backward = jnp.where(distance == TAPS - 1 - t, tap, backward)
        for k, band in enumerate((forward, backward)):
            upper, lower = split(jnp.where(outside, 0.0, band))
            band_y[k, v] = jnp.where(
                group < 2, upper.astype(jnp.float32), lower.astype(jnp.float32)).astype(jnp.bfloat16)
        r = lax.broadcasted_iota(jnp.int32, (CZ, CZ), 0)
        c = lax.broadcasted_iota(jnp.int32, (CZ, CZ), 1)
        distance = r - c + HALF
        forward = jnp.zeros((CZ, CZ), jnp.float32)
        backward = forward
        for t in range(TAPS):
            tap = params[v, 2:3, t : t + 1]
            forward = jnp.where(distance == t, tap, forward)
            backward = jnp.where(distance == TAPS - 1 - t, tap, backward)
        for k, band in enumerate((forward, backward)):
            upper, lower = split(band)
            for n in range(2):
                band_z[k, v, n * CZ : (n + 1) * CZ, 0:CZ] = upper
                band_z[k, v, n * CZ : (n + 1) * CZ, CZ : 2 * CZ] = lower
        return carry

    lax.fori_loop(0, VIEWS, build, 0)

    def conv_x(field, v, k, target, row):
        def tile(j, carry):
            weights = [taps[v, TAPS - 1 - t if k else t] for t in range(TAPS)]
            sums = [None] * PX
            for a in range(WIDE_X):
                value = field[a, pl.ds(pl.multiple_of(8 * j, 8), 8), :]
                for i in range(PX):
                    if 0 <= a - i < TAPS:
                        term = weights[a - i] * value
                        sums[i] = term if sums[i] is None else sums[i] + term
            for i in range(PX):
                target[i, pl.ds(pl.multiple_of(row + 8 * j, 8), 8), :] = sums[i]
            return carry

        lax.fori_loop(0, PY // 8, tile, 0)

    def conv_y(field, v, k):
        blocks = []
        for p in range(0, PX, 2):
            both = jnp.concatenate([field[p], field[p + 1]], axis=1)
            upper, lower = split(both)
            stacked = jnp.concatenate([upper, lower, upper, lower], axis=0)
            both = jnp.dot(band_y[k, v], stacked, preferred_element_type=jnp.float32)
            blocks += [both[:, :CZ], both[:, CZ:]]
        return jnp.concatenate(blocks, axis=0)

    def conv_z(value, v, k):
        both = jnp.concatenate(split(value), axis=1)
        both = jnp.dot(both, band_z[k, v], preferred_element_type=jnp.float32)
        return both[:, :CZ] + both[:, CZ:]

    def store_aligned():
        aligned[vw] = own_aligned[piece(part), piece(core), :]

    aligned_start, aligned_wait, aligned_finish = spread(
        lambda r: own_aligned.at[piece(r // 2), piece(r % 2)], lambda s: aligned.at[s], store_aligned)

    def align():
        local_view.wait()
        for copy in raw_copies:
            copy.wait_recv()
        ox, oy, oz = off[0, 0, 0, 0], off[0, 0, 0, 1], off[0, 0, 0, 2]
        gy = by * CY + oy + lax.broadcasted_iota(jnp.int32, (CY, CZ), 0)
        gz = oz + lax.broadcasted_iota(jnp.int32, (CY, CZ), 1)
        inside = (gy >= 0) & (gy < nx * CY) & (gz >= 0) & (gz < CZ)
        turn = lax.rem(CZ - oz, CZ)

        def plane(p, carry):
            value = wide[SHIFT + ox + p, pl.ds(SHIFT + oy, CY), :]
            value = pltpu.roll(value, turn, 1)
            gx = bx * CX + ox + p
            ok = inside & (gx >= 0) & (gx < 2 * nz * CX)
            own_aligned[p] = jnp.where(ok, value, -1.0)
            return carry

        lax.fori_loop(0, CX, plane, 0)
        aligned_start()

    weights = params[0, 4:8, :]
    total = jnp.sum(weights, axis=0, keepdims=True)

    x_first = (True, True, False, False)
    x_first_back = (False, True, True, False)
    order, order_back = (2, 0, 1, 3), (0, 2, 3, 1)

    def begin_x(iteration, k, v, source):
        field = x_wide.at[iteration, k, v]
        field[HALF : HALF + PX] = source.reshape(PX, PY, CZ)
        return send_x(field)

    def begin_y(iteration, k, v, source):
        field = y_wide.at[iteration, k, v]
        field[:, PY : 2 * PY, :] = source.reshape(PX, PY, CZ)
        return send_y(field)

    def end_x(iteration, k, v, copies):
        field = x_wide.at[iteration, k, v]
        wait_x(field, copies)
        conv_x(field, v, k, value.at[v], 0)
        return value[v].reshape(PX * PY, CZ)

    def end_y(iteration, k, v, copies):
        for copy in copies:
            copy.wait_recv()
        return conv_y(y_wide.at[iteration, k, v], v, k)

    for iteration in range(ITERS):
        if iteration == 0:
            align()
        copies = {}
        for copy in current_copies[0]:
            copy.wait_recv()
        for v in range(VIEWS):
            if not x_first[v]:
                copies[v] = begin_x(iteration, 0, v, conv_y(raw_y.at[iteration], v, 0))
        wait_x(raw_x.at[iteration], current_copies[1])
        for v in range(VIEWS):
            if x_first[v]:
                field = y_wide.at[iteration, 0, v]
                conv_x(raw_x.at[iteration], v, 0, field, PY)
                copies[v] = send_y(field)
        for v in order:
            blurred = (end_y if x_first[v] else end_x)(iteration, 0, v, copies[v])
            blurred = conv_z(blurred, v, 0)
            if iteration == 0:
                aligned_wait(v)
            recorded = aligned[v].reshape(PX * PY, CZ)
            ratio = jnp.where(recorded >= 0.0, recorded / blurred, 1.0)
            back = conv_z(ratio, v, 1)
            copies[v] = (begin_x if x_first_back[v] else begin_y)(iteration, 1, v, back)
        for v in order_back:
            if x_first_back[v]:
                wait_x(x_wide.at[iteration, 1, v], copies[v])
                field = y_wide.at[iteration, 1, v]
                conv_x(x_wide.at[iteration, 1, v], v, 1, field, PY)
                copies[v] = send_y(field)
            else:
                copies[v] = begin_x(iteration, 1, v, end_y(iteration, 1, v, copies[v]))
        for n, v in enumerate(order_back):
            back = (end_y if x_first_back[v] else end_x)(iteration, 1, v, copies[v])
            term = params[0, 4 + v : 5 + v, :] * jnp.log(back)
            summed[...] = term if n == 0 else summed[...] + term
        update = jnp.exp(summed[...] / total).reshape(PX, PY, CZ)
        updated = raw_x[iteration, HALF : HALF + PX] * update
        if iteration + 1 < ITERS:
            raw_x[iteration + 1, HALF : HALF + PX] = updated
            current_copies = send_current(iteration + 1)
        else:
            result[...] = updated

    shared = PX // 2
    own_target = out.at[piece(part), piece(core)]
    chip_mate = dev(zc, by, y, other)
    base = new_sem(4)
    mate_copy = remote(result, own_target, new_sem(), chip_mate)
    results = []
    for n in range(2):
        y_ = side + 2 * n
        for c in range(2):
            copy = remote(
                result.at[pl.ds(c * shared, shared)],
                out.at[pl.ds(part * PX + c * shared, shared), piece(core)],
                base + 2 * n + c, dev(zc, by, y_, c), base + 2 * part + core)
            results.append((y_ != y, copy))
    for away, copy in results:
        pl.when(away)(copy.start)

    @pl.when(stays)
    def _():
        mate_copy.start()
        own_target[...] = result[...]

    base_mate = new_sem(4)
    forwards = []
    for s in range(4):
        away = chip_at(zc, 2 * y_lo + s // 2) != y
        got, missing = [
            out.at[pl.ds(s // 2 * PX + c * shared, shared), piece(s % 2)] for c in (core, other)
        ]
        arrival = remote(got, got, base + s, x_left)
        forward = remote(got, got, base_mate + s, chip_mate)
        missed = remote(missing, missing, base_mate + s, chip_mate)

        @pl.when(away)
        def _(arrival=arrival, forward=forward):
            arrival.wait_recv()
            forward.start()

        forwards.append((away, forward, missed))

    @pl.when(stays)
    def _():
        mate_copy.wait()

    for away, forward, missed in forwards:

        @pl.when(away)
        def _(forward=forward, missed=missed):
            missed.wait_recv()
            forward.wait_send()

    for away, copy in results:
        pl.when(away)(copy.wait_send)
    params_finish()
    aligned_finish()
    for copy in sent:
        copy.wait_send()


def solution(mesh):
    nz, nx = mesh.shape["bx"] // 2, mesh.shape["by"]
    f32, bf16 = jnp.float32, jnp.bfloat16

    def shards(estimate, views_raw, psf_taps, offsets, view_weights):
        vmem = pl.BlockSpec(memory_space=pltpu.VMEM)
        hbm = pl.BlockSpec(memory_space=pltpu.HBM)
        return pl.pallas_call(
            functools.partial(kernel, (nz, nx)),
            out_shape=jax.ShapeDtypeStruct((CX, CY, CZ), f32),
            in_specs=[hbm] * 5,
            out_specs=vmem,
            scratch_shapes=[
                pltpu.VMEM((ITERS, WIDE_X, PY, CZ), f32),
                pltpu.VMEM((ITERS, PX, WIDE_Y, CZ), f32),
                pltpu.VMEM((ITERS, 2, VIEWS, WIDE_X, PY, CZ), f32),
                pltpu.VMEM((ITERS, 2, VIEWS, PX, WIDE_Y, CZ), f32),
                pltpu.VMEM((VIEWS, PX, PY, CZ), f32),
                pltpu.VMEM((PX * PY, CZ), f32),
                pltpu.VMEM((PX, PY, CZ), f32),
                pltpu.VMEM((3, 1, TAPS), f32),
                pltpu.SMEM((1, 1, 1, 3), jnp.int32),
                pltpu.SMEM((1, 1, VIEWS), jnp.int32),
                pltpu.VMEM((CX + 2 * SHIFT, CY + 2 * SHIFT, CZ), f32),
                pltpu.VMEM((CX, CY, CZ), f32),
                pltpu.VMEM((VIEWS, PX, PY, CZ), f32),
                pltpu.VMEM((8, 128), f32),
                pltpu.VMEM((VIEWS, 8, 128), f32),
                pltpu.VMEM((VIEWS, TAPS, 8, CZ), f32),
                pltpu.VMEM((2, VIEWS, PY, 4 * WIDE_Y), bf16),
                pltpu.VMEM((2, VIEWS, 2 * CZ, 2 * CZ), bf16),
                pltpu.SemaphoreType.DMA((N_SEMS,)),
                pltpu.SemaphoreType.DMA((N_SEMS,)),
                pltpu.SemaphoreType.DMA((5,)),
            ],
            compiler_params=pltpu.CompilerParams(
                collective_id=0, has_side_effects=True, vmem_limit_bytes=53 * 1024 * 1024
            ),
            cost_estimate=pl.CostEstimate(flops=10**9, bytes_accessed=2 * 10**6, transcendentals=10**6),
        )(
            estimate,
            views_raw,
            jnp.transpose(psf_taps, (1, 0, 2)),
            offsets,
            jnp.transpose(view_weights, (1, 2, 0)),
        )

    return jax.shard_map(
        shards,
        mesh=mesh,
        in_specs=(
            P("bx", "by", None),
            P("view", "bx", "by", None),
            P("view", None, None),
            P("view", "bx", "by", None),
            P(None, "bx", "by"),
        ),
        out_specs=P("bx", "by", None),
        check_vma=False,
    )
```

```python
import functools

import jax
import jax.numpy as jnp
from jax import lax
from jax.experimental import pallas as pl
from jax.experimental.pallas import tpu as pltpu
from jax.sharding import PartitionSpec as P

ITERS = 2
TAPS = 31
HALF = 15
SHIFT = 8
VIEWS = 4
CX, CY, CZ = 32, 32, 128
PX, PY = 16, 16
WIDE_X = PX + 2 * HALF
WIDE_Y = 3 * PY
N_SEMS = 128
MESH = pl.DeviceIdType.MESH


def split(value):
    high = value.astype(jnp.bfloat16)
    low = (value - high.astype(jnp.float32)).astype(jnp.bfloat16)
    return high, low


def kernel(
    sizes,
    est, view, psf_hbm, off_hbm, wts_hbm,
    out,
    raw_x, raw_y, x_wide, y_wide, value, summed, result, psf, off, wts, wide, own_aligned, aligned, own_params, params,
    taps, band_y, band_z,
    send_sem, recv_sem, local_sem,
):
    nz, nx = sizes
    bx, by, vw = lax.axis_index("bx"), lax.axis_index("by"), lax.axis_index("view")
    zc, y_lo = lax.div(bx, 2), lax.rem(bx, 2)
    y_hi, core = lax.div(vw, 2), lax.rem(vw, 2)
    y = 2 * y_hi + y_lo
    other = 1 - core
    pos = jnp.where(lax.rem(zc, 2) == 0, y, 3 - y)
    side, part = lax.div(pos, 2), lax.rem(pos, 2)
    stays = side == y_lo

    def dev(zc_, x_, y_, core_):
        return (zc_ * 2 + lax.rem(y_, 2), x_, lax.div(y_, 2) * 2 + core_)

    def chip_at(zc_, pos_):
        return jnp.where(lax.rem(zc_, 2) == 0, pos_, 3 - pos_)

    def along_x(step):
        place = lax.rem(4 * zc + pos + 4 * nz + step, 4 * nz)
        zc_, pos_ = lax.div(place, 4), lax.rem(place, 4)
        return dev(zc_, by, chip_at(zc_, pos_), core)

    def along_y(step):
        place = lax.rem(2 * by + core + 2 * nx + step, 2 * nx)
        return dev(zc, lax.div(place, 2), y, lax.rem(place, 2))

    x_left, x_right = along_x(-1), along_x(1)
    y_left, y_right = along_y(-1), along_y(1)
    first_x, last_x = (zc == 0) & (pos == 0), (zc == nz - 1) & (pos == 3)
    first_y, last_y = (by == 0) & (core == 0), (by == nx - 1) & (core == 1)

    def raw(step_x, step_y):
        return (lax.rem(bx + 2 * nz + step_x, 2 * nz), lax.rem(by + nx + step_y, nx), vw)

    far_y = dev(zc, lax.rem(by + nx + jnp.where(core == 0, -1, 1), nx), y, other)
    raw_far = raw(jnp.where(y_lo == 0, -1, 1), 0)
    barrier = pltpu.get_barrier_semaphore()
    peers = [dev(zc, by, lax.rem(y + d, 4), core) for d in (1, 2, 3)]
    peers += [dev(zc, by, lax.rem(y + d, 4), other) for d in (0, 1, 2, 3)]
    peers += [dev(lax.rem(zc + nz + d, nz), by, y, core) for d in (-1, 1)]
    peers += [far_y, raw_far, raw(0, -1), raw(0, 1)]
    peers += [raw(i, j) for i in (-1, 1) for j in (-1, 1)]
    for peer in peers:
        pl.semaphore_signal(barrier, inc=1, device_id=peer, device_id_type=MESH)

    used = [0]
    sent = []

    def new_sem(count=1):
        first = used[0]
        used[0] += count
        return first

    def remote(src, dst, sem, device, at=None):
        return pltpu.make_async_remote_copy(
            src_ref=src, dst_ref=dst, send_sem=send_sem.at[sem],
            recv_sem=recv_sem.at[sem if at is None else at],
            device_id=device, device_id_type=MESH)

    def go(src, dst, device):
        copy = remote(src, dst, new_sem(), device)
        copy.start()
        sent.append(copy)
        return copy

    def piece(n):
        return pl.ds(n * PX, PX)

    def spread(source_at, target, own_store):
        base = new_sem(4)
        copies = []
        for r in range(4):
            y_, core_ = chip_at(zc, 2 * y_lo + r // 2), r % 2
            me = (y_ == y) & (core_ == core)
            copy = remote(source_at(r), target(vw), base + r, dev(zc, by, y_, core_), base + vw)
            copies.append((me, copy))

        def start(chosen=range(4), last=True):
            for r in chosen:
                me, copy = copies[r]
                pl.when(jnp.logical_not(me))(copy.start)

            if last:

                @pl.when(stays)
                def _():
                    own_store()

        def wait(s):
            @pl.when(jnp.logical_not(stays & (vw == s)))
            def _():
                remote(target(s), target(s), base + s, x_left).wait_recv()

        def finish():
            for me, copy in copies:
                pl.when(jnp.logical_not(me))(copy.wait_send)

        return start, wait, finish

    local_view = pltpu.make_async_copy(
        view.at[0], wide.at[pl.ds(SHIFT, CX), pl.ds(SHIFT, CY)], local_sem.at[0])
    local_view.start()
    small = [
        pltpu.make_async_copy(src, dst, local_sem.at[2 + n])
        for n, (src, dst) in enumerate(((psf_hbm, psf), (wts_hbm, wts), (off_hbm, off)))
    ]
    for copy in small:
        copy.start()
    own_block = raw_x.at[0, pl.ds(HALF, PX)]
    local_est = pltpu.make_async_copy(
        est.at[piece(part), piece(core)], own_block, local_sem.at[1])
    pl.when(stays)(local_est.start)
    pair = jnp.where(y_lo == 0, lax.rem(y + 3, 4), lax.rem(y + 1, 4))
    pair_part = lax.rem(jnp.where(lax.rem(zc, 2) == 0, pair, 3 - pair), 2)
    est_copy = remote(
        est.at[piece(pair_part), piece(core)], own_block, new_sem(), dev(zc, by, pair, core))

    own_params[...] = jnp.zeros((8, 128), jnp.float32)
    for copy in small:
        copy.wait()
    row = psf[:, 0, :]
    own_params[0:3, 0:TAPS] = row / jnp.sum(row, axis=-1, keepdims=True)
    for v in range(VIEWS):
        own_params[4 + v : 5 + v, :] = jnp.full((1, 128), wts[0, 0, v].astype(jnp.float32))

    def store_params():
        params[vw] = own_params[...]

    params_start, params_wait, params_finish = spread(
        lambda r: own_params, lambda s: params.at[s], store_params)

    pl.semaphore_wait(barrier, len(peers))
    raw_copies = []
    low, high, middle = pl.ds(0, SHIFT), pl.ds(CX - SHIFT, SHIFT), pl.ds(0, CX)
    to_low, to_high, to_middle = pl.ds(0, SHIFT), pl.ds(SHIFT + CX, SHIFT), pl.ds(SHIFT, CX)
    moves = {-1: (low, to_high), 0: (middle, to_middle), 1: (high, to_low)}
    for i, j in ((-1, 0), (1, 0), (0, -1), (0, 1), (-1, -1), (-1, 1), (1, -1), (1, 1)):
        raw_copies.append(go(
            view.at[0, moves[i][0], moves[j][0]], wide.at[moves[i][1], moves[j][1]], raw(i, j)))
    pl.when(jnp.logical_not(stays))(est_copy.start)
    params_start()

    def send_x(field):
        return [
            go(field.at[pl.ds(HALF, HALF)], field.at[pl.ds(HALF + PX, HALF)], x_left),
            go(field.at[pl.ds(PX, HALF)], field.at[pl.ds(0, HALF)], x_right),
        ]

    def wait_x(field, copies):
        for copy in copies:
            copy.wait_recv()

        @pl.when(first_x)
        def _():
            field[0:HALF] = jnp.zeros((HALF, PY, CZ), jnp.float32)

        @pl.when(last_x)
        def _():
            field[HALF + PX : WIDE_X] = jnp.zeros((HALF, PY, CZ), jnp.float32)

    def send_y(field):
        own = field.at[:, pl.ds(PY, PY)]
        return [
            go(own, field.at[:, pl.ds(2 * PY, PY)], y_left),
            go(own, field.at[:, pl.ds(0, PY)], y_right),
        ]

    pl.when(stays)(local_est.wait)
    pl.when(jnp.logical_not(stays))(est_copy.wait)

    def send_current(iteration):
        if iteration == 0:
            return [], send_x(raw_x.at[iteration])
        raw_y[iteration, :, PY : 2 * PY, :] = raw_x[iteration, HALF : HALF + PX]
        return send_y(raw_y.at[iteration]), send_x(raw_x.at[iteration])

    current_copies = send_current(0)

    for s in range(VIEWS):
        params_wait(s)

    def build(v, carry):
        for t in range(TAPS):
            taps[v, t] = jnp.broadcast_to(params[v, 0:1, t : t + 1], (8, CZ))
        r = lax.broadcasted_iota(jnp.int32, (PY, 4 * WIDE_Y), 0)
        c = lax.broadcasted_iota(jnp.int32, (PY, 4 * WIDE_Y), 1)
        group, c = lax.div(c, WIDE_Y), lax.rem(c, WIDE_Y)
        distance = c - r - 1
        outside = (first_y & (c < PY)) | (last_y & (c >= 2 * PY))
        forward = jnp.zeros((PY, 4 * WIDE_Y), jnp.float32)
        backward = forward
        for t in range(TAPS):
            tap = params[v, 1:2, t : t + 1]
            forward = jnp.where(distance == t, tap, forward)
            backward = jnp.where(distance == TAPS - 1 - t, tap, backward)
        for k, band in enumerate((forward, backward)):
            upper, lower = split(jnp.where(outside, 0.0, band))
            band_y[k, v] = jnp.where(
                group < 2, upper.astype(jnp.float32), lower.astype(jnp.float32)).astype(jnp.bfloat16)
        r = lax.broadcasted_iota(jnp.int32, (CZ, CZ), 0)
        c = lax.broadcasted_iota(jnp.int32, (CZ, CZ), 1)
        distance = r - c + HALF
        forward = jnp.zeros((CZ, CZ), jnp.float32)
        backward = forward
        for t in range(TAPS):
            tap = params[v, 2:3, t : t + 1]
            forward = jnp.where(distance == t, tap, forward)
            backward = jnp.where(distance == TAPS - 1 - t, tap, backward)
        for k, band in enumerate((forward, backward)):
            upper, lower = split(band)
            for n in range(2):
                band_z[k, v, n * CZ : (n + 1) * CZ, 0:CZ] = upper
                band_z[k, v, n * CZ : (n + 1) * CZ, CZ : 2 * CZ] = lower
        return carry

    lax.fori_loop(0, VIEWS, build, 0)

    def conv_x(field, v, k, target, row):
        def tile(j, carry):
            weights = [taps[v, TAPS - 1 - t if k else t] for t in range(TAPS)]
            sums = [None] * PX
            for a in range(WIDE_X):
                value = field[a, pl.ds(pl.multiple_of(8 * j, 8), 8), :]
                for i in range(PX):
                    if 0 <= a - i < TAPS:
                        term = weights[a - i] * value
                        sums[i] = term if sums[i] is None else sums[i] + term
            for i in range(PX):
                target[i, pl.ds(pl.multiple_of(row + 8 * j, 8), 8), :] = sums[i]
            return carry

        lax.fori_loop(0, PY // 8, tile, 0)

    def conv_y(field, v, k):
        blocks = []
        for p in range(0, PX, 2):
            both = jnp.concatenate([field[p], field[p + 1]], axis=1)
            upper, lower = split(both)
            stacked = jnp.concatenate([upper, lower, upper, lower], axis=0)
            both = jnp.dot(band_y[k, v], stacked, preferred_element_type=jnp.float32)
            blocks += [both[:, :CZ], both[:, CZ:]]
        return jnp.concatenate(blocks, axis=0)

    def conv_z(value, v, k):
        both = jnp.concatenate(split(value), axis=1)
        both = jnp.dot(both, band_z[k, v], preferred_element_type=jnp.float32)
        return both[:, :CZ] + both[:, CZ:]

    def store_aligned():
        aligned[vw] = own_aligned[piece(part), piece(core), :]

    aligned_start, aligned_wait, aligned_finish = spread(
        lambda r: own_aligned.at[piece(r // 2), piece(r % 2)], lambda s: aligned.at[s], store_aligned)

    def align():
        local_view.wait()
        for copy in raw_copies:
            copy.wait_recv()
        ox, oy, oz = off[0, 0, 0, 0], off[0, 0, 0, 1], off[0, 0, 0, 2]
        gy = by * CY + oy + lax.broadcasted_iota(jnp.int32, (CY, CZ), 0)
        gz = oz + lax.broadcasted_iota(jnp.int32, (CY, CZ), 1)
        inside = (gy >= 0) & (gy < nx * CY) & (gz >= 0) & (gz < CZ)
        turn = lax.rem(CZ - oz, CZ)

        def planes(n, carry):
            for i in range(8):
                p = 8 * n + i
                value = wide[SHIFT + ox + p, pl.ds(SHIFT + oy, CY), :]
                value = pltpu.roll(value, turn, 1)
                gx = bx * CX + ox + p
                ok = inside & (gx >= 0) & (gx < 2 * nz * CX)
                own_aligned[p] = jnp.where(ok, value, -1.0)
            return carry

        for n in range(2):
            lax.fori_loop(2 * n, 2 * n + 2, planes, 0)
            aligned_start((2 * n, 2 * n + 1), n == 1)

    weights = params[0, 4:8, :]
    total = jnp.sum(weights, axis=0, keepdims=True)

    x_first_back = (False, True, True, False)

    def begin_x(iteration, k, v, source):
        field = x_wide.at[iteration, k, v]
        field[HALF : HALF + PX] = source.reshape(PX, PY, CZ)
        return send_x(field)

    def begin_y(iteration, k, v, source):
        field = y_wide.at[iteration, k, v]
        field[:, PY : 2 * PY, :] = source.reshape(PX, PY, CZ)
        return send_y(field)

    def end_x(iteration, k, v, copies):
        field = x_wide.at[iteration, k, v]
        wait_x(field, copies)
        conv_x(field, v, k, value.at[v], 0)
        return value[v].reshape(PX * PY, CZ)

    def end_y(iteration, k, v, copies):
        for copy in copies:
            copy.wait_recv()
        return conv_y(y_wide.at[iteration, k, v], v, k)

    for iteration in range(ITERS):
        if iteration == 0:
            x_first, order, order_back = (True,) * VIEWS, (0, 1, 2, 3), (0, 1, 3, 2)
            align()
        else:
            x_first, order, order_back = (True, True, False, False), (2, 0, 1, 3), (0, 2, 3, 1)
        copies = {}
        for copy in current_copies[0]:
            copy.wait_recv()
        for v in range(VIEWS):
            if not x_first[v]:
                copies[v] = begin_x(iteration, 0, v, conv_y(raw_y.at[iteration], v, 0))
        wait_x(raw_x.at[iteration], current_copies[1])
        for v in range(VIEWS):
            if x_first[v]:
                field = y_wide.at[iteration, 0, v]
                conv_x(raw_x.at[iteration], v, 0, field, PY)
                copies[v] = send_y(field)
        for v in order:
            blurred = (end_y if x_first[v] else end_x)(iteration, 0, v, copies[v])
            blurred = conv_z(blurred, v, 0)
            if iteration == 0:
                aligned_wait(v)
            recorded = aligned[v].reshape(PX * PY, CZ)
            ratio = jnp.where(recorded >= 0.0, recorded / blurred, 1.0)
            back = conv_z(ratio, v, 1)
            copies[v] = (begin_x if x_first_back[v] else begin_y)(iteration, 1, v, back)
        for v in order_back:
            if x_first_back[v]:
                wait_x(x_wide.at[iteration, 1, v], copies[v])
                field = y_wide.at[iteration, 1, v]
                conv_x(x_wide.at[iteration, 1, v], v, 1, field, PY)
                copies[v] = send_y(field)
            else:
                copies[v] = begin_x(iteration, 1, v, end_y(iteration, 1, v, copies[v]))
        for n, v in enumerate(order_back):
            back = (end_y if x_first_back[v] else end_x)(iteration, 1, v, copies[v])
            term = params[0, 4 + v : 5 + v, :] * jnp.log(back)
            summed[...] = term if n == 0 else summed[...] + term
        update = jnp.exp(summed[...] / total).reshape(PX, PY, CZ)
        updated = raw_x[iteration, HALF : HALF + PX] * update
        if iteration + 1 < ITERS:
            raw_x[iteration + 1, HALF : HALF + PX] = updated
            current_copies = send_current(iteration + 1)
        else:
            result[...] = updated

    shared = PX // 2
    own_target = out.at[piece(part), piece(core)]
    chip_mate = dev(zc, by, y, other)
    base = new_sem(4)
    mate_copy = remote(result, own_target, new_sem(), chip_mate)
    results = []
    for n in range(2):
        y_ = side + 2 * n
        for c in range(2):
            copy = remote(
                result.at[pl.ds(c * shared, shared)],
                out.at[pl.ds(part * PX + c * shared, shared), piece(core)],
                base + 2 * n + c, dev(zc, by, y_, c), base + 2 * part + core)
            results.append((y_ != y, copy))
    for away, copy in results:
        pl.when(away)(copy.start)

    @pl.when(stays)
    def _():
        mate_copy.start()
        own_target[...] = result[...]

    base_mate = new_sem(4)
    forwards = []
    for s in range(4):
        away = chip_at(zc, 2 * y_lo + s // 2) != y
        got, missing = [
            out.at[pl.ds(s // 2 * PX + c * shared, shared), piece(s % 2)] for c in (core, other)
        ]
        arrival = remote(got, got, base + s, x_left)
        forward = remote(got, got, base_mate + s, chip_mate)
        missed = remote(missing, missing, base_mate + s, chip_mate)

        @pl.when(away)
        def _(arrival=arrival, forward=forward):
            arrival.wait_recv()
            forward.start()

        forwards.append((away, forward, missed))

    @pl.when(stays)
    def _():
        mate_copy.wait()

    for away, forward, missed in forwards:

        @pl.when(away)
        def _(forward=forward, missed=missed):
            missed.wait_recv()
            forward.wait_send()

    for away, copy in results:
        pl.when(away)(copy.wait_send)
    params_finish()
    aligned_finish()
    for copy in sent:
        copy.wait_send()


def solution(mesh):
    nz, nx = mesh.shape["bx"] // 2, mesh.shape["by"]
    f32, bf16 = jnp.float32, jnp.bfloat16

    def shards(estimate, views_raw, psf_taps, offsets, view_weights):
        vmem = pl.BlockSpec(memory_space=pltpu.VMEM)
        hbm = pl.BlockSpec(memory_space=pltpu.HBM)
        return pl.pallas_call(
            functools.partial(kernel, (nz, nx)),
            out_shape=jax.ShapeDtypeStruct((CX, CY, CZ), f32),
            in_specs=[hbm] * 5,
            out_specs=vmem,
            scratch_shapes=[
                pltpu.VMEM((ITERS, WIDE_X, PY, CZ), f32),
                pltpu.VMEM((ITERS, PX, WIDE_Y, CZ), f32),
                pltpu.VMEM((ITERS, 2, VIEWS, WIDE_X, PY, CZ), f32),
                pltpu.VMEM((ITERS, 2, VIEWS, PX, WIDE_Y, CZ), f32),
                pltpu.VMEM((VIEWS, PX, PY, CZ), f32),
                pltpu.VMEM((PX * PY, CZ), f32),
                pltpu.VMEM((PX, PY, CZ), f32),
                pltpu.VMEM((3, 1, TAPS), f32),
                pltpu.SMEM((1, 1, 1, 3), jnp.int32),
                pltpu.SMEM((1, 1, VIEWS), jnp.int32),
                pltpu.VMEM((CX + 2 * SHIFT, CY + 2 * SHIFT, CZ), f32),
                pltpu.VMEM((CX, CY, CZ), f32),
                pltpu.VMEM((VIEWS, PX, PY, CZ), f32),
                pltpu.VMEM((8, 128), f32),
                pltpu.VMEM((VIEWS, 8, 128), f32),
                pltpu.VMEM((VIEWS, TAPS, 8, CZ), f32),
                pltpu.VMEM((2, VIEWS, PY, 4 * WIDE_Y), bf16),
                pltpu.VMEM((2, VIEWS, 2 * CZ, 2 * CZ), bf16),
                pltpu.SemaphoreType.DMA((N_SEMS,)),
                pltpu.SemaphoreType.DMA((N_SEMS,)),
                pltpu.SemaphoreType.DMA((5,)),
            ],
            compiler_params=pltpu.CompilerParams(
                collective_id=0, has_side_effects=True, vmem_limit_bytes=53 * 1024 * 1024
            ),
            cost_estimate=pl.CostEstimate(flops=10**9, bytes_accessed=2 * 10**6, transcendentals=10**6),
        )(
            estimate,
            views_raw,
            jnp.transpose(psf_taps, (1, 0, 2)),
            offsets,
            jnp.transpose(view_weights, (1, 2, 0)),
        )

    return jax.shard_map(
        shards,
        mesh=mesh,
        in_specs=(
            P("bx", "by", None),
            P("view", "bx", "by", None),
            P("view", None, None),
            P("view", "bx", "by", None),
            P(None, "bx", "by"),
        ),
        out_specs=P("bx", "by", None),
        check_vma=False,
    )
```

```python
import functools

import jax
import jax.numpy as jnp
from jax import lax
from jax.experimental import pallas as pl
from jax.experimental.pallas import tpu as pltpu
from jax.sharding import PartitionSpec as P

ITERS = 2
TAPS = 31
HALF = 15
SHIFT = 8
VIEWS = 4
CX, CY, CZ = 32, 32, 128
PX, PY = 16, 16
WIDE_X = PX + 2 * HALF
WIDE_Y = 3 * PY
N_SEMS = 128
MESH = pl.DeviceIdType.MESH


def split(value):
    high = value.astype(jnp.bfloat16)
    low = (value - high.astype(jnp.float32)).astype(jnp.bfloat16)
    return high, low


def kernel(
    sizes,
    est, view, psf_hbm, off_hbm, wts_hbm,
    out,
    raw_x, raw_y, x_wide, y_wide, value, summed, result, psf, off, wts, wide, own_aligned, aligned, own_params, params,
    taps, band_y, band_z,
    send_sem, recv_sem, local_sem,
):
    nz, nx = sizes
    bx, by, vw = lax.axis_index("bx"), lax.axis_index("by"), lax.axis_index("view")
    zc, y_lo = lax.div(bx, 2), lax.rem(bx, 2)
    y_hi, core = lax.div(vw, 2), lax.rem(vw, 2)
    y = 2 * y_hi + y_lo
    other = 1 - core
    pos = jnp.where(lax.rem(zc, 2) == 0, y, 3 - y)
    side, part = lax.div(pos, 2), lax.rem(pos, 2)
    stays = side == y_lo

    def dev(zc_, x_, y_, core_):
        return (zc_ * 2 + lax.rem(y_, 2), x_, lax.div(y_, 2) * 2 + core_)

    def chip_at(zc_, pos_):
        return jnp.where(lax.rem(zc_, 2) == 0, pos_, 3 - pos_)

    def along_x(step):
        place = lax.rem(4 * zc + pos + 4 * nz + step, 4 * nz)
        zc_, pos_ = lax.div(place, 4), lax.rem(place, 4)
        return dev(zc_, by, chip_at(zc_, pos_), core)

    def along_y(step):
        place = lax.rem(2 * by + core + 2 * nx + step, 2 * nx)
        return dev(zc, lax.div(place, 2), y, lax.rem(place, 2))

    x_left, x_right = along_x(-1), along_x(1)
    y_left, y_right = along_y(-1), along_y(1)
    first_x, last_x = (zc == 0) & (pos == 0), (zc == nz - 1) & (pos == 3)
    first_y, last_y = (by == 0) & (core == 0), (by == nx - 1) & (core == 1)

    def raw(step_x, step_y):
        return (lax.rem(bx + 2 * nz + step_x, 2 * nz), lax.rem(by + nx + step_y, nx), vw)

    far_y = dev(zc, lax.rem(by + nx + jnp.where(core == 0, -1, 1), nx), y, other)
    raw_far = raw(jnp.where(y_lo == 0, -1, 1), 0)
    barrier = pltpu.get_barrier_semaphore()
    peers = [dev(zc, by, lax.rem(y + d, 4), core) for d in (1, 2, 3)]
    peers += [dev(zc, by, lax.rem(y + d, 4), other) for d in (0, 1, 2, 3)]
    peers += [dev(lax.rem(zc + nz + d, nz), by, y, core) for d in (-1, 1)]
    peers += [far_y, raw_far, raw(0, -1), raw(0, 1)]
    for peer in peers:
        pl.semaphore_signal(barrier, inc=1, device_id=peer, device_id_type=MESH)

    used = [0]
    sent = []

    def new_sem(count=1):
        first = used[0]
        used[0] += count
        return first

    def remote(src, dst, sem, device, at=None):
        return pltpu.make_async_remote_copy(
            src_ref=src, dst_ref=dst, send_sem=send_sem.at[sem],
            recv_sem=recv_sem.at[sem if at is None else at],
            device_id=device, device_id_type=MESH)

    def go(src, dst, device):
        copy = remote(src, dst, new_sem(), device)
        copy.start()
        sent.append(copy)
        return copy

    def piece(n):
        return pl.ds(n * PX, PX)

    def spread(source_at, target, own_store):
        base = new_sem(4)
        copies = []
        for r in range(4):
            y_, core_ = chip_at(zc, 2 * y_lo + r // 2), r % 2
            me = (y_ == y) & (core_ == core)
            copy = remote(source_at(r), target(vw), base + r, dev(zc, by, y_, core_), base + vw)
            copies.append((me, copy))

        def start(chosen=range(4), last=True):
            for r in chosen:
                me, copy = copies[r]
                pl.when(jnp.logical_not(me))(copy.start)

            if last:

                @pl.when(stays)
                def _():
                    own_store()

        def wait(s):
            @pl.when(jnp.logical_not(stays & (vw == s)))
            def _():
                remote(target(s), target(s), base + s, x_left).wait_recv()

        def finish():
            for me, copy in copies:
                pl.when(jnp.logical_not(me))(copy.wait_send)

        return start, wait, finish

    local_view = pltpu.make_async_copy(
        view.at[0], wide.at[pl.ds(SHIFT, CX), pl.ds(SHIFT, CY)], local_sem.at[0])
    local_view.start()
    small = [
        pltpu.make_async_copy(src, dst, local_sem.at[2 + n])
        for n, (src, dst) in enumerate(((psf_hbm, psf), (wts_hbm, wts), (off_hbm, off)))
    ]
    for copy in small:
        copy.start()
    own_block = raw_x.at[0, pl.ds(HALF, PX)]
    local_est = pltpu.make_async_copy(
        est.at[piece(part), piece(core)], own_block, local_sem.at[1])
    pl.when(stays)(local_est.start)
    pair = jnp.where(y_lo == 0, lax.rem(y + 3, 4), lax.rem(y + 1, 4))
    pair_part = lax.rem(jnp.where(lax.rem(zc, 2) == 0, pair, 3 - pair), 2)
    est_copy = remote(
        est.at[piece(pair_part), piece(core)], own_block, new_sem(), dev(zc, by, pair, core))

    own_params[...] = jnp.zeros((8, 128), jnp.float32)
    for copy in small:
        copy.wait()
    row = psf[:, 0, :]
    own_params[0:3, 0:TAPS] = row / jnp.sum(row, axis=-1, keepdims=True)
    for v in range(VIEWS):
        own_params[4 + v : 5 + v, :] = jnp.full((1, 128), wts[0, 0, v].astype(jnp.float32))

    def store_params():
        params[vw] = own_params[...]

    params_start, params_wait, params_finish = spread(
        lambda r: own_params, lambda s: params.at[s], store_params)

    pl.semaphore_wait(barrier, len(peers))
    raw_copies, outer_copies = [], []
    low, high = pl.ds(0, SHIFT), pl.ds(CX - SHIFT, SHIFT)
    inner_rows, all_rows = pl.ds(SHIFT, CY - 2 * SHIFT), pl.ds(0, CY)
    to_low, to_high = pl.ds(0, SHIFT), pl.ds(SHIFT + CX, SHIFT)

    def send_raw(planes, rows, to_planes, to_rows, device):
        return go(view.at[0, planes, rows], wide.at[to_planes, to_rows], device)

    x_moves = ((low, to_high, raw(-1, 0)), (high, to_low, raw(1, 0)))
    for planes, to_planes, device in x_moves:
        for start in (0, CY - SHIFT):
            outer_copies.append(send_raw(
                planes, pl.ds(start, SHIFT), to_planes, pl.ds(SHIFT + start, SHIFT), device))
    for planes, to_planes, device in x_moves:
        raw_copies.append(send_raw(
            planes, inner_rows, to_planes, pl.ds(2 * SHIFT, CY - 2 * SHIFT), device))
    for rows, to_rows, device in ((low, to_high, raw(0, -1)), (high, to_low, raw(0, 1))):
        raw_copies.append(send_raw(all_rows, rows, pl.ds(SHIFT, CX), to_rows, device))
    pl.when(jnp.logical_not(stays))(est_copy.start)
    params_start()

    def send_x(field):
        return [
            go(field.at[pl.ds(HALF, HALF)], field.at[pl.ds(HALF + PX, HALF)], x_left),
            go(field.at[pl.ds(PX, HALF)], field.at[pl.ds(0, HALF)], x_right),
        ]

    def wait_x(field, copies):
        for copy in copies:
            copy.wait_recv()

        @pl.when(first_x)
        def _():
            field[0:HALF] = jnp.zeros((HALF, PY, CZ), jnp.float32)

        @pl.when(last_x)
        def _():
            field[HALF + PX : WIDE_X] = jnp.zeros((HALF, PY, CZ), jnp.float32)

    def send_y(field):
        own = field.at[:, pl.ds(PY, PY)]
        return [
            go(own, field.at[:, pl.ds(2 * PY, PY)], y_left),
            go(own, field.at[:, pl.ds(0, PY)], y_right),
        ]

    pl.when(stays)(local_est.wait)
    pl.when(jnp.logical_not(stays))(est_copy.wait)

    def send_current(iteration):
        if iteration == 0:
            return [], send_x(raw_x.at[iteration])
        raw_y[iteration, :, PY : 2 * PY, :] = raw_x[iteration, HALF : HALF + PX]
        return send_y(raw_y.at[iteration]), send_x(raw_x.at[iteration])

    current_copies = send_current(0)

    for copy in outer_copies:
        copy.wait_recv()
    for planes in (to_low, to_high):
        for rows, to_rows, device in (
            (pl.ds(SHIFT, SHIFT), to_high, raw(0, -1)),
            (pl.ds(CY, SHIFT), to_low, raw(0, 1)),
        ):
            raw_copies.append(go(wide.at[planes, rows], wide.at[planes, to_rows], device))

    for s in range(VIEWS):
        params_wait(s)

    def build(v, carry):
        for t in range(TAPS):
            taps[v, t] = jnp.broadcast_to(params[v, 0:1, t : t + 1], (8, CZ))
        r = lax.broadcasted_iota(jnp.int32, (PY, 4 * WIDE_Y), 0)
        c = lax.broadcasted_iota(jnp.int32, (PY, 4 * WIDE_Y), 1)
        group, c = lax.div(c, WIDE_Y), lax.rem(c, WIDE_Y)
        distance = c - r - 1
        outside = (first_y & (c < PY)) | (last_y & (c >= 2 * PY))
        forward = jnp.zeros((PY, 4 * WIDE_Y), jnp.float32)
        backward = forward
        for t in range(TAPS):
            tap = params[v, 1:2, t : t + 1]
            forward = jnp.where(distance == t, tap, forward)
            backward = jnp.where(distance == TAPS - 1 - t, tap, backward)
        for k, band in enumerate((forward, backward)):
            upper, lower = split(jnp.where(outside, 0.0, band))
            band_y[k, v] = jnp.where(
                group < 2, upper.astype(jnp.float32), lower.astype(jnp.float32)).astype(jnp.bfloat16)
        r = lax.broadcasted_iota(jnp.int32, (CZ, CZ), 0)
        c = lax.broadcasted_iota(jnp.int32, (CZ, CZ), 1)
        distance = r - c + HALF
        forward = jnp.zeros((CZ, CZ), jnp.float32)
        backward = forward
        for t in range(TAPS):
            tap = params[v, 2:3, t : t + 1]
            forward = jnp.where(distance == t, tap, forward)
            backward = jnp.where(distance == TAPS - 1 - t, tap, backward)
        for k, band in enumerate((forward, backward)):
            upper, lower = split(band)
            for n in range(2):
                band_z[k, v, n * CZ : (n + 1) * CZ, 0:CZ] = upper
                band_z[k, v, n * CZ : (n + 1) * CZ, CZ : 2 * CZ] = lower
        return carry

    lax.fori_loop(0, VIEWS, build, 0)

    def conv_x(field, v, k, target, row):
        def tile(j, carry):
            weights = [taps[v, TAPS - 1 - t if k else t] for t in range(TAPS)]
            sums = [None] * PX
            for a in range(WIDE_X):
                value = field[a, pl.ds(pl.multiple_of(8 * j, 8), 8), :]
                for i in range(PX):
                    if 0 <= a - i < TAPS:
                        term = weights[a - i] * value
                        sums[i] = term if sums[i] is None else sums[i] + term
            for i in range(PX):
                target[i, pl.ds(pl.multiple_of(row + 8 * j, 8), 8), :] = sums[i]
            return carry

        lax.fori_loop(0, PY // 8, tile, 0)

    def conv_y(field, v, k):
        blocks = []
        for p in range(0, PX, 2):
            both = jnp.concatenate([field[p], field[p + 1]], axis=1)
            upper, lower = split(both)
            stacked = jnp.concatenate([upper, lower, upper, lower], axis=0)
            both = jnp.dot(band_y[k, v], stacked, preferred_element_type=jnp.float32)
            blocks += [both[:, :CZ], both[:, CZ:]]
        return jnp.concatenate(blocks, axis=0)

    def conv_z(value, v, k):
        both = jnp.concatenate(split(value), axis=1)
        both = jnp.dot(both, band_z[k, v], preferred_element_type=jnp.float32)
        return both[:, :CZ] + both[:, CZ:]

    def store_aligned():
        aligned[vw] = own_aligned[piece(part), piece(core), :]

    aligned_start, aligned_wait, aligned_finish = spread(
        lambda r: own_aligned.at[piece(r // 2), piece(r % 2)], lambda s: aligned.at[s], store_aligned)

    def align():
        local_view.wait()
        for copy in raw_copies:
            copy.wait_recv()
        ox, oy, oz = off[0, 0, 0, 0], off[0, 0, 0, 1], off[0, 0, 0, 2]
        gy = by * CY + oy + lax.broadcasted_iota(jnp.int32, (CY, CZ), 0)
        gz = oz + lax.broadcasted_iota(jnp.int32, (CY, CZ), 1)
        inside = (gy >= 0) & (gy < nx * CY) & (gz >= 0) & (gz < CZ)
        turn = lax.rem(CZ - oz, CZ)

        def planes(n, carry):
            for i in range(8):
                p = 8 * n + i
                value = wide[SHIFT + ox + p, pl.ds(SHIFT + oy, CY), :]
                value = pltpu.roll(value, turn, 1)
                gx = bx * CX + ox + p
                ok = inside & (gx >= 0) & (gx < 2 * nz * CX)
                own_aligned[p] = jnp.where(ok, value, -1.0)
            return carry

        for n in range(2):
            lax.fori_loop(2 * n, 2 * n + 2, planes, 0)
            aligned_start((2 * n, 2 * n + 1), n == 1)

    weights = params[0, 4:8, :]
    total = jnp.sum(weights, axis=0, keepdims=True)

    x_first_back = (False, True, True, False)

    def begin_x(iteration, k, v, source):
        field = x_wide.at[iteration, k, v]
        field[HALF : HALF + PX] = source.reshape(PX, PY, CZ)
        return send_x(field)

    def begin_y(iteration, k, v, source):
        field = y_wide.at[iteration, k, v]
        field[:, PY : 2 * PY, :] = source.reshape(PX, PY, CZ)
        return send_y(field)

    def end_x(iteration, k, v, copies):
        field = x_wide.at[iteration, k, v]
        wait_x(field, copies)
        conv_x(field, v, k, value.at[v], 0)
        return value[v].reshape(PX * PY, CZ)

    def end_y(iteration, k, v, copies):
        for copy in copies:
            copy.wait_recv()
        return conv_y(y_wide.at[iteration, k, v], v, k)

    for iteration in range(ITERS):
        if iteration == 0:
            x_first, order, order_back = (True,) * VIEWS, (0, 1, 2, 3), (0, 1, 3, 2)
            align()
        else:
            x_first, order, order_back = (True, True, False, False), (2, 0, 1, 3), (0, 2, 3, 1)
        copies = {}
        for copy in current_copies[0]:
            copy.wait_recv()
        for v in range(VIEWS):
            if not x_first[v]:
                copies[v] = begin_x(iteration, 0, v, conv_y(raw_y.at[iteration], v, 0))
        wait_x(raw_x.at[iteration], current_copies[1])
        for v in range(VIEWS):
            if x_first[v]:
                field = y_wide.at[iteration, 0, v]
                conv_x(raw_x.at[iteration], v, 0, field, PY)
                copies[v] = send_y(field)
        for v in order:
            blurred = (end_y if x_first[v] else end_x)(iteration, 0, v, copies[v])
            blurred = conv_z(blurred, v, 0)
            if iteration == 0:
                aligned_wait(v)
            recorded = aligned[v].reshape(PX * PY, CZ)
            ratio = jnp.where(recorded >= 0.0, recorded / blurred, 1.0)
            back = conv_z(ratio, v, 1)
            copies[v] = (begin_x if x_first_back[v] else begin_y)(iteration, 1, v, back)
        for v in order_back:
            if x_first_back[v]:
                wait_x(x_wide.at[iteration, 1, v], copies[v])
                field = y_wide.at[iteration, 1, v]
                conv_x(x_wide.at[iteration, 1, v], v, 1, field, PY)
                copies[v] = send_y(field)
            else:
                copies[v] = begin_x(iteration, 1, v, end_y(iteration, 1, v, copies[v]))
        for n, v in enumerate(order_back):
            back = (end_y if x_first_back[v] else end_x)(iteration, 1, v, copies[v])
            term = params[0, 4 + v : 5 + v, :] * jnp.log(back)
            summed[...] = term if n == 0 else summed[...] + term
        update = jnp.exp(summed[...] / total).reshape(PX, PY, CZ)
        updated = raw_x[iteration, HALF : HALF + PX] * update
        if iteration + 1 < ITERS:
            raw_x[iteration + 1, HALF : HALF + PX] = updated
            current_copies = send_current(iteration + 1)
        else:
            result[...] = updated

    shared = PX // 2
    own_target = out.at[piece(part), piece(core)]
    chip_mate = dev(zc, by, y, other)
    base = new_sem(4)
    mate_copy = remote(result, own_target, new_sem(), chip_mate)
    results = []
    for n in range(2):
        y_ = side + 2 * n
        for c in range(2):
            copy = remote(
                result.at[pl.ds(c * shared, shared)],
                out.at[pl.ds(part * PX + c * shared, shared), piece(core)],
                base + 2 * n + c, dev(zc, by, y_, c), base + 2 * part + core)
            results.append((y_ != y, copy))
    for away, copy in results:
        pl.when(away)(copy.start)

    @pl.when(stays)
    def _():
        mate_copy.start()
        own_target[...] = result[...]

    base_mate = new_sem(4)
    forwards = []
    for s in range(4):
        away = chip_at(zc, 2 * y_lo + s // 2) != y
        got, missing = [
            out.at[pl.ds(s // 2 * PX + c * shared, shared), piece(s % 2)] for c in (core, other)
        ]
        arrival = remote(got, got, base + s, x_left)
        forward = remote(got, got, base_mate + s, chip_mate)
        missed = remote(missing, missing, base_mate + s, chip_mate)

        @pl.when(away)
        def _(arrival=arrival, forward=forward):
            arrival.wait_recv()
            forward.start()

        forwards.append((away, forward, missed))

    @pl.when(stays)
    def _():
        mate_copy.wait()

    for away, forward, missed in forwards:

        @pl.when(away)
        def _(forward=forward, missed=missed):
            missed.wait_recv()
            forward.wait_send()

    for away, copy in results:
        pl.when(away)(copy.wait_send)
    params_finish()
    aligned_finish()
    for copy in sent:
        copy.wait_send()


def solution(mesh):
    nz, nx = mesh.shape["bx"] // 2, mesh.shape["by"]
    f32, bf16 = jnp.float32, jnp.bfloat16

    def shards(estimate, views_raw, psf_taps, offsets, view_weights):
        vmem = pl.BlockSpec(memory_space=pltpu.VMEM)
        hbm = pl.BlockSpec(memory_space=pltpu.HBM)
        return pl.pallas_call(
            functools.partial(kernel, (nz, nx)),
            out_shape=jax.ShapeDtypeStruct((CX, CY, CZ), f32),
            in_specs=[hbm] * 5,
            out_specs=vmem,
            scratch_shapes=[
                pltpu.VMEM((ITERS, WIDE_X, PY, CZ), f32),
                pltpu.VMEM((ITERS, PX, WIDE_Y, CZ), f32),
                pltpu.VMEM((ITERS, 2, VIEWS, WIDE_X, PY, CZ), f32),
                pltpu.VMEM((ITERS, 2, VIEWS, PX, WIDE_Y, CZ), f32),
                pltpu.VMEM((VIEWS, PX, PY, CZ), f32),
                pltpu.VMEM((PX * PY, CZ), f32),
                pltpu.VMEM((PX, PY, CZ), f32),
                pltpu.VMEM((3, 1, TAPS), f32),
                pltpu.SMEM((1, 1, 1, 3), jnp.int32),
                pltpu.SMEM((1, 1, VIEWS), jnp.int32),
                pltpu.VMEM((CX + 2 * SHIFT, CY + 2 * SHIFT, CZ), f32),
                pltpu.VMEM((CX, CY, CZ), f32),
                pltpu.VMEM((VIEWS, PX, PY, CZ), f32),
                pltpu.VMEM((8, 128), f32),
                pltpu.VMEM((VIEWS, 8, 128), f32),
                pltpu.VMEM((VIEWS, TAPS, 8, CZ), f32),
                pltpu.VMEM((2, VIEWS, PY, 4 * WIDE_Y), bf16),
                pltpu.VMEM((2, VIEWS, 2 * CZ, 2 * CZ), bf16),
                pltpu.SemaphoreType.DMA((N_SEMS,)),
                pltpu.SemaphoreType.DMA((N_SEMS,)),
                pltpu.SemaphoreType.DMA((5,)),
            ],
            compiler_params=pltpu.CompilerParams(
                collective_id=0, has_side_effects=True, vmem_limit_bytes=53 * 1024 * 1024
            ),
            cost_estimate=pl.CostEstimate(flops=10**9, bytes_accessed=2 * 10**6, transcendentals=10**6),
        )(
            estimate,
            views_raw,
            jnp.transpose(psf_taps, (1, 0, 2)),
            offsets,
            jnp.transpose(view_weights, (1, 2, 0)),
        )

    return jax.shard_map(
        shards,
        mesh=mesh,
        in_specs=(
            P("bx", "by", None),
            P("view", "bx", "by", None),
            P("view", None, None),
            P("view", "bx", "by", None),
            P(None, "bx", "by"),
        ),
        out_specs=P("bx", "by", None),
        check_vma=False,
    )
```

```python
import functools

import jax
import jax.numpy as jnp
from jax import lax
from jax.experimental import pallas as pl
from jax.experimental.pallas import tpu as pltpu
from jax.sharding import PartitionSpec as P

ITERS = 2
TAPS = 31
HALF = 15
SHIFT = 8
VIEWS = 4
CX, CY, CZ = 32, 32, 128
PX, PY = 16, 16
WIDE_X = PX + 2 * HALF
WIDE_Y = 3 * PY
N_SEMS = 128
MESH = pl.DeviceIdType.MESH


def split(value):
    high = value.astype(jnp.bfloat16)
    low = (value - high.astype(jnp.float32)).astype(jnp.bfloat16)
    return high, low


def kernel(
    sizes,
    est, view, psf_hbm, off_hbm, wts_hbm,
    out,
    raw_x, raw_y, x_wide, y_wide, value, summed, result, psf, off, wts, wide, own_aligned, aligned, own_params, params,
    taps, band_y, band_z,
    send_sem, recv_sem, local_sem,
):
    nz, nx = sizes
    bx, by, vw = lax.axis_index("bx"), lax.axis_index("by"), lax.axis_index("view")
    zc, y_lo = lax.div(bx, 2), lax.rem(bx, 2)
    y_hi, core = lax.div(vw, 2), lax.rem(vw, 2)
    y = 2 * y_hi + y_lo
    other = 1 - core
    pos = jnp.where(lax.rem(zc, 2) == 0, y, 3 - y)
    side, part = lax.div(pos, 2), lax.rem(pos, 2)
    stays = side == y_lo

    def dev(zc_, x_, y_, core_):
        return (zc_ * 2 + lax.rem(y_, 2), x_, lax.div(y_, 2) * 2 + core_)

    def chip_at(zc_, pos_):
        return jnp.where(lax.rem(zc_, 2) == 0, pos_, 3 - pos_)

    def along_x(step):
        place = lax.rem(4 * zc + pos + 4 * nz + step, 4 * nz)
        zc_, pos_ = lax.div(place, 4), lax.rem(place, 4)
        return dev(zc_, by, chip_at(zc_, pos_), core)

    def along_y(step):
        place = lax.rem(2 * by + core + 2 * nx + step, 2 * nx)
        return dev(zc, lax.div(place, 2), y, lax.rem(place, 2))

    x_left, x_right = along_x(-1), along_x(1)
    y_left, y_right = along_y(-1), along_y(1)
    first_x, last_x = (zc == 0) & (pos == 0), (zc == nz - 1) & (pos == 3)
    first_y, last_y = (by == 0) & (core == 0), (by == nx - 1) & (core == 1)

    def raw(step_x, step_y):
        return (lax.rem(bx + 2 * nz + step_x, 2 * nz), lax.rem(by + nx + step_y, nx), vw)

    far_y = dev(zc, lax.rem(by + nx + jnp.where(core == 0, -1, 1), nx), y, other)
    raw_far = raw(jnp.where(y_lo == 0, -1, 1), 0)
    barrier = pltpu.get_barrier_semaphore()
    peers = [dev(zc, by, lax.rem(y + d, 4), core) for d in (1, 2, 3)]
    peers += [dev(zc, by, lax.rem(y + d, 4), other) for d in (0, 1, 2, 3)]
    peers += [dev(lax.rem(zc + nz + d, nz), by, y, core) for d in (-1, 1)]
    peers += [far_y, raw_far, raw(0, -1), raw(0, 1)]
    for peer in peers:
        pl.semaphore_signal(barrier, inc=1, device_id=peer, device_id_type=MESH)

    used = [0]
    sent = []

    def new_sem(count=1):
        first = used[0]
        used[0] += count
        return first

    def remote(src, dst, sem, device, at=None):
        return pltpu.make_async_remote_copy(
            src_ref=src, dst_ref=dst, send_sem=send_sem.at[sem],
            recv_sem=recv_sem.at[sem if at is None else at],
            device_id=device, device_id_type=MESH)

    def go(src, dst, device):
        copy = remote(src, dst, new_sem(), device)
        copy.start()
        sent.append(copy)
        return copy

    def piece(n):
        return pl.ds(n * PX, PX)

    def spread(source_at, target, own_store):
        base = new_sem(4)
        copies = []
        for r in range(4):
            y_, core_ = chip_at(zc, 2 * y_lo + r // 2), r % 2
            me = (y_ == y) & (core_ == core)
            copy = remote(source_at(r), target(vw), base + r, dev(zc, by, y_, core_), base + vw)
            copies.append((me, copy))

        def start(chosen=range(4), last=True):
            for r in chosen:
                me, copy = copies[r]
                pl.when(jnp.logical_not(me))(copy.start)

            if last:

                @pl.when(stays)
                def _():
                    own_store()

        def wait(s):
            @pl.when(jnp.logical_not(stays & (vw == s)))
            def _():
                remote(target(s), target(s), base + s, x_left).wait_recv()

        def finish():
            for me, copy in copies:
                pl.when(jnp.logical_not(me))(copy.wait_send)

        return start, wait, finish

    local_view = pltpu.make_async_copy(
        view.at[0], wide.at[pl.ds(SHIFT, CX), pl.ds(SHIFT, CY)], local_sem.at[0])
    local_view.start()
    small = [
        pltpu.make_async_copy(src, dst, local_sem.at[2 + n])
        for n, (src, dst) in enumerate(((psf_hbm, psf), (wts_hbm, wts), (off_hbm, off)))
    ]
    for copy in small:
        copy.start()
    own_block = raw_x.at[0, pl.ds(HALF, PX)]
    local_est = pltpu.make_async_copy(
        est.at[piece(part), piece(core)], own_block, local_sem.at[1])
    pl.when(stays)(local_est.start)
    pair = jnp.where(y_lo == 0, lax.rem(y + 3, 4), lax.rem(y + 1, 4))
    pair_part = lax.rem(jnp.where(lax.rem(zc, 2) == 0, pair, 3 - pair), 2)
    est_copy = remote(
        est.at[piece(pair_part), piece(core)], own_block, new_sem(), dev(zc, by, pair, core))

    own_params[...] = jnp.zeros((8, 128), jnp.float32)
    for copy in small:
        copy.wait()
    row = psf[:, 0, :]
    own_params[0:3, 0:TAPS] = row / jnp.sum(row, axis=-1, keepdims=True)
    for v in range(VIEWS):
        own_params[4 + v : 5 + v, :] = jnp.full((1, 128), wts[0, 0, v].astype(jnp.float32))

    def store_params():
        params[vw] = own_params[...]

    params_start, params_wait, params_finish = spread(
        lambda r: own_params, lambda s: params.at[s], store_params)

    pl.semaphore_wait(barrier, len(peers))
    raw_copies, outer_copies = [], []
    low, high = pl.ds(0, SHIFT), pl.ds(CX - SHIFT, SHIFT)
    inner_rows, all_rows = pl.ds(SHIFT, CY - 2 * SHIFT), pl.ds(0, CY)
    to_low, to_high = pl.ds(0, SHIFT), pl.ds(SHIFT + CX, SHIFT)

    def send_raw(planes, rows, to_planes, to_rows, device):
        return go(view.at[0, planes, rows], wide.at[to_planes, to_rows], device)

    x_moves = ((low, to_high, raw(-1, 0)), (high, to_low, raw(1, 0)))
    for planes, to_planes, device in x_moves:
        for start in (0, CY - SHIFT):
            outer_copies.append(send_raw(
                planes, pl.ds(start, SHIFT), to_planes, pl.ds(SHIFT + start, SHIFT), device))
    for planes, to_planes, device in x_moves:
        raw_copies.append(send_raw(
            planes, inner_rows, to_planes, pl.ds(2 * SHIFT, CY - 2 * SHIFT), device))
    for rows, to_rows, device in ((low, to_high, raw(0, -1)), (high, to_low, raw(0, 1))):
        raw_copies.append(send_raw(all_rows, rows, pl.ds(SHIFT, CX), to_rows, device))
    pl.when(jnp.logical_not(stays))(est_copy.start)
    params_start()

    def send_x(field):
        return [
            go(field.at[pl.ds(HALF, HALF)], field.at[pl.ds(HALF + PX, HALF)], x_left),
            go(field.at[pl.ds(PX, HALF)], field.at[pl.ds(0, HALF)], x_right),
        ]

    def wait_x(field, copies):
        for copy in copies:
            copy.wait_recv()

        @pl.when(first_x)
        def _():
            field[0:HALF] = jnp.zeros((HALF, PY, CZ), jnp.float32)

        @pl.when(last_x)
        def _():
            field[HALF + PX : WIDE_X] = jnp.zeros((HALF, PY, CZ), jnp.float32)

    def send_y(field):
        own = field.at[:, pl.ds(PY, PY)]
        return [
            go(own, field.at[:, pl.ds(2 * PY, PY)], y_left),
            go(own, field.at[:, pl.ds(0, PY)], y_right),
        ]

    pl.when(stays)(local_est.wait)
    pl.when(jnp.logical_not(stays))(est_copy.wait)

    def send_current(iteration):
        if iteration == 0:
            return [], send_x(raw_x.at[iteration])
        raw_y[iteration, :, PY : 2 * PY, :] = raw_x[iteration, HALF : HALF + PX]
        return send_y(raw_y.at[iteration]), send_x(raw_x.at[iteration])

    current_copies = send_current(0)

    for copy in outer_copies:
        copy.wait_recv()
    for planes in (to_low, to_high):
        for rows, to_rows, device in (
            (pl.ds(SHIFT, SHIFT), to_high, raw(0, -1)),
            (pl.ds(CY, SHIFT), to_low, raw(0, 1)),
        ):
            raw_copies.append(go(wide.at[planes, rows], wide.at[planes, to_rows], device))

    for s in range(VIEWS):
        params_wait(s)

    def build(v, carry):
        for t in range(TAPS):
            taps[v, t] = jnp.broadcast_to(params[v, 0:1, t : t + 1], (8, CZ))
        r = lax.broadcasted_iota(jnp.int32, (PY, 4 * WIDE_Y), 0)
        c = lax.broadcasted_iota(jnp.int32, (PY, 4 * WIDE_Y), 1)
        group, c = lax.div(c, WIDE_Y), lax.rem(c, WIDE_Y)
        distance = c - r - 1
        outside = (first_y & (c < PY)) | (last_y & (c >= 2 * PY))
        forward = jnp.zeros((PY, 4 * WIDE_Y), jnp.float32)
        backward = forward
        for t in range(TAPS):
            tap = params[v, 1:2, t : t + 1]
            forward = jnp.where(distance == t, tap, forward)
            backward = jnp.where(distance == TAPS - 1 - t, tap, backward)
        for k, band in enumerate((forward, backward)):
            upper, lower = split(jnp.where(outside, 0.0, band))
            band_y[k, v] = jnp.where(
                group < 2, upper.astype(jnp.float32), lower.astype(jnp.float32)).astype(jnp.bfloat16)
        r = lax.broadcasted_iota(jnp.int32, (CZ, CZ), 0)
        c = lax.broadcasted_iota(jnp.int32, (CZ, CZ), 1)
        distance = r - c + HALF
        forward = jnp.zeros((CZ, CZ), jnp.float32)
        backward = forward
        for t in range(TAPS):
            tap = params[v, 2:3, t : t + 1]
            forward = jnp.where(distance == t, tap, forward)
            backward = jnp.where(distance == TAPS - 1 - t, tap, backward)
        for k, band in enumerate((forward, backward)):
            upper, lower = split(band)
            for n in range(2):
                band_z[k, v, n * CZ : (n + 1) * CZ, 0:CZ] = upper
                band_z[k, v, n * CZ : (n + 1) * CZ, CZ : 2 * CZ] = lower
        return carry

    lax.fori_loop(0, VIEWS, build, 0)

    def conv_x(field, v, k, target, row):
        def tile(j, carry):
            weights = [taps[v, TAPS - 1 - t if k else t] for t in range(TAPS)]
            sums = [None] * PX
            for a in range(WIDE_X):
                value = field[a, pl.ds(pl.multiple_of(8 * j, 8), 8), :]
                for i in range(PX):
                    if 0 <= a - i < TAPS:
                        term = weights[a - i] * value
                        sums[i] = term if sums[i] is None else sums[i] + term
            for i in range(PX):
                target[i, pl.ds(pl.multiple_of(row + 8 * j, 8), 8), :] = sums[i]
            return carry

        lax.fori_loop(0, PY // 8, tile, 0)

    def conv_y(field, v, k):
        blocks = []
        for p in range(0, PX, 2):
            both = jnp.concatenate([field[p], field[p + 1]], axis=1)
            upper, lower = split(both)
            stacked = jnp.concatenate([upper, lower, upper, lower], axis=0)
            both = jnp.dot(band_y[k, v], stacked, preferred_element_type=jnp.float32)
            blocks += [both[:, :CZ], both[:, CZ:]]
        return jnp.concatenate(blocks, axis=0)

    def conv_z(value, v, k):
        both = jnp.concatenate(split(value), axis=1)
        both = jnp.dot(both, band_z[k, v], preferred_element_type=jnp.float32)
        return both[:, :CZ] + both[:, CZ:]

    def store_aligned():
        aligned[vw] = own_aligned[piece(part), piece(core), :]

    aligned_start, aligned_wait, aligned_finish = spread(
        lambda r: own_aligned.at[piece(r // 2), piece(r % 2)], lambda s: aligned.at[s], store_aligned)

    def align():
        local_view.wait()
        for copy in raw_copies:
            copy.wait_recv()
        ox, oy, oz = off[0, 0, 0, 0], off[0, 0, 0, 1], off[0, 0, 0, 2]
        gy = by * CY + oy + lax.broadcasted_iota(jnp.int32, (CY, CZ), 0)
        gz = oz + lax.broadcasted_iota(jnp.int32, (CY, CZ), 1)
        inside = (gy >= 0) & (gy < nx * CY) & (gz >= 0) & (gz < CZ)
        turn = lax.rem(CZ - oz, CZ)

        def planes(n, carry):
            for i in range(8):
                p = 8 * n + i
                value = wide[SHIFT + ox + p, pl.ds(SHIFT + oy, CY), :]
                value = pltpu.roll(value, turn, 1)
                gx = bx * CX + ox + p
                ok = inside & (gx >= 0) & (gx < 2 * nz * CX)
                own_aligned[p] = jnp.where(ok, value, -1.0)
            return carry

        for n in range(2):
            lax.fori_loop(2 * n, 2 * n + 2, planes, 0)
            pl.when(core == 0)(functools.partial(aligned_start, (2 * n, 2 * n + 1), n == 1))

    weights = params[0, 4:8, :]
    total = jnp.sum(weights, axis=0, keepdims=True)


    def begin_x(iteration, k, v, source):
        field = x_wide.at[iteration, k, v]
        field[HALF : HALF + PX] = source.reshape(PX, PY, CZ)
        return send_x(field)

    def begin_y(iteration, k, v, source):
        field = y_wide.at[iteration, k, v]
        field[:, PY : 2 * PY, :] = source.reshape(PX, PY, CZ)
        return send_y(field)

    def end_x(iteration, k, v, copies):
        field = x_wide.at[iteration, k, v]
        wait_x(field, copies)
        conv_x(field, v, k, value.at[v], 0)
        return value[v].reshape(PX * PY, CZ)

    def end_y(iteration, k, v, copies):
        for copy in copies:
            copy.wait_recv()
        return conv_y(y_wide.at[iteration, k, v], v, k)

    for iteration in range(ITERS):
        if iteration == 0:
            x_first, x_first_back = (True,) * VIEWS, (True, True, False, False)
            order, order_back = (0, 2, 1, 3), (2, 0, 3, 1)
            align()
        else:
            x_first, x_first_back = (True, True, False, False), (False, True, True, False)
            order, order_back = (2, 0, 1, 3), (0, 2, 3, 1)
        copies = {}
        for copy in current_copies[0]:
            copy.wait_recv()
        for v in range(VIEWS):
            if not x_first[v]:
                copies[v] = begin_x(iteration, 0, v, conv_y(raw_y.at[iteration], v, 0))
        wait_x(raw_x.at[iteration], current_copies[1])
        for v in range(VIEWS):
            if x_first[v]:
                field = y_wide.at[iteration, 0, v]
                conv_x(raw_x.at[iteration], v, 0, field, PY)
                copies[v] = send_y(field)
        if iteration == 0:
            pl.when(core == 1)(aligned_start)
        for v in order:
            blurred = (end_y if x_first[v] else end_x)(iteration, 0, v, copies[v])
            blurred = conv_z(blurred, v, 0)
            if iteration == 0:
                aligned_wait(v)
            recorded = aligned[v].reshape(PX * PY, CZ)
            ratio = jnp.where(recorded >= 0.0, recorded / blurred, 1.0)
            back = conv_z(ratio, v, 1)
            copies[v] = (begin_x if x_first_back[v] else begin_y)(iteration, 1, v, back)
        for v in order_back:
            if x_first_back[v]:
                wait_x(x_wide.at[iteration, 1, v], copies[v])
                field = y_wide.at[iteration, 1, v]
                conv_x(x_wide.at[iteration, 1, v], v, 1, field, PY)
                copies[v] = send_y(field)
            else:
                copies[v] = begin_x(iteration, 1, v, end_y(iteration, 1, v, copies[v]))
        for n, v in enumerate(order_back):
            back = (end_y if x_first_back[v] else end_x)(iteration, 1, v, copies[v])
            term = params[0, 4 + v : 5 + v, :] * jnp.log(back)
            summed[...] = term if n == 0 else summed[...] + term
        update = jnp.exp(summed[...] / total).reshape(PX, PY, CZ)
        updated = raw_x[iteration, HALF : HALF + PX] * update
        if iteration + 1 < ITERS:
            raw_x[iteration + 1, HALF : HALF + PX] = updated
            current_copies = send_current(iteration + 1)
        else:
            result[...] = updated

    shared = PX // 2
    own_target = out.at[piece(part), piece(core)]
    chip_mate = dev(zc, by, y, other)
    base = new_sem(4)
    mate_copy = remote(result, own_target, new_sem(), chip_mate)
    results = []
    for n in range(2):
        y_ = side + 2 * n
        for c in range(2):
            copy = remote(
                result.at[pl.ds(c * shared, shared)],
                out.at[pl.ds(part * PX + c * shared, shared), piece(core)],
                base + 2 * n + c, dev(zc, by, y_, c), base + 2 * part + core)
            results.append((y_ != y, copy))
    for away, copy in results:
        pl.when(away)(copy.start)

    @pl.when(stays)
    def _():
        mate_copy.start()
        own_target[...] = result[...]

    base_mate = new_sem(4)
    forwards = []
    for s in range(4):
        away = chip_at(zc, 2 * y_lo + s // 2) != y
        got, missing = [
            out.at[pl.ds(s // 2 * PX + c * shared, shared), piece(s % 2)] for c in (core, other)
        ]
        arrival = remote(got, got, base + s, x_left)
        forward = remote(got, got, base_mate + s, chip_mate)
        missed = remote(missing, missing, base_mate + s, chip_mate)

        @pl.when(away)
        def _(arrival=arrival, forward=forward):
            arrival.wait_recv()
            forward.start()

        forwards.append((away, forward, missed))

    @pl.when(stays)
    def _():
        mate_copy.wait()

    for away, forward, missed in forwards:

        @pl.when(away)
        def _(forward=forward, missed=missed):
            missed.wait_recv()
            forward.wait_send()

    for away, copy in results:
        pl.when(away)(copy.wait_send)
    params_finish()
    aligned_finish()
    for copy in sent:
        copy.wait_send()


def solution(mesh):
    nz, nx = mesh.shape["bx"] // 2, mesh.shape["by"]
    f32, bf16 = jnp.float32, jnp.bfloat16

    def shards(estimate, views_raw, psf_taps, offsets, view_weights):
        vmem = pl.BlockSpec(memory_space=pltpu.VMEM)
        hbm = pl.BlockSpec(memory_space=pltpu.HBM)
        return pl.pallas_call(
            functools.partial(kernel, (nz, nx)),
            out_shape=jax.ShapeDtypeStruct((CX, CY, CZ), f32),
            in_specs=[hbm] * 5,
            out_specs=vmem,
            scratch_shapes=[
                pltpu.VMEM((ITERS, WIDE_X, PY, CZ), f32),
                pltpu.VMEM((ITERS, PX, WIDE_Y, CZ), f32),
                pltpu.VMEM((ITERS, 2, VIEWS, WIDE_X, PY, CZ), f32),
                pltpu.VMEM((ITERS, 2, VIEWS, PX, WIDE_Y, CZ), f32),
                pltpu.VMEM((VIEWS, PX, PY, CZ), f32),
                pltpu.VMEM((PX * PY, CZ), f32),
                pltpu.VMEM((PX, PY, CZ), f32),
                pltpu.VMEM((3, 1, TAPS), f32),
                pltpu.SMEM((1, 1, 1, 3), jnp.int32),
                pltpu.SMEM((1, 1, VIEWS), jnp.int32),
                pltpu.VMEM((CX + 2 * SHIFT, CY + 2 * SHIFT, CZ), f32),
                pltpu.VMEM((CX, CY, CZ), f32),
                pltpu.VMEM((VIEWS, PX, PY, CZ), f32),
                pltpu.VMEM((8, 128), f32),
                pltpu.VMEM((VIEWS, 8, 128), f32),
                pltpu.VMEM((VIEWS, TAPS, 8, CZ), f32),
                pltpu.VMEM((2, VIEWS, PY, 4 * WIDE_Y), bf16),
                pltpu.VMEM((2, VIEWS, 2 * CZ, 2 * CZ), bf16),
                pltpu.SemaphoreType.DMA((N_SEMS,)),
                pltpu.SemaphoreType.DMA((N_SEMS,)),
                pltpu.SemaphoreType.DMA((5,)),
            ],
            compiler_params=pltpu.CompilerParams(
                collective_id=0, has_side_effects=True, vmem_limit_bytes=53 * 1024 * 1024
            ),
            cost_estimate=pl.CostEstimate(flops=10**9, bytes_accessed=2 * 10**6, transcendentals=10**6),
        )(
            estimate,
            views_raw,
            jnp.transpose(psf_taps, (1, 0, 2)),
            offsets,
            jnp.transpose(view_weights, (1, 2, 0)),
        )

    return jax.shard_map(
        shards,
        mesh=mesh,
        in_specs=(
            P("bx", "by", None),
            P("view", "bx", "by", None),
            P("view", None, None),
            P("view", "bx", "by", None),
            P(None, "bx", "by"),
        ),
        out_specs=P("bx", "by", None),
        check_vma=False,
    )
```

```python
import functools

import jax
import jax.numpy as jnp
from jax import lax
from jax.experimental import pallas as pl
from jax.experimental.pallas import tpu as pltpu
from jax.sharding import PartitionSpec as P

ITERS = 2
TAPS = 31
HALF = 15
SHIFT = 8
VIEWS = 4
CX, CY, CZ = 32, 32, 128
PX, PY = 16, 16
WIDE_X = PX + 2 * HALF
WIDE_Y = 3 * PY
N_SEMS = 128
MESH = pl.DeviceIdType.MESH


def split(value):
    high = value.astype(jnp.bfloat16)
    low = (value - high.astype(jnp.float32)).astype(jnp.bfloat16)
    return high, low


def kernel(
    sizes,
    est, view, psf_hbm, off_hbm, wts_hbm,
    out,
    raw_x, raw_y, x_wide, y_wide, value, summed, result, psf, off, wts, wide, own_aligned, aligned, own_params, params,
    taps, band_y, band_z,
    send_sem, recv_sem, local_sem,
):
    nz, nx = sizes
    bx, by, vw = lax.axis_index("bx"), lax.axis_index("by"), lax.axis_index("view")
    zc, y_lo = lax.div(bx, 2), lax.rem(bx, 2)
    y_hi, core = lax.div(vw, 2), lax.rem(vw, 2)
    y = 2 * y_hi + y_lo
    other = 1 - core
    pos = jnp.where(lax.rem(zc, 2) == 0, y, 3 - y)
    side, part = lax.div(pos, 2), lax.rem(pos, 2)
    stays = side == y_lo

    def dev(zc_, x_, y_, core_):
        return (zc_ * 2 + lax.rem(y_, 2), x_, lax.div(y_, 2) * 2 + core_)

    def chip_at(zc_, pos_):
        return jnp.where(lax.rem(zc_, 2) == 0, pos_, 3 - pos_)

    def along_x(step):
        place = lax.rem(4 * zc + pos + 4 * nz + step, 4 * nz)
        zc_, pos_ = lax.div(place, 4), lax.rem(place, 4)
        return dev(zc_, by, chip_at(zc_, pos_), core)

    def along_y(step):
        place = lax.rem(2 * by + core + 2 * nx + step, 2 * nx)
        return dev(zc, lax.div(place, 2), y, lax.rem(place, 2))

    x_left, x_right = along_x(-1), along_x(1)
    y_left, y_right = along_y(-1), along_y(1)
    first_x, last_x = (zc == 0) & (pos == 0), (zc == nz - 1) & (pos == 3)
    first_y, last_y = (by == 0) & (core == 0), (by == nx - 1) & (core == 1)

    def raw(step_x, step_y):
        return (lax.rem(bx + 2 * nz + step_x, 2 * nz), lax.rem(by + nx + step_y, nx), vw)

    far_y = dev(zc, lax.rem(by + nx + jnp.where(core == 0, -1, 1), nx), y, other)
    raw_far = raw(jnp.where(y_lo == 0, -1, 1), 0)
    barrier = pltpu.get_barrier_semaphore()
    peers = [dev(zc, by, lax.rem(y + d, 4), core) for d in (1, 2, 3)]
    peers += [dev(zc, by, lax.rem(y + d, 4), other) for d in (0, 1, 2, 3)]
    peers += [dev(lax.rem(zc + nz + d, nz), by, y, core) for d in (-1, 1)]
    peers += [far_y, raw_far, raw(0, -1), raw(0, 1)]
    for peer in peers:
        pl.semaphore_signal(barrier, inc=1, device_id=peer, device_id_type=MESH)

    used = [0]
    sent = []

    def new_sem(count=1):
        first = used[0]
        used[0] += count
        return first

    def remote(src, dst, sem, device, at=None):
        return pltpu.make_async_remote_copy(
            src_ref=src, dst_ref=dst, send_sem=send_sem.at[sem],
            recv_sem=recv_sem.at[sem if at is None else at],
            device_id=device, device_id_type=MESH)

    def go(src, dst, device):
        copy = remote(src, dst, new_sem(), device)
        copy.start()
        sent.append(copy)
        return copy

    def piece(n):
        return pl.ds(n * PX, PX)

    def spread(source_at, target, own_store):
        base = new_sem(4)
        copies = []
        for r in range(4):
            y_, core_ = chip_at(zc, 2 * y_lo + r // 2), r % 2
            me = (y_ == y) & (core_ == core)
            copy = remote(source_at(r), target(vw), base + r, dev(zc, by, y_, core_), base + vw)
            copies.append((me, copy))

        def start(chosen=range(4), last=True):
            for r in chosen:
                me, copy = copies[r]
                pl.when(jnp.logical_not(me))(copy.start)

            if last:

                @pl.when(stays)
                def _():
                    own_store()

        def wait(s):
            @pl.when(jnp.logical_not(stays & (vw == s)))
            def _():
                remote(target(s), target(s), base + s, x_left).wait_recv()

        def finish():
            for me, copy in copies:
                pl.when(jnp.logical_not(me))(copy.wait_send)

        return start, wait, finish

    local_view = pltpu.make_async_copy(
        view.at[0], wide.at[pl.ds(SHIFT, CX), pl.ds(SHIFT, CY)], local_sem.at[0])
    local_view.start()
    small = [
        pltpu.make_async_copy(src, dst, local_sem.at[2 + n])
        for n, (src, dst) in enumerate(((psf_hbm, psf), (wts_hbm, wts), (off_hbm, off)))
    ]
    for copy in small:
        copy.start()
    own_block = raw_x.at[0, pl.ds(HALF, PX)]
    local_est = pltpu.make_async_copy(
        est.at[piece(part), piece(core)], own_block, local_sem.at[1])
    pl.when(stays)(local_est.start)
    pair = jnp.where(y_lo == 0, lax.rem(y + 3, 4), lax.rem(y + 1, 4))
    pair_part = lax.rem(jnp.where(lax.rem(zc, 2) == 0, pair, 3 - pair), 2)
    est_copy = remote(
        est.at[piece(pair_part), piece(core)], own_block, new_sem(), dev(zc, by, pair, core))

    own_params[...] = jnp.zeros((8, 128), jnp.float32)
    for copy in small:
        copy.wait()
    row = psf[:, 0, :]
    own_params[0:3, 0:TAPS] = row / jnp.sum(row, axis=-1, keepdims=True)
    for v in range(VIEWS):
        own_params[4 + v : 5 + v, :] = jnp.full((1, 128), wts[0, 0, v].astype(jnp.float32))

    def store_params():
        params[vw] = own_params[...]

    params_start, params_wait, params_finish = spread(
        lambda r: own_params, lambda s: params.at[s], store_params)

    pl.semaphore_wait(barrier, len(peers))
    raw_copies, outer_copies = [], []
    low, high = pl.ds(0, SHIFT), pl.ds(CX - SHIFT, SHIFT)
    inner_rows, all_rows = pl.ds(SHIFT, CY - 2 * SHIFT), pl.ds(0, CY)
    to_low, to_high = pl.ds(0, SHIFT), pl.ds(SHIFT + CX, SHIFT)

    def send_raw(planes, rows, to_planes, to_rows, device):
        return go(view.at[0, planes, rows], wide.at[to_planes, to_rows], device)

    x_moves = ((low, to_high, raw(-1, 0)), (high, to_low, raw(1, 0)))
    for planes, to_planes, device in x_moves:
        for start in (0, CY - SHIFT):
            outer_copies.append(send_raw(
                planes, pl.ds(start, SHIFT), to_planes, pl.ds(SHIFT + start, SHIFT), device))
    for planes, to_planes, device in x_moves:
        raw_copies.append(send_raw(
            planes, inner_rows, to_planes, pl.ds(2 * SHIFT, CY - 2 * SHIFT), device))
    for rows, to_rows, device in ((low, to_high, raw(0, -1)), (high, to_low, raw(0, 1))):
        raw_copies.append(send_raw(all_rows, rows, pl.ds(SHIFT, CX), to_rows, device))
    pl.when(jnp.logical_not(stays))(est_copy.start)
    params_start()

    def send_x(field):
        return [
            go(field.at[pl.ds(HALF, HALF)], field.at[pl.ds(HALF + PX, HALF)], x_left),
            go(field.at[pl.ds(PX, HALF)], field.at[pl.ds(0, HALF)], x_right),
        ]

    def wait_x(field, copies):
        for copy in copies:
            copy.wait_recv()

        @pl.when(first_x)
        def _():
            field[0:HALF] = jnp.zeros((HALF, PY, CZ), jnp.float32)

        @pl.when(last_x)
        def _():
            field[HALF + PX : WIDE_X] = jnp.zeros((HALF, PY, CZ), jnp.float32)

    def send_y(field):
        own = field.at[:, pl.ds(PY, PY)]
        return [
            go(own, field.at[:, pl.ds(2 * PY, PY)], y_left),
            go(own, field.at[:, pl.ds(0, PY)], y_right),
        ]

    pl.when(stays)(local_est.wait)
    pl.when(jnp.logical_not(stays))(est_copy.wait)

    def send_current(iteration):
        if iteration == 0:
            return [], send_x(raw_x.at[iteration])
        raw_y[iteration, :, PY : 2 * PY, :] = raw_x[iteration, HALF : HALF + PX]
        return send_y(raw_y.at[iteration]), send_x(raw_x.at[iteration])

    current_copies = send_current(0)

    for copy in outer_copies:
        copy.wait_recv()
    for planes in (to_low, to_high):
        for rows, to_rows, device in (
            (pl.ds(SHIFT, SHIFT), to_high, raw(0, -1)),
            (pl.ds(CY, SHIFT), to_low, raw(0, 1)),
        ):
            raw_copies.append(go(wide.at[planes, rows], wide.at[planes, to_rows], device))

    for s in range(VIEWS):
        params_wait(s)

    def build(v, carry):
        for t in range(TAPS):
            taps[v, t] = jnp.broadcast_to(params[v, 0:1, t : t + 1], (8, CZ))
        r = lax.broadcasted_iota(jnp.int32, (PY, 3 * WIDE_Y), 0)
        c = lax.broadcasted_iota(jnp.int32, (PY, 3 * WIDE_Y), 1)
        group, c = lax.div(c, WIDE_Y), lax.rem(c, WIDE_Y)
        distance = c - r - 1
        outside = (first_y & (c < PY)) | (last_y & (c >= 2 * PY))
        forward = jnp.zeros((PY, 3 * WIDE_Y), jnp.float32)
        backward = forward
        for t in range(TAPS):
            tap = params[v, 1:2, t : t + 1]
            forward = jnp.where(distance == t, tap, forward)
            backward = jnp.where(distance == TAPS - 1 - t, tap, backward)
        for k, band in enumerate((forward, backward)):
            upper, lower = split(jnp.where(outside, 0.0, band))
            band_y[k, v] = jnp.where(
                group < 2, upper.astype(jnp.float32), lower.astype(jnp.float32)).astype(jnp.bfloat16)
        r = lax.broadcasted_iota(jnp.int32, (CZ, CZ), 0)
        c = lax.broadcasted_iota(jnp.int32, (CZ, CZ), 1)
        distance = r - c + HALF
        forward = jnp.zeros((CZ, CZ), jnp.float32)
        backward = forward
        for t in range(TAPS):
            tap = params[v, 2:3, t : t + 1]
            forward = jnp.where(distance == t, tap, forward)
            backward = jnp.where(distance == TAPS - 1 - t, tap, backward)
        for k, band in enumerate((forward, backward)):
            upper, lower = split(band)
            for n in range(2):
                band_z[k, v, n * CZ : (n + 1) * CZ, 0:CZ] = upper
                band_z[k, v, n * CZ : (n + 1) * CZ, CZ : 2 * CZ] = lower
        return carry

    lax.fori_loop(0, VIEWS, build, 0)

    def conv_x(field, v, k, target, row):
        def tile(j, carry):
            weights = [taps[v, TAPS - 1 - t if k else t] for t in range(TAPS)]
            sums = [None] * PX
            for a in range(WIDE_X):
                value = field[a, pl.ds(pl.multiple_of(8 * j, 8), 8), :]
                for i in range(PX):
                    if 0 <= a - i < TAPS:
                        term = weights[a - i] * value
                        sums[i] = term if sums[i] is None else sums[i] + term
            for i in range(PX):
                target[i, pl.ds(pl.multiple_of(row + 8 * j, 8), 8), :] = sums[i]
            return carry

        lax.fori_loop(0, PY // 8, tile, 0)

    def conv_y(field, v, k):
        blocks = []
        for p in range(0, PX, 2):
            both = jnp.concatenate([field[p], field[p + 1]], axis=1)
            upper, lower = split(both)
            stacked = jnp.concatenate([upper, lower, upper], axis=0)
            both = jnp.dot(band_y[k, v], stacked, preferred_element_type=jnp.float32)
            blocks += [both[:, :CZ], both[:, CZ:]]
        return jnp.concatenate(blocks, axis=0)

    def conv_z(value, v, k):
        both = jnp.concatenate(split(value), axis=1)
        both = jnp.dot(both, band_z[k, v], preferred_element_type=jnp.float32)
        return both[:, :CZ] + both[:, CZ:]

    def store_aligned():
        aligned[vw] = own_aligned[piece(part), piece(core), :]

    aligned_start, aligned_wait, aligned_finish = spread(
        lambda r: own_aligned.at[piece(r // 2), piece(r % 2)], lambda s: aligned.at[s], store_aligned)

    def align():
        local_view.wait()
        for copy in raw_copies:
            copy.wait_recv()
        ox, oy, oz = off[0, 0, 0, 0], off[0, 0, 0, 1], off[0, 0, 0, 2]
        gy = by * CY + oy + lax.broadcasted_iota(jnp.int32, (CY, CZ), 0)
        gz = oz + lax.broadcasted_iota(jnp.int32, (CY, CZ), 1)
        inside = (gy >= 0) & (gy < nx * CY) & (gz >= 0) & (gz < CZ)
        turn = lax.rem(CZ - oz, CZ)

        def planes(n, carry):
            for i in range(8):
                p = 8 * n + i
                value = wide[SHIFT + ox + p, pl.ds(SHIFT + oy, CY), :]
                value = pltpu.roll(value, turn, 1)
                gx = bx * CX + ox + p
                ok = inside & (gx >= 0) & (gx < 2 * nz * CX)
                own_aligned[p] = jnp.where(ok, value, -1.0)
            return carry

        for n in range(2):
            lax.fori_loop(2 * n, 2 * n + 2, planes, 0)
            pl.when(core == 0)(functools.partial(aligned_start, (2 * n, 2 * n + 1), n == 1))

    weights = params[0, 4:8, :]
    total = jnp.sum(weights, axis=0, keepdims=True)


    def begin_x(iteration, k, v, source):
        field = x_wide.at[iteration, k, v]
        field[HALF : HALF + PX] = source.reshape(PX, PY, CZ)
        return send_x(field)

    def begin_y(iteration, k, v, source):
        field = y_wide.at[iteration, k, v]
        field[:, PY : 2 * PY, :] = source.reshape(PX, PY, CZ)
        return send_y(field)

    def end_x(iteration, k, v, copies):
        field = x_wide.at[iteration, k, v]
        wait_x(field, copies)
        conv_x(field, v, k, value.at[v], 0)
        return value[v].reshape(PX * PY, CZ)

    def end_y(iteration, k, v, copies):
        for copy in copies:
            copy.wait_recv()
        return conv_y(y_wide.at[iteration, k, v], v, k)

    for iteration in range(ITERS):
        if iteration == 0:
            x_first, x_first_back = (True,) * VIEWS, (True, True, False, False)
            order, order_back = (0, 2, 1, 3), (2, 0, 3, 1)
            align()
        else:
            x_first, x_first_back = (True, True, False, False), (False, False, True, True)
            order, order_back = (2, 0, 1, 3), (0, 2, 1, 3)
        copies = {}
        for copy in current_copies[0]:
            copy.wait_recv()
        for v in range(VIEWS):
            if not x_first[v]:
                copies[v] = begin_x(iteration, 0, v, conv_y(raw_y.at[iteration], v, 0))
        wait_x(raw_x.at[iteration], current_copies[1])
        for v in range(VIEWS):
            if x_first[v]:
                field = y_wide.at[iteration, 0, v]
                conv_x(raw_x.at[iteration], v, 0, field, PY)
                copies[v] = send_y(field)
        if iteration == 0:
            pl.when(core == 1)(aligned_start)
        for v in order:
            blurred = (end_y if x_first[v] else end_x)(iteration, 0, v, copies[v])
            blurred = conv_z(blurred, v, 0)
            if iteration == 0:
                aligned_wait(v)
            recorded = aligned[v].reshape(PX * PY, CZ)
            ratio = jnp.where(recorded >= 0.0, recorded / blurred, 1.0)
            back = conv_z(ratio, v, 1)
            copies[v] = (begin_x if x_first_back[v] else begin_y)(iteration, 1, v, back)
        for v in order_back:
            if x_first_back[v]:
                wait_x(x_wide.at[iteration, 1, v], copies[v])
                field = y_wide.at[iteration, 1, v]
                conv_x(x_wide.at[iteration, 1, v], v, 1, field, PY)
                copies[v] = send_y(field)
            else:
                copies[v] = begin_x(iteration, 1, v, end_y(iteration, 1, v, copies[v]))
        for n, v in enumerate(order_back):
            back = (end_y if x_first_back[v] else end_x)(iteration, 1, v, copies[v])
            term = params[0, 4 + v : 5 + v, :] * jnp.log(back)
            summed[...] = term if n == 0 else summed[...] + term
        update = jnp.exp(summed[...] / total).reshape(PX, PY, CZ)
        updated = raw_x[iteration, HALF : HALF + PX] * update
        if iteration + 1 < ITERS:
            raw_x[iteration + 1, HALF : HALF + PX] = updated
            current_copies = send_current(iteration + 1)
        else:
            result[...] = updated

    shared = PX // 2
    own_target = out.at[piece(part), piece(core)]
    chip_mate = dev(zc, by, y, other)
    base = new_sem(4)
    mate_copy = remote(result, own_target, new_sem(), chip_mate)
    results = []
    for n in range(2):
        y_ = side + 2 * n
        for c in range(2):
            copy = remote(
                result.at[pl.ds(c * shared, shared)],
                out.at[pl.ds(part * PX + c * shared, shared), piece(core)],
                base + 2 * n + c, dev(zc, by, y_, c), base + 2 * part + core)
            results.append((y_ != y, copy))
    for away, copy in results:
        pl.when(away)(copy.start)

    @pl.when(stays)
    def _():
        mate_copy.start()
        own_target[...] = result[...]

    params_finish()
    aligned_finish()
    for copy in sent:
        copy.wait_send()

    base_mate = new_sem(4)
    forwards = []
    for s in (2, 3, 0, 1):
        away = chip_at(zc, 2 * y_lo + s // 2) != y
        got, missing = [
            out.at[pl.ds(s // 2 * PX + c * shared, shared), piece(s % 2)] for c in (core, other)
        ]
        arrival = remote(got, got, base + s, x_left)
        forward = remote(got, got, base_mate + s, chip_mate)
        missed = remote(missing, missing, base_mate + s, chip_mate)

        @pl.when(away)
        def _(arrival=arrival, forward=forward):
            arrival.wait_recv()
            forward.start()

        forwards.append((away, forward, missed))

    @pl.when(stays)
    def _():
        mate_copy.wait()

    for away, forward, missed in forwards:

        @pl.when(away)
        def _(forward=forward, missed=missed):
            missed.wait_recv()
            forward.wait_send()

    for away, copy in results:
        pl.when(away)(copy.wait_send)


def solution(mesh):
    nz, nx = mesh.shape["bx"] // 2, mesh.shape["by"]
    f32, bf16 = jnp.float32, jnp.bfloat16

    def shards(estimate, views_raw, psf_taps, offsets, view_weights):
        vmem = pl.BlockSpec(memory_space=pltpu.VMEM)
        hbm = pl.BlockSpec(memory_space=pltpu.HBM)
        return pl.pallas_call(
            functools.partial(kernel, (nz, nx)),
            out_shape=jax.ShapeDtypeStruct((CX, CY, CZ), f32),
            in_specs=[hbm] * 5,
            out_specs=vmem,
            scratch_shapes=[
                pltpu.VMEM((ITERS, WIDE_X, PY, CZ), f32),
                pltpu.VMEM((ITERS, PX, WIDE_Y, CZ), f32),
                pltpu.VMEM((ITERS, 2, VIEWS, WIDE_X, PY, CZ), f32),
                pltpu.VMEM((ITERS, 2, VIEWS, PX, WIDE_Y, CZ), f32),
                pltpu.VMEM((VIEWS, PX, PY, CZ), f32),
                pltpu.VMEM((PX * PY, CZ), f32),
                pltpu.VMEM((PX, PY, CZ), f32),
                pltpu.VMEM((3, 1, TAPS), f32),
                pltpu.SMEM((1, 1, 1, 3), jnp.int32),
                pltpu.SMEM((1, 1, VIEWS), jnp.int32),
                pltpu.VMEM((CX + 2 * SHIFT, CY + 2 * SHIFT, CZ), f32),
                pltpu.VMEM((CX, CY, CZ), f32),
                pltpu.VMEM((VIEWS, PX, PY, CZ), f32),
                pltpu.VMEM((8, 128), f32),
                pltpu.VMEM((VIEWS, 8, 128), f32),
                pltpu.VMEM((VIEWS, TAPS, 8, CZ), f32),
                pltpu.VMEM((2, VIEWS, PY, 3 * WIDE_Y), bf16),
                pltpu.VMEM((2, VIEWS, 2 * CZ, 2 * CZ), bf16),
                pltpu.SemaphoreType.DMA((N_SEMS,)),
                pltpu.SemaphoreType.DMA((N_SEMS,)),
                pltpu.SemaphoreType.DMA((5,)),
            ],
            compiler_params=pltpu.CompilerParams(
                collective_id=0, has_side_effects=True, vmem_limit_bytes=53 * 1024 * 1024
            ),
            cost_estimate=pl.CostEstimate(flops=10**9, bytes_accessed=2 * 10**6, transcendentals=10**6),
        )(
            estimate,
            views_raw,
            jnp.transpose(psf_taps, (1, 0, 2)),
            offsets,
            jnp.transpose(view_weights, (1, 2, 0)),
        )

    return jax.shard_map(
        shards,
        mesh=mesh,
        in_specs=(
            P("bx", "by", None),
            P("view", "bx", "by", None),
            P("view", None, None),
            P("view", "bx", "by", None),
            P(None, "bx", "by"),
        ),
        out_specs=P("bx", "by", None),
        check_vma=False,
    )
```

```python
import functools

import jax
import jax.numpy as jnp
from jax import lax
from jax.experimental import pallas as pl
from jax.experimental.pallas import tpu as pltpu
from jax.sharding import PartitionSpec as P

ITERS = 2
TAPS = 31
HALF = 15
SHIFT = 8
VIEWS = 4
CX, CY, CZ = 32, 32, 128
PX, PY = 16, 16
WIDE_X = PX + 2 * HALF
WIDE_Y = 3 * PY
N_SEMS = 128
MESH = pl.DeviceIdType.MESH


def split(value):
    high = value.astype(jnp.bfloat16)
    low = (value - high.astype(jnp.float32)).astype(jnp.bfloat16)
    return high, low


def kernel(
    sizes,
    est, view, psf_hbm, off_hbm, wts_hbm,
    out,
    raw_x, raw_y, x_wide, y_wide, value, summed, result, psf, off, wts, wide, own_aligned, aligned, own_params, params,
    taps, band_y, band_z,
    send_sem, recv_sem, local_sem,
):
    nz, nx = sizes
    bx, by, vw = lax.axis_index("bx"), lax.axis_index("by"), lax.axis_index("view")
    zc, y_lo = lax.div(bx, 2), lax.rem(bx, 2)
    y_hi, core = lax.div(vw, 2), lax.rem(vw, 2)
    y = 2 * y_hi + y_lo
    other = 1 - core
    pos = jnp.where(lax.rem(zc, 2) == 0, y, 3 - y)
    side, part = lax.div(pos, 2), lax.rem(pos, 2)
    stays = side == y_lo

    def dev(zc_, x_, y_, core_):
        return (zc_ * 2 + lax.rem(y_, 2), x_, lax.div(y_, 2) * 2 + core_)

    def chip_at(zc_, pos_):
        return jnp.where(lax.rem(zc_, 2) == 0, pos_, 3 - pos_)

    def along_x(step):
        place = lax.rem(4 * zc + pos + 4 * nz + step, 4 * nz)
        zc_, pos_ = lax.div(place, 4), lax.rem(place, 4)
        return dev(zc_, by, chip_at(zc_, pos_), core)

    def along_y(step):
        place = lax.rem(2 * by + core + 2 * nx + step, 2 * nx)
        return dev(zc, lax.div(place, 2), y, lax.rem(place, 2))

    x_left, x_right = along_x(-1), along_x(1)
    y_left, y_right = along_y(-1), along_y(1)
    first_x, last_x = (zc == 0) & (pos == 0), (zc == nz - 1) & (pos == 3)
    first_y, last_y = (by == 0) & (core == 0), (by == nx - 1) & (core == 1)

    def raw(step_x, step_y):
        return (lax.rem(bx + 2 * nz + step_x, 2 * nz), lax.rem(by + nx + step_y, nx), vw)

    far_y = dev(zc, lax.rem(by + nx + jnp.where(core == 0, -1, 1), nx), y, other)
    raw_far = raw(jnp.where(y_lo == 0, -1, 1), 0)
    barrier = pltpu.get_barrier_semaphore()
    peers = [dev(zc, by, lax.rem(y + d, 4), core) for d in (1, 2, 3)]
    peers += [dev(zc, by, lax.rem(y + d, 4), other) for d in (0, 1, 2, 3)]
    peers += [dev(lax.rem(zc + nz + d, nz), by, y, core) for d in (-1, 1)]
    peers += [far_y, raw_far, raw(0, -1), raw(0, 1)]
    for peer in peers:
        pl.semaphore_signal(barrier, inc=1, device_id=peer, device_id_type=MESH)

    used = [0]
    sent = []

    def new_sem(count=1):
        first = used[0]
        used[0] += count
        return first

    def remote(src, dst, sem, device, at=None):
        return pltpu.make_async_remote_copy(
            src_ref=src, dst_ref=dst, send_sem=send_sem.at[sem],
            recv_sem=recv_sem.at[sem if at is None else at],
            device_id=device, device_id_type=MESH)

    def go(src, dst, device):
        copy = remote(src, dst, new_sem(), device)
        copy.start()
        sent.append(copy)
        return copy

    def piece(n):
        return pl.ds(n * PX, PX)

    def spread(source_at, target, own_store):
        base = new_sem(4)
        copies = []
        for r in range(4):
            y_, core_ = chip_at(zc, 2 * y_lo + r // 2), r % 2
            me = (y_ == y) & (core_ == core)
            copy = remote(source_at(r), target(vw), base + r, dev(zc, by, y_, core_), base + vw)
            copies.append((me, copy))

        def start(chosen=range(4), last=True):
            for r in chosen:
                me, copy = copies[r]
                pl.when(jnp.logical_not(me))(copy.start)

            if last:

                @pl.when(stays)
                def _():
                    own_store()

        def wait(s):
            @pl.when(jnp.logical_not(stays & (vw == s)))
            def _():
                remote(target(s), target(s), base + s, x_left).wait_recv()

        def finish():
            for me, copy in copies:
                pl.when(jnp.logical_not(me))(copy.wait_send)

        return start, wait, finish

    local_view = pltpu.make_async_copy(
        view.at[0], wide.at[pl.ds(SHIFT, CX), pl.ds(SHIFT, CY)], local_sem.at[0])
    local_view.start()
    small = [
        pltpu.make_async_copy(src, dst, local_sem.at[2 + n])
        for n, (src, dst) in enumerate(((psf_hbm, psf), (wts_hbm, wts), (off_hbm, off)))
    ]
    for copy in small:
        copy.start()
    own_block = raw_x.at[0, pl.ds(HALF, PX)]
    local_est = pltpu.make_async_copy(
        est.at[piece(part), piece(core)], own_block, local_sem.at[1])
    pl.when(stays)(local_est.start)
    pair = jnp.where(y_lo == 0, lax.rem(y + 3, 4), lax.rem(y + 1, 4))
    pair_part = lax.rem(jnp.where(lax.rem(zc, 2) == 0, pair, 3 - pair), 2)
    est_copy = remote(
        est.at[piece(pair_part), piece(core)], own_block, new_sem(), dev(zc, by, pair, core))

    own_params[...] = jnp.zeros((8, 128), jnp.float32)
    for copy in small:
        copy.wait()
    row = psf[:, 0, :]
    own_params[0:3, 0:TAPS] = row / jnp.sum(row, axis=-1, keepdims=True)
    for v in range(VIEWS):
        own_params[4 + v : 5 + v, :] = jnp.full((1, 128), wts[0, 0, v].astype(jnp.float32))

    def store_params():
        params[vw] = own_params[...]

    params_start, params_wait, params_finish = spread(
        lambda r: own_params, lambda s: params.at[s], store_params)

    pl.semaphore_wait(barrier, len(peers))
    pl.when(jnp.logical_not(stays))(est_copy.start)
    params_start()
    raw_copies, outer_copies = [], []
    low, high = pl.ds(0, SHIFT), pl.ds(CX - SHIFT, SHIFT)
    inner_rows, all_rows = pl.ds(SHIFT, CY - 2 * SHIFT), pl.ds(0, CY)
    to_low, to_high = pl.ds(0, SHIFT), pl.ds(SHIFT + CX, SHIFT)

    def send_raw(planes, rows, to_planes, to_rows, device):
        return go(view.at[0, planes, rows], wide.at[to_planes, to_rows], device)

    x_moves = ((low, to_high, raw(-1, 0)), (high, to_low, raw(1, 0)))
    for planes, to_planes, device in x_moves:
        for start in (0, CY - SHIFT):
            outer_copies.append(send_raw(
                planes, pl.ds(start, SHIFT), to_planes, pl.ds(SHIFT + start, SHIFT), device))
    for planes, to_planes, device in x_moves:
        raw_copies.append(send_raw(
            planes, inner_rows, to_planes, pl.ds(2 * SHIFT, CY - 2 * SHIFT), device))
    for rows, to_rows, device in ((low, to_high, raw(0, -1)), (high, to_low, raw(0, 1))):
        raw_copies.append(send_raw(all_rows, rows, pl.ds(SHIFT, CX), to_rows, device))

    def send_x(field):
        return [
            go(field.at[pl.ds(HALF, HALF)], field.at[pl.ds(HALF + PX, HALF)], x_left),
            go(field.at[pl.ds(PX, HALF)], field.at[pl.ds(0, HALF)], x_right),
        ]

    def wait_x(field, copies):
        for copy in copies:
            copy.wait_recv()

        @pl.when(first_x)
        def _():
            field[0:HALF] = jnp.zeros((HALF, PY, CZ), jnp.float32)

        @pl.when(last_x)
        def _():
            field[HALF + PX : WIDE_X] = jnp.zeros((HALF, PY, CZ), jnp.float32)

    def send_y(field):
        own = field.at[:, pl.ds(PY, PY)]
        return [
            go(own, field.at[:, pl.ds(2 * PY, PY)], y_left),
            go(own, field.at[:, pl.ds(0, PY)], y_right),
        ]

    pl.when(stays)(local_est.wait)
    pl.when(jnp.logical_not(stays))(est_copy.wait)

    def send_current(iteration):
        if iteration == 0:
            return [], send_x(raw_x.at[iteration])
        raw_y[iteration, :, PY : 2 * PY, :] = raw_x[iteration, HALF : HALF + PX]
        return send_y(raw_y.at[iteration]), send_x(raw_x.at[iteration])

    current_copies = send_current(0)

    for copy in outer_copies:
        copy.wait_recv()
    for planes in (to_low, to_high):
        for rows, to_rows, device in (
            (pl.ds(SHIFT, SHIFT), to_high, raw(0, -1)),
            (pl.ds(CY, SHIFT), to_low, raw(0, 1)),
        ):
            raw_copies.append(go(wide.at[planes, rows], wide.at[planes, to_rows], device))

    for s in range(VIEWS):
        params_wait(s)

    def build(v, carry):
        for t in range(TAPS):
            taps[v, t] = jnp.broadcast_to(params[v, 0:1, t : t + 1], (8, CZ))
        r = lax.broadcasted_iota(jnp.int32, (PY, 3 * WIDE_Y), 0)
        c = lax.broadcasted_iota(jnp.int32, (PY, 3 * WIDE_Y), 1)
        group, c = lax.div(c, WIDE_Y), lax.rem(c, WIDE_Y)
        distance = c - r - 1
        outside = (first_y & (c < PY)) | (last_y & (c >= 2 * PY))
        forward = jnp.zeros((PY, 3 * WIDE_Y), jnp.float32)
        backward = forward
        for t in range(TAPS):
            tap = params[v, 1:2, t : t + 1]
            forward = jnp.where(distance == t, tap, forward)
            backward = jnp.where(distance == TAPS - 1 - t, tap, backward)
        for k, band in enumerate((forward, backward)):
            upper, lower = split(jnp.where(outside, 0.0, band))
            band_y[k, v] = jnp.where(
                group < 2, upper.astype(jnp.float32), lower.astype(jnp.float32)).astype(jnp.bfloat16)
        r = lax.broadcasted_iota(jnp.int32, (CZ, CZ), 0)
        c = lax.broadcasted_iota(jnp.int32, (CZ, CZ), 1)
        distance = r - c + HALF
        forward = jnp.zeros((CZ, CZ), jnp.float32)
        backward = forward
        for t in range(TAPS):
            tap = params[v, 2:3, t : t + 1]
            forward = jnp.where(distance == t, tap, forward)
            backward = jnp.where(distance == TAPS - 1 - t, tap, backward)
        for k, band in enumerate((forward, backward)):
            upper, lower = split(band)
            for n in range(2):
                band_z[k, v, n * CZ : (n + 1) * CZ, 0:CZ] = upper
                band_z[k, v, n * CZ : (n + 1) * CZ, CZ : 2 * CZ] = lower
        return carry

    lax.fori_loop(0, VIEWS, build, 0)

    def conv_x(field, v, k, target, row):
        def tile(j, carry):
            weights = [taps[v, TAPS - 1 - t if k else t] for t in range(TAPS)]
            sums = [None] * PX
            for a in range(WIDE_X):
                value = field[a, pl.ds(pl.multiple_of(8 * j, 8), 8), :]
                for i in range(PX):
                    if 0 <= a - i < TAPS:
                        term = weights[a - i] * value
                        sums[i] = term if sums[i] is None else sums[i] + term
            for i in range(PX):
                target[i, pl.ds(pl.multiple_of(row + 8 * j, 8), 8), :] = sums[i]
            return carry

        lax.fori_loop(0, PY // 8, tile, 0)

    def conv_y(field, v, k, planes=(0, PX)):
        blocks = []
        for p in range(*planes, 2):
            both = jnp.concatenate([field[p], field[p + 1]], axis=1)
            upper, lower = split(both)
            stacked = jnp.concatenate([upper, lower, upper], axis=0)
            both = jnp.dot(band_y[k, v], stacked, preferred_element_type=jnp.float32)
            blocks += [both[:, :CZ], both[:, CZ:]]
        return jnp.concatenate(blocks, axis=0)

    def conv_z(value, v, k):
        both = jnp.concatenate(split(value), axis=1)
        both = jnp.dot(both, band_z[k, v], preferred_element_type=jnp.float32)
        return both[:, :CZ] + both[:, CZ:]

    def store_aligned():
        aligned[vw] = own_aligned[piece(part), piece(core), :]

    aligned_start, aligned_wait, aligned_finish = spread(
        lambda r: own_aligned.at[piece(r // 2), piece(r % 2)], lambda s: aligned.at[s], store_aligned)

    def align():
        local_view.wait()
        for copy in raw_copies:
            copy.wait_recv()
        ox, oy, oz = off[0, 0, 0, 0], off[0, 0, 0, 1], off[0, 0, 0, 2]
        gy = by * CY + oy + lax.broadcasted_iota(jnp.int32, (CY, CZ), 0)
        gz = oz + lax.broadcasted_iota(jnp.int32, (CY, CZ), 1)
        inside = (gy >= 0) & (gy < nx * CY) & (gz >= 0) & (gz < CZ)
        turn = lax.rem(CZ - oz, CZ)

        def planes(n, carry):
            for i in range(8):
                p = 8 * n + i
                value = wide[SHIFT + ox + p, pl.ds(SHIFT + oy, CY), :]
                value = pltpu.roll(value, turn, 1)
                gx = bx * CX + ox + p
                ok = inside & (gx >= 0) & (gx < 2 * nz * CX)
                own_aligned[p] = jnp.where(ok, value, -1.0)
            return carry

        for n in range(2):
            planes(2 * n, 0)
            planes(2 * n + 1, 0)
            pl.when(core == 0)(functools.partial(aligned_start, (2 * n, 2 * n + 1), n == 1))

    weights = params[0, 4:8, :]
    total = jnp.sum(weights, axis=0, keepdims=True)

    shared = PX // 2
    own_target = out.at[piece(part), piece(core)]
    chip_mate = dev(zc, by, y, other)
    base = new_sem(4)
    mate_copy = remote(result, own_target, new_sem(), chip_mate)
    results = []
    for n in range(2):
        y_ = side + 2 * n
        for c in range(2):
            copy = remote(
                result.at[pl.ds(c * shared, shared)],
                out.at[pl.ds(part * PX + c * shared, shared), piece(core)],
                base + 2 * n + c, dev(zc, by, y_, c), base + 2 * part + core)
            results.append((y_ != y, copy))


    def begin_x(iteration, k, v, source):
        field = x_wide.at[iteration, k, v]
        field[HALF : HALF + PX] = source.reshape(PX, PY, CZ)
        return send_x(field)

    def begin_y(iteration, k, v, source):
        field = y_wide.at[iteration, k, v]
        field[:, PY : 2 * PY, :] = source.reshape(PX, PY, CZ)
        return send_y(field)

    def end_x(iteration, k, v, copies):
        field = x_wide.at[iteration, k, v]
        wait_x(field, copies)
        conv_x(field, v, k, value.at[v], 0)
        return value[v].reshape(PX * PY, CZ)

    def end_y(iteration, k, v, copies):
        for copy in copies:
            copy.wait_recv()
        return conv_y(y_wide.at[iteration, k, v], v, k)

    for iteration in range(ITERS):
        if iteration == 0:
            x_first, x_first_back = (True,) * VIEWS, (True, True, False, False)
            order, order_back = (0, 2, 1, 3), (2, 0, 3, 1)
            align()
        else:
            x_first, x_first_back = (True, True, False, False), (False, False, True, True)
            order, order_back = (2, 0, 1, 3), (0, 2, 1, 3)
        copies = {}
        for copy in current_copies[0]:
            copy.wait_recv()
        for v in range(VIEWS):
            if not x_first[v]:
                copies[v] = begin_x(iteration, 0, v, conv_y(raw_y.at[iteration], v, 0))
        wait_x(raw_x.at[iteration], current_copies[1])
        for v in range(VIEWS):
            if x_first[v]:
                field = y_wide.at[iteration, 0, v]
                conv_x(raw_x.at[iteration], v, 0, field, PY)
                copies[v] = send_y(field)
        if iteration == 0:
            pl.when(core == 1)(aligned_start)
        for v in order:
            blurred = (end_y if x_first[v] else end_x)(iteration, 0, v, copies[v])
            blurred = conv_z(blurred, v, 0)
            if iteration == 0:
                aligned_wait(v)
            recorded = aligned[v].reshape(PX * PY, CZ)
            ratio = jnp.where(recorded >= 0.0, recorded / blurred, 1.0)
            back = conv_z(ratio, v, 1)
            copies[v] = (begin_x if x_first_back[v] else begin_y)(iteration, 1, v, back)
        for v in order_back:
            if x_first_back[v]:
                wait_x(x_wide.at[iteration, 1, v], copies[v])
                field = y_wide.at[iteration, 1, v]
                conv_x(x_wide.at[iteration, 1, v], v, 1, field, PY)
                copies[v] = send_y(field)
            else:
                copies[v] = begin_x(iteration, 1, v, end_y(iteration, 1, v, copies[v]))
        last = order_back[-1] if iteration + 1 == ITERS else None
        for n, v in enumerate(order_back):
            if v == last:
                break
            back = (end_y if x_first_back[v] else end_x)(iteration, 1, v, copies[v])
            term = params[0, 4 + v : 5 + v, :] * jnp.log(back)
            summed[...] = term if n == 0 else summed[...] + term
        if last is None:
            update = jnp.exp(summed[...] / total).reshape(PX, PY, CZ)
            raw_x[iteration + 1, HALF : HALF + PX] = raw_x[iteration, HALF : HALF + PX] * update
            current_copies = send_current(iteration + 1)
            continue
        for copy in copies[last]:
            copy.wait_recv()
        for c in range(2):
            planes = (c * shared, (c + 1) * shared)
            back = conv_y(y_wide.at[iteration, 1, last], last, 1, planes)
            term = params[0, 4 + last : 5 + last, :] * jnp.log(back)
            log_sum = summed[planes[0] * PY : planes[1] * PY, :] + term
            update = jnp.exp(log_sum / total).reshape(shared, PY, CZ)
            result[planes[0] : planes[1]] = (
                raw_x[iteration, HALF + planes[0] : HALF + planes[1]] * update)
            for away, copy in results[c::2]:
                pl.when(away)(copy.start)

    @pl.when(stays)
    def _():
        mate_copy.start()
        own_target[...] = result[...]

    params_finish()
    aligned_finish()
    for copy in sent:
        copy.wait_send()

    base_mate = new_sem(4)
    forwards = []
    for s in (2, 3, 0, 1):
        away = chip_at(zc, 2 * y_lo + s // 2) != y
        got, missing = [
            out.at[pl.ds(s // 2 * PX + c * shared, shared), piece(s % 2)] for c in (core, other)
        ]
        arrival = remote(got, got, base + s, x_left)
        forward = remote(got, got, base_mate + s, chip_mate)
        missed = remote(missing, missing, base_mate + s, chip_mate)

        @pl.when(away)
        def _(arrival=arrival, forward=forward):
            arrival.wait_recv()
            forward.start()

        forwards.append((away, forward, missed))

    @pl.when(stays)
    def _():
        mate_copy.wait()

    for away, forward, missed in forwards:

        @pl.when(away)
        def _(forward=forward, missed=missed):
            missed.wait_recv()
            forward.wait_send()

    for away, copy in results:
        pl.when(away)(copy.wait_send)


def solution(mesh):
    nz, nx = mesh.shape["bx"] // 2, mesh.shape["by"]
    f32, bf16 = jnp.float32, jnp.bfloat16

    def shards(estimate, views_raw, psf_taps, offsets, view_weights):
        vmem = pl.BlockSpec(memory_space=pltpu.VMEM)
        hbm = pl.BlockSpec(memory_space=pltpu.HBM)
        return pl.pallas_call(
            functools.partial(kernel, (nz, nx)),
            out_shape=jax.ShapeDtypeStruct((CX, CY, CZ), f32),
            in_specs=[hbm] * 5,
            out_specs=vmem,
            scratch_shapes=[
                pltpu.VMEM((ITERS, WIDE_X, PY, CZ), f32),
                pltpu.VMEM((ITERS, PX, WIDE_Y, CZ), f32),
                pltpu.VMEM((ITERS, 2, VIEWS, WIDE_X, PY, CZ), f32),
                pltpu.VMEM((ITERS, 2, VIEWS, PX, WIDE_Y, CZ), f32),
                pltpu.VMEM((VIEWS, PX, PY, CZ), f32),
                pltpu.VMEM((PX * PY, CZ), f32),
                pltpu.VMEM((PX, PY, CZ), f32),
                pltpu.VMEM((3, 1, TAPS), f32),
                pltpu.SMEM((1, 1, 1, 3), jnp.int32),
                pltpu.SMEM((1, 1, VIEWS), jnp.int32),
                pltpu.VMEM((CX + 2 * SHIFT, CY + 2 * SHIFT, CZ), f32),
                pltpu.VMEM((CX, CY, CZ), f32),
                pltpu.VMEM((VIEWS, PX, PY, CZ), f32),
                pltpu.VMEM((8, 128), f32),
                pltpu.VMEM((VIEWS, 8, 128), f32),
                pltpu.VMEM((VIEWS, TAPS, 8, CZ), f32),
                pltpu.VMEM((2, VIEWS, PY, 3 * WIDE_Y), bf16),
                pltpu.VMEM((2, VIEWS, 2 * CZ, 2 * CZ), bf16),
                pltpu.SemaphoreType.DMA((N_SEMS,)),
                pltpu.SemaphoreType.DMA((N_SEMS,)),
                pltpu.SemaphoreType.DMA((5,)),
            ],
            compiler_params=pltpu.CompilerParams(
                collective_id=0, has_side_effects=True, vmem_limit_bytes=53 * 1024 * 1024
            ),
            cost_estimate=pl.CostEstimate(flops=10**9, bytes_accessed=2 * 10**6, transcendentals=10**6),
        )(
            estimate,
            views_raw,
            jnp.transpose(psf_taps, (1, 0, 2)),
            offsets,
            jnp.transpose(view_weights, (1, 2, 0)),
        )

    return jax.shard_map(
        shards,
        mesh=mesh,
        in_specs=(
            P("bx", "by", None),
            P("view", "bx", "by", None),
            P("view", None, None),
            P("view", "bx", "by", None),
            P(None, "bx", "by"),
        ),
        out_specs=P("bx", "by", None),
        check_vma=False,
    )
```

```python
import functools

import jax
import jax.numpy as jnp
from jax import lax
from jax.experimental import pallas as pl
from jax.experimental.pallas import tpu as pltpu
from jax.sharding import PartitionSpec as P

ITERS = 2
TAPS = 31
HALF = 15
SHIFT = 8
VIEWS = 4
CX, CY, CZ = 32, 32, 128
PX, PY = 16, 16
WIDE_X = PX + 2 * HALF
WIDE_Y = 3 * PY
N_SEMS = 128
MESH = pl.DeviceIdType.MESH


def split(value):
    high = value.astype(jnp.bfloat16)
    low = (value - high.astype(jnp.float32)).astype(jnp.bfloat16)
    return high, low


def kernel(
    sizes,
    est, view, psf_hbm, off_hbm, wts_hbm,
    out,
    raw_x, raw_y, x_wide, y_wide, value, summed, result, psf, off, wts, wide, own_aligned, aligned, own_params, params,
    taps, band_y, band_z,
    send_sem, recv_sem, local_sem,
):
    nz, nx = sizes
    bx, by, vw = lax.axis_index("bx"), lax.axis_index("by"), lax.axis_index("view")
    zc, y_lo = lax.div(bx, 2), lax.rem(bx, 2)
    y_hi, core = lax.div(vw, 2), lax.rem(vw, 2)
    y = 2 * y_hi + y_lo
    other = 1 - core
    pos = jnp.where(lax.rem(zc, 2) == 0, y, 3 - y)
    side, part = lax.div(pos, 2), lax.rem(pos, 2)
    stays = side == y_lo

    def dev(zc_, x_, y_, core_):
        return (zc_ * 2 + lax.rem(y_, 2), x_, lax.div(y_, 2) * 2 + core_)

    def chip_at(zc_, pos_):
        return jnp.where(lax.rem(zc_, 2) == 0, pos_, 3 - pos_)

    def along_x(step):
        place = lax.rem(4 * zc + pos + 4 * nz + step, 4 * nz)
        zc_, pos_ = lax.div(place, 4), lax.rem(place, 4)
        return dev(zc_, by, chip_at(zc_, pos_), core)

    def along_y(step):
        place = lax.rem(2 * by + core + 2 * nx + step, 2 * nx)
        return dev(zc, lax.div(place, 2), y, lax.rem(place, 2))

    x_left, x_right = along_x(-1), along_x(1)
    y_left, y_right = along_y(-1), along_y(1)
    first_x, last_x = (zc == 0) & (pos == 0), (zc == nz - 1) & (pos == 3)
    first_y, last_y = (by == 0) & (core == 0), (by == nx - 1) & (core == 1)

    def raw(step_x, step_y):
        return (lax.rem(bx + 2 * nz + step_x, 2 * nz), lax.rem(by + nx + step_y, nx), vw)

    far_y = dev(zc, lax.rem(by + nx + jnp.where(core == 0, -1, 1), nx), y, other)
    raw_far = raw(jnp.where(y_lo == 0, -1, 1), 0)
    barrier = pltpu.get_barrier_semaphore()
    peers = [dev(zc, by, lax.rem(y + d, 4), core) for d in (1, 2, 3)]
    peers += [dev(zc, by, lax.rem(y + d, 4), other) for d in (0, 1, 2, 3)]
    peers += [dev(lax.rem(zc + nz + d, nz), by, y, core) for d in (-1, 1)]
    peers += [far_y, raw_far, raw(0, -1), raw(0, 1)]
    for peer in peers:
        pl.semaphore_signal(barrier, inc=1, device_id=peer, device_id_type=MESH)

    used = [0]
    sent = []

    def new_sem(count=1):
        first = used[0]
        used[0] += count
        return first

    def remote(src, dst, sem, device, at=None):
        return pltpu.make_async_remote_copy(
            src_ref=src, dst_ref=dst, send_sem=send_sem.at[sem],
            recv_sem=recv_sem.at[sem if at is None else at],
            device_id=device, device_id_type=MESH)

    def go(src, dst, device):
        copy = remote(src, dst, new_sem(), device)
        copy.start()
        sent.append(copy)
        return copy

    def piece(n):
        return pl.ds(n * PX, PX)

    def spread(source_at, target, own_store):
        base = new_sem(4)
        copies = []
        for r in range(4):
            y_, core_ = chip_at(zc, 2 * y_lo + r // 2), r % 2
            me = (y_ == y) & (core_ == core)
            copy = remote(source_at(r), target(vw), base + r, dev(zc, by, y_, core_), base + vw)
            copies.append((me, copy))

        def start(chosen=range(4), last=True):
            for r in chosen:
                me, copy = copies[r]
                pl.when(jnp.logical_not(me))(copy.start)

            if last:

                @pl.when(stays)
                def _():
                    own_store()

        def wait(s):
            @pl.when(jnp.logical_not(stays & (vw == s)))
            def _():
                remote(target(s), target(s), base + s, x_left).wait_recv()

        def finish():
            for me, copy in copies:
                pl.when(jnp.logical_not(me))(copy.wait_send)

        return start, wait, finish

    local_view = pltpu.make_async_copy(
        view.at[0], wide.at[pl.ds(SHIFT, CX), pl.ds(SHIFT, CY)], local_sem.at[0])
    local_view.start()
    small = [
        pltpu.make_async_copy(src, dst, local_sem.at[2 + n])
        for n, (src, dst) in enumerate(((psf_hbm, psf), (wts_hbm, wts), (off_hbm, off)))
    ]
    for copy in small:
        copy.start()
    own_block = raw_x.at[0, pl.ds(HALF, PX)]
    local_est = pltpu.make_async_copy(
        est.at[piece(part), piece(core)], own_block, local_sem.at[1])
    pl.when(stays)(local_est.start)
    pair = jnp.where(y_lo == 0, lax.rem(y + 3, 4), lax.rem(y + 1, 4))
    pair_part = lax.rem(jnp.where(lax.rem(zc, 2) == 0, pair, 3 - pair), 2)
    est_copy = remote(
        est.at[piece(pair_part), piece(core)], own_block, new_sem(), dev(zc, by, pair, core))

    own_params[...] = jnp.zeros((8, 128), jnp.float32)
    for copy in small:
        copy.wait()
    row = psf[:, 0, :]
    own_params[0:3, 0:TAPS] = row / jnp.sum(row, axis=-1, keepdims=True)
    for v in range(VIEWS):
        own_params[4 + v : 5 + v, :] = jnp.full((1, 128), wts[0, 0, v].astype(jnp.float32))

    def store_params():
        params[vw] = own_params[...]

    params_start, params_wait, params_finish = spread(
        lambda r: own_params, lambda s: params.at[s], store_params)

    pl.semaphore_wait(barrier, len(peers))
    pl.when(jnp.logical_not(stays))(est_copy.start)
    params_start()
    raw_copies, outer_copies = [], []
    low, high = pl.ds(0, SHIFT), pl.ds(CX - SHIFT, SHIFT)
    inner_rows, all_rows = pl.ds(SHIFT, CY - 2 * SHIFT), pl.ds(0, CY)
    to_low, to_high = pl.ds(0, SHIFT), pl.ds(SHIFT + CX, SHIFT)

    def send_raw(planes, rows, to_planes, to_rows, device):
        return go(view.at[0, planes, rows], wide.at[to_planes, to_rows], device)

    x_moves = ((low, to_high, raw(-1, 0)), (high, to_low, raw(1, 0)))
    for planes, to_planes, device in x_moves:
        for start in (0, CY - SHIFT):
            outer_copies.append(send_raw(
                planes, pl.ds(start, SHIFT), to_planes, pl.ds(SHIFT + start, SHIFT), device))
    for planes, to_planes, device in x_moves:
        raw_copies.append(send_raw(
            planes, inner_rows, to_planes, pl.ds(2 * SHIFT, CY - 2 * SHIFT), device))
    for rows, to_rows, device in ((low, to_high, raw(0, -1)), (high, to_low, raw(0, 1))):
        raw_copies.append(send_raw(all_rows, rows, pl.ds(SHIFT, CX), to_rows, device))

    def send_x(field):
        return [
            go(field.at[pl.ds(HALF, HALF)], field.at[pl.ds(HALF + PX, HALF)], x_left),
            go(field.at[pl.ds(PX, HALF)], field.at[pl.ds(0, HALF)], x_right),
        ]

    def wait_x(field, copies):
        for copy in copies:
            copy.wait_recv()

        @pl.when(first_x)
        def _():
            field[0:HALF] = jnp.zeros((HALF, PY, CZ), jnp.float32)

        @pl.when(last_x)
        def _():
            field[HALF + PX : WIDE_X] = jnp.zeros((HALF, PY, CZ), jnp.float32)

    def send_y(field, start=0, count=PX):
        planes = pl.ds(start, count)
        own = field.at[planes, pl.ds(PY, PY)]
        return [
            go(own, field.at[planes, pl.ds(2 * PY, PY)], y_left),
            go(own, field.at[planes, pl.ds(0, PY)], y_right),
        ]

    pl.when(stays)(local_est.wait)
    pl.when(jnp.logical_not(stays))(est_copy.wait)

    current_copies = [], send_x(raw_x.at[0])

    for copy in outer_copies:
        copy.wait_recv()
    for planes in (to_low, to_high):
        for rows, to_rows, device in (
            (pl.ds(SHIFT, SHIFT), to_high, raw(0, -1)),
            (pl.ds(CY, SHIFT), to_low, raw(0, 1)),
        ):
            raw_copies.append(go(wide.at[planes, rows], wide.at[planes, to_rows], device))

    for s in range(VIEWS):
        params_wait(s)

    def build(v, carry):
        for t in range(TAPS):
            taps[v, t] = jnp.broadcast_to(params[v, 0:1, t : t + 1], (8, CZ))
        r = lax.broadcasted_iota(jnp.int32, (PY, 3 * WIDE_Y), 0)
        c = lax.broadcasted_iota(jnp.int32, (PY, 3 * WIDE_Y), 1)
        group, c = lax.div(c, WIDE_Y), lax.rem(c, WIDE_Y)
        distance = c - r - 1
        outside = (first_y & (c < PY)) | (last_y & (c >= 2 * PY))
        forward = jnp.zeros((PY, 3 * WIDE_Y), jnp.float32)
        backward = forward
        for t in range(TAPS):
            tap = params[v, 1:2, t : t + 1]
            forward = jnp.where(distance == t, tap, forward)
            backward = jnp.where(distance == TAPS - 1 - t, tap, backward)
        for k, band in enumerate((forward, backward)):
            upper, lower = split(jnp.where(outside, 0.0, band))
            band_y[k, v] = jnp.where(
                group < 2, upper.astype(jnp.float32), lower.astype(jnp.float32)).astype(jnp.bfloat16)
        r = lax.broadcasted_iota(jnp.int32, (CZ, CZ), 0)
        c = lax.broadcasted_iota(jnp.int32, (CZ, CZ), 1)
        distance = r - c + HALF
        forward = jnp.zeros((CZ, CZ), jnp.float32)
        backward = forward
        for t in range(TAPS):
            tap = params[v, 2:3, t : t + 1]
            forward = jnp.where(distance == t, tap, forward)
            backward = jnp.where(distance == TAPS - 1 - t, tap, backward)
        for k, band in enumerate((forward, backward)):
            upper, lower = split(band)
            for n in range(2):
                band_z[k, v, n * CZ : (n + 1) * CZ, 0:CZ] = upper
                band_z[k, v, n * CZ : (n + 1) * CZ, CZ : 2 * CZ] = lower
        return carry

    lax.fori_loop(0, VIEWS, build, 0)

    def conv_x(field, v, k, target, row):
        def tile(j, carry):
            weights = [taps[v, TAPS - 1 - t if k else t] for t in range(TAPS)]
            sums = [None] * PX
            for a in range(WIDE_X):
                value = field[a, pl.ds(pl.multiple_of(8 * j, 8), 8), :]
                for i in range(PX):
                    if 0 <= a - i < TAPS:
                        term = weights[a - i] * value
                        sums[i] = term if sums[i] is None else sums[i] + term
            for i in range(PX):
                target[i, pl.ds(pl.multiple_of(row + 8 * j, 8), 8), :] = sums[i]
            return carry

        lax.fori_loop(0, PY // 8, tile, 0)

    def conv_y(field, v, k, planes=(0, PX)):
        blocks = []
        for p in range(*planes, 2):
            both = jnp.concatenate([field[p], field[p + 1]], axis=1)
            upper, lower = split(both)
            stacked = jnp.concatenate([upper, lower, upper], axis=0)
            both = jnp.dot(band_y[k, v], stacked, preferred_element_type=jnp.float32)
            blocks += [both[:, :CZ], both[:, CZ:]]
        return jnp.concatenate(blocks, axis=0)

    def conv_z(value, v, k):
        both = jnp.concatenate(split(value), axis=1)
        both = jnp.dot(both, band_z[k, v], preferred_element_type=jnp.float32)
        return both[:, :CZ] + both[:, CZ:]

    def store_aligned():
        aligned[vw] = own_aligned[piece(part), piece(core), :]

    aligned_start, aligned_wait, aligned_finish = spread(
        lambda r: own_aligned.at[piece(r // 2), piece(r % 2)], lambda s: aligned.at[s], store_aligned)

    def align():
        local_view.wait()
        for copy in raw_copies:
            copy.wait_recv()
        ox, oy, oz = off[0, 0, 0, 0], off[0, 0, 0, 1], off[0, 0, 0, 2]
        gy = by * CY + oy + lax.broadcasted_iota(jnp.int32, (CY, CZ), 0)
        gz = oz + lax.broadcasted_iota(jnp.int32, (CY, CZ), 1)
        inside = (gy >= 0) & (gy < nx * CY) & (gz >= 0) & (gz < CZ)
        turn = lax.rem(CZ - oz, CZ)

        def planes(n, carry):
            for i in range(8):
                p = 8 * n + i
                value = wide[SHIFT + ox + p, pl.ds(SHIFT + oy, CY), :]
                value = pltpu.roll(value, turn, 1)
                gx = bx * CX + ox + p
                ok = inside & (gx >= 0) & (gx < 2 * nz * CX)
                own_aligned[p] = jnp.where(ok, value, -1.0)
            return carry

        for n in range(2):
            planes(2 * n, 0)
            planes(2 * n + 1, 0)
            pl.when(core == 0)(functools.partial(aligned_start, (2 * n, 2 * n + 1), n == 1))

    weights = params[0, 4:8, :]
    total = jnp.sum(weights, axis=0, keepdims=True)

    shared = PX // 2
    own_target = out.at[piece(part), piece(core)]
    chip_mate = dev(zc, by, y, other)
    base = new_sem(4)
    mate_copy = remote(result, own_target, new_sem(), chip_mate)
    results = []
    for n in range(2):
        y_ = side + 2 * n
        for c in range(2):
            copy = remote(
                result.at[pl.ds(c * shared, shared)],
                out.at[pl.ds(part * PX + c * shared, shared), piece(core)],
                base + 2 * n + c, dev(zc, by, y_, c), base + 2 * part + core)
            results.append((y_ != y, copy))


    def begin_x(iteration, k, v, source):
        field = x_wide.at[iteration, k, v]
        field[HALF : HALF + PX] = source.reshape(PX, PY, CZ)
        return send_x(field)

    def begin_y(iteration, k, v, source):
        field = y_wide.at[iteration, k, v]
        field[:, PY : 2 * PY, :] = source.reshape(PX, PY, CZ)
        return send_y(field)

    def end_x(iteration, k, v, copies):
        field = x_wide.at[iteration, k, v]
        wait_x(field, copies)
        conv_x(field, v, k, value.at[v], 0)
        return value[v].reshape(PX * PY, CZ)

    def end_y(iteration, k, v, copies):
        for copy in copies:
            copy.wait_recv()
        return conv_y(y_wide.at[iteration, k, v], v, k)

    for iteration in range(ITERS):
        if iteration == 0:
            x_first, x_first_back = (True,) * VIEWS, (True, True, False, False)
            order, order_back = (0, 2, 1, 3), (2, 0, 3, 1)
            align()
        else:
            x_first, x_first_back = (True, True, False, False), (False, False, True, True)
            order, order_back = (2, 0, 1, 3), (0, 2, 1, 3)
        copies = {}
        for copy in current_copies[0]:
            copy.wait_recv()
        for v in range(VIEWS):
            if not x_first[v]:
                copies[v] = begin_x(iteration, 0, v, conv_y(raw_y.at[iteration], v, 0))
        wait_x(raw_x.at[iteration], current_copies[1])
        for v in range(VIEWS):
            if x_first[v]:
                field = y_wide.at[iteration, 0, v]
                conv_x(raw_x.at[iteration], v, 0, field, PY)
                copies[v] = send_y(field)
        if iteration == 0:
            pl.when(core == 1)(aligned_start)
        for v in order:
            blurred = (end_y if x_first[v] else end_x)(iteration, 0, v, copies[v])
            blurred = conv_z(blurred, v, 0)
            if iteration == 0:
                aligned_wait(v)
            recorded = aligned[v].reshape(PX * PY, CZ)
            ratio = jnp.where(recorded >= 0.0, recorded / blurred, 1.0)
            back = conv_z(ratio, v, 1)
            copies[v] = (begin_x if x_first_back[v] else begin_y)(iteration, 1, v, back)
        for v in order_back:
            if x_first_back[v]:
                wait_x(x_wide.at[iteration, 1, v], copies[v])
                field = y_wide.at[iteration, 1, v]
                conv_x(x_wide.at[iteration, 1, v], v, 1, field, PY)
                copies[v] = send_y(field)
            else:
                copies[v] = begin_x(iteration, 1, v, end_y(iteration, 1, v, copies[v]))
        last = order_back[-1]
        for n, v in enumerate(order_back):
            if v == last:
                break
            back = (end_y if x_first_back[v] else end_x)(iteration, 1, v, copies[v])
            term = params[0, 4 + v : 5 + v, :] * jnp.log(back)
            summed[...] = term if n == 0 else summed[...] + term
        for copy in copies[last]:
            copy.wait_recv()
        raw_y_sent = []
        for c in range(2):
            planes = (c * shared, (c + 1) * shared)
            back = conv_y(y_wide.at[iteration, 1, last], last, 1, planes)
            term = params[0, 4 + last : 5 + last, :] * jnp.log(back)
            log_sum = summed[planes[0] * PY : planes[1] * PY, :] + term
            update = jnp.exp(log_sum / total).reshape(shared, PY, CZ)
            updated = raw_x[iteration, HALF + planes[0] : HALF + planes[1]] * update
            if iteration + 1 < ITERS:
                raw_y[iteration + 1, planes[0] : planes[1], PY : 2 * PY] = updated
                raw_y_sent += send_y(raw_y.at[iteration + 1], planes[0], shared)
                raw_x[iteration + 1, HALF + planes[0] : HALF + planes[1]] = updated
            else:
                result[planes[0] : planes[1]] = updated
                for away, copy in results[c::2]:
                    pl.when(away)(copy.start)
        if iteration + 1 < ITERS:
            current_copies = raw_y_sent, send_x(raw_x.at[iteration + 1])

    @pl.when(stays)
    def _():
        mate_copy.start()
        own_target[...] = result[...]

    params_finish()
    aligned_finish()
    for copy in sent:
        copy.wait_send()

    base_mate = new_sem(4)
    forwards = []
    for s in (2, 3, 0, 1):
        away = chip_at(zc, 2 * y_lo + s // 2) != y
        got, missing = [
            out.at[pl.ds(s // 2 * PX + c * shared, shared), piece(s % 2)] for c in (core, other)
        ]
        arrival = remote(got, got, base + s, x_left)
        forward = remote(got, got, base_mate + s, chip_mate)
        missed = remote(missing, missing, base_mate + s, chip_mate)

        @pl.when(away)
        def _(arrival=arrival, forward=forward):
            arrival.wait_recv()
            forward.start()

        forwards.append((away, forward, missed))

    @pl.when(stays)
    def _():
        mate_copy.wait()

    for away, forward, missed in forwards:

        @pl.when(away)
        def _(forward=forward, missed=missed):
            missed.wait_recv()
            forward.wait_send()

    for away, copy in results:
        pl.when(away)(copy.wait_send)


def solution(mesh):
    nz, nx = mesh.shape["bx"] // 2, mesh.shape["by"]
    f32, bf16 = jnp.float32, jnp.bfloat16

    def shards(estimate, views_raw, psf_taps, offsets, view_weights):
        vmem = pl.BlockSpec(memory_space=pltpu.VMEM)
        hbm = pl.BlockSpec(memory_space=pltpu.HBM)
        return pl.pallas_call(
            functools.partial(kernel, (nz, nx)),
            out_shape=jax.ShapeDtypeStruct((CX, CY, CZ), f32),
            in_specs=[hbm] * 5,
            out_specs=vmem,
            scratch_shapes=[
                pltpu.VMEM((ITERS, WIDE_X, PY, CZ), f32),
                pltpu.VMEM((ITERS, PX, WIDE_Y, CZ), f32),
                pltpu.VMEM((ITERS, 2, VIEWS, WIDE_X, PY, CZ), f32),
                pltpu.VMEM((ITERS, 2, VIEWS, PX, WIDE_Y, CZ), f32),
                pltpu.VMEM((VIEWS, PX, PY, CZ), f32),
                pltpu.VMEM((PX * PY, CZ), f32),
                pltpu.VMEM((PX, PY, CZ), f32),
                pltpu.VMEM((3, 1, TAPS), f32),
                pltpu.SMEM((1, 1, 1, 3), jnp.int32),
                pltpu.SMEM((1, 1, VIEWS), jnp.int32),
                pltpu.VMEM((CX + 2 * SHIFT, CY + 2 * SHIFT, CZ), f32),
                pltpu.VMEM((CX, CY, CZ), f32),
                pltpu.VMEM((VIEWS, PX, PY, CZ), f32),
                pltpu.VMEM((8, 128), f32),
                pltpu.VMEM((VIEWS, 8, 128), f32),
                pltpu.VMEM((VIEWS, TAPS, 8, CZ), f32),
                pltpu.VMEM((2, VIEWS, PY, 3 * WIDE_Y), bf16),
                pltpu.VMEM((2, VIEWS, 2 * CZ, 2 * CZ), bf16),
                pltpu.SemaphoreType.DMA((N_SEMS,)),
                pltpu.SemaphoreType.DMA((N_SEMS,)),
                pltpu.SemaphoreType.DMA((5,)),
            ],
            compiler_params=pltpu.CompilerParams(
                collective_id=0, has_side_effects=True, vmem_limit_bytes=53 * 1024 * 1024
            ),
            cost_estimate=pl.CostEstimate(flops=10**9, bytes_accessed=2 * 10**6, transcendentals=10**6),
        )(
            estimate,
            views_raw,
            jnp.transpose(psf_taps, (1, 0, 2)),
            offsets,
            jnp.transpose(view_weights, (1, 2, 0)),
        )

    return jax.shard_map(
        shards,
        mesh=mesh,
        in_specs=(
            P("bx", "by", None),
            P("view", "bx", "by", None),
            P("view", None, None),
            P("view", "bx", "by", None),
            P(None, "bx", "by"),
        ),
        out_specs=P("bx", "by", None),
        check_vma=False,
    )
```

```python
import functools

import jax
import jax.numpy as jnp
from jax import lax
from jax.experimental import pallas as pl
from jax.experimental.pallas import tpu as pltpu
from jax.sharding import PartitionSpec as P

ITERS = 2
TAPS = 31
HALF = 15
SHIFT = 8
VIEWS = 4
CX, CY, CZ = 32, 32, 128
PX, PY = 16, 16
WIDE_X = PX + 2 * HALF
WIDE_Y = 3 * PY
N_SEMS = 128
MESH = pl.DeviceIdType.MESH


def split(value):
    high = value.astype(jnp.bfloat16)
    low = (value - high.astype(jnp.float32)).astype(jnp.bfloat16)
    return high, low


def kernel(
    sizes,
    est, view, psf_hbm, off_hbm, wts_hbm,
    out,
    raw_x, raw_y, x_wide, y_wide, value, summed, result, psf, off, wts, wide, own_aligned, aligned, own_params, params,
    taps, band_y, band_z,
    send_sem, recv_sem, local_sem,
):
    nz, nx = sizes
    bx, by, vw = lax.axis_index("bx"), lax.axis_index("by"), lax.axis_index("view")
    zc, y_lo = lax.div(bx, 2), lax.rem(bx, 2)
    y_hi, core = lax.div(vw, 2), lax.rem(vw, 2)
    y = 2 * y_hi + y_lo
    other = 1 - core
    pos = jnp.where(lax.rem(zc, 2) == 0, y, 3 - y)
    side, part = lax.div(pos, 2), lax.rem(pos, 2)
    stays = side == y_lo

    def dev(zc_, x_, y_, core_):
        return (zc_ * 2 + lax.rem(y_, 2), x_, lax.div(y_, 2) * 2 + core_)

    def chip_at(zc_, pos_):
        return jnp.where(lax.rem(zc_, 2) == 0, pos_, 3 - pos_)

    def along_x(step):
        place = lax.rem(4 * zc + pos + 4 * nz + step, 4 * nz)
        zc_, pos_ = lax.div(place, 4), lax.rem(place, 4)
        return dev(zc_, by, chip_at(zc_, pos_), core)

    def along_y(step):
        place = lax.rem(2 * by + core + 2 * nx + step, 2 * nx)
        return dev(zc, lax.div(place, 2), y, lax.rem(place, 2))

    x_left, x_right = along_x(-1), along_x(1)
    y_left, y_right = along_y(-1), along_y(1)
    first_x, last_x = (zc == 0) & (pos == 0), (zc == nz - 1) & (pos == 3)
    first_y, last_y = (by == 0) & (core == 0), (by == nx - 1) & (core == 1)

    def raw(step_x, step_y):
        return (lax.rem(bx + 2 * nz + step_x, 2 * nz), lax.rem(by + nx + step_y, nx), vw)

    far_y = dev(zc, lax.rem(by + nx + jnp.where(core == 0, -1, 1), nx), y, other)
    raw_far = raw(jnp.where(y_lo == 0, -1, 1), 0)
    barrier = pltpu.get_barrier_semaphore()
    peers = [dev(zc, by, lax.rem(y + d, 4), core) for d in (1, 2, 3)]
    peers += [dev(zc, by, lax.rem(y + d, 4), other) for d in (0, 1, 2, 3)]
    peers += [dev(lax.rem(zc + nz + d, nz), by, y, core) for d in (-1, 1)]
    peers += [far_y, raw_far, raw(0, -1), raw(0, 1)]
    for peer in peers:
        pl.semaphore_signal(barrier, inc=1, device_id=peer, device_id_type=MESH)

    used = [0]
    sent = []

    def new_sem(count=1):
        first = used[0]
        used[0] += count
        return first

    def remote(src, dst, sem, device, at=None):
        return pltpu.make_async_remote_copy(
            src_ref=src, dst_ref=dst, send_sem=send_sem.at[sem],
            recv_sem=recv_sem.at[sem if at is None else at],
            device_id=device, device_id_type=MESH)

    def go(src, dst, device):
        copy = remote(src, dst, new_sem(), device)
        copy.start()
        sent.append(copy)
        return copy

    def piece(n):
        return pl.ds(n * PX, PX)

    def spread(source_at, target, own_store):
        base = new_sem(4)
        copies = []
        for r in range(4):
            y_, core_ = chip_at(zc, 2 * y_lo + r // 2), r % 2
            me = (y_ == y) & (core_ == core)
            copy = remote(source_at(r), target(vw), base + r, dev(zc, by, y_, core_), base + vw)
            copies.append((me, copy))

        def start(chosen=range(4), last=True):
            for r in chosen:
                me, copy = copies[r]
                pl.when(jnp.logical_not(me))(copy.start)

            if last:

                @pl.when(stays)
                def _():
                    own_store()

        def wait(s):
            @pl.when(jnp.logical_not(stays & (vw == s)))
            def _():
                remote(target(s), target(s), base + s, x_left).wait_recv()

        def finish():
            for me, copy in copies:
                pl.when(jnp.logical_not(me))(copy.wait_send)

        return start, wait, finish

    local_view = pltpu.make_async_copy(
        view.at[0], wide.at[pl.ds(SHIFT, CX), pl.ds(SHIFT, CY)], local_sem.at[0])
    local_view.start()
    small = [
        pltpu.make_async_copy(src, dst, local_sem.at[2 + n])
        for n, (src, dst) in enumerate(((psf_hbm, psf), (wts_hbm, wts), (off_hbm, off)))
    ]
    for copy in small:
        copy.start()
    own_block = raw_x.at[0, pl.ds(HALF, PX)]
    local_est = pltpu.make_async_copy(
        est.at[piece(part), piece(core)], own_block, local_sem.at[1])
    pl.when(stays)(local_est.start)
    pair = jnp.where(y_lo == 0, lax.rem(y + 3, 4), lax.rem(y + 1, 4))
    pair_part = lax.rem(jnp.where(lax.rem(zc, 2) == 0, pair, 3 - pair), 2)
    est_copy = remote(
        est.at[piece(pair_part), piece(core)], own_block, new_sem(), dev(zc, by, pair, core))

    own_params[...] = jnp.zeros((8, 128), jnp.float32)
    for copy in small:
        copy.wait()
    row = psf[:, 0, :]
    own_params[0:3, 0:TAPS] = row / jnp.sum(row, axis=-1, keepdims=True)
    for v in range(VIEWS):
        own_params[4 + v : 5 + v, :] = jnp.full((1, 128), wts[0, 0, v].astype(jnp.float32))

    def store_params():
        params[vw] = own_params[...]

    params_start, params_wait, params_finish = spread(
        lambda r: own_params, lambda s: params.at[s], store_params)

    pl.semaphore_wait(barrier, len(peers))
    pl.when(jnp.logical_not(stays))(est_copy.start)
    params_start()
    raw_copies, outer_copies = [], []
    low, high = pl.ds(0, SHIFT), pl.ds(CX - SHIFT, SHIFT)
    inner_rows, all_rows = pl.ds(SHIFT, CY - 2 * SHIFT), pl.ds(0, CY)
    to_low, to_high = pl.ds(0, SHIFT), pl.ds(SHIFT + CX, SHIFT)

    def send_raw(planes, rows, to_planes, to_rows, device):
        return go(view.at[0, planes, rows], wide.at[to_planes, to_rows], device)

    x_moves = ((low, to_high, raw(-1, 0)), (high, to_low, raw(1, 0)))
    for planes, to_planes, device in x_moves:
        for start in (0, CY - SHIFT):
            outer_copies.append(send_raw(
                planes, pl.ds(start, SHIFT), to_planes, pl.ds(SHIFT + start, SHIFT), device))
    for planes, to_planes, device in x_moves:
        raw_copies.append(send_raw(
            planes, inner_rows, to_planes, pl.ds(2 * SHIFT, CY - 2 * SHIFT), device))
    for rows, to_rows, device in ((low, to_high, raw(0, -1)), (high, to_low, raw(0, 1))):
        raw_copies.append(send_raw(all_rows, rows, pl.ds(SHIFT, CX), to_rows, device))

    not_first, not_last = jnp.logical_not(first_x), jnp.logical_not(last_x)
    x_sent = []

    def send_x(field):
        left = remote(
            field.at[pl.ds(HALF, HALF)], field.at[pl.ds(HALF + PX, HALF)], new_sem(), x_left)
        right = remote(field.at[pl.ds(PX, HALF)], field.at[pl.ds(0, HALF)], new_sem(), x_right)
        pl.when(not_first)(left.start)
        pl.when(not_last)(right.start)
        x_sent.append((left, right))
        return left, right

    def wait_x(field, copies):
        pl.when(not_last)(copies[0].wait_recv)
        pl.when(not_first)(copies[1].wait_recv)

        @pl.when(first_x)
        def _():
            field[0:HALF] = jnp.zeros((HALF, PY, CZ), jnp.float32)

        @pl.when(last_x)
        def _():
            field[HALF + PX : WIDE_X] = jnp.zeros((HALF, PY, CZ), jnp.float32)

    def send_y(field):
        own = field.at[:, pl.ds(PY, PY)]
        return [
            go(own, field.at[:, pl.ds(2 * PY, PY)], y_left),
            go(own, field.at[:, pl.ds(0, PY)], y_right),
        ]

    pl.when(stays)(local_est.wait)
    pl.when(jnp.logical_not(stays))(est_copy.wait)

    def send_current(iteration):
        if iteration == 0:
            return [], send_x(raw_x.at[iteration])
        raw_y[iteration, :, PY : 2 * PY, :] = raw_x[iteration, HALF : HALF + PX]
        return send_y(raw_y.at[iteration]), send_x(raw_x.at[iteration])

    current_copies = send_current(0)

    for copy in outer_copies:
        copy.wait_recv()
    for planes in (to_low, to_high):
        for rows, to_rows, device in (
            (pl.ds(SHIFT, SHIFT), to_high, raw(0, -1)),
            (pl.ds(CY, SHIFT), to_low, raw(0, 1)),
        ):
            raw_copies.append(go(wide.at[planes, rows], wide.at[planes, to_rows], device))

    for s in range(VIEWS):
        params_wait(s)

    def build(v, carry):
        for t in range(TAPS):
            taps[v, t] = jnp.broadcast_to(params[v, 0:1, t : t + 1], (8, CZ))
        r = lax.broadcasted_iota(jnp.int32, (PY, 3 * WIDE_Y), 0)
        c = lax.broadcasted_iota(jnp.int32, (PY, 3 * WIDE_Y), 1)
        group, c = lax.div(c, WIDE_Y), lax.rem(c, WIDE_Y)
        distance = c - r - 1
        outside = (first_y & (c < PY)) | (last_y & (c >= 2 * PY))
        forward = jnp.zeros((PY, 3 * WIDE_Y), jnp.float32)
        backward = forward
        for t in range(TAPS):
            tap = params[v, 1:2, t : t + 1]
            forward = jnp.where(distance == t, tap, forward)
            backward = jnp.where(distance == TAPS - 1 - t, tap, backward)
        for k, band in enumerate((forward, backward)):
            upper, lower = split(jnp.where(outside, 0.0, band))
            band_y[k, v] = jnp.where(
                group < 2, upper.astype(jnp.float32), lower.astype(jnp.float32)).astype(jnp.bfloat16)
        r = lax.broadcasted_iota(jnp.int32, (CZ, CZ), 0)
        c = lax.broadcasted_iota(jnp.int32, (CZ, CZ), 1)
        distance = r - c + HALF
        forward = jnp.zeros((CZ, CZ), jnp.float32)
        backward = forward
        for t in range(TAPS):
            tap = params[v, 2:3, t : t + 1]
            forward = jnp.where(distance == t, tap, forward)
            backward = jnp.where(distance == TAPS - 1 - t, tap, backward)
        for k, band in enumerate((forward, backward)):
            upper, lower = split(band)
            for n in range(2):
                band_z[k, v, n * CZ : (n + 1) * CZ, 0:CZ] = upper
                band_z[k, v, n * CZ : (n + 1) * CZ, CZ : 2 * CZ] = lower
        return carry

    lax.fori_loop(0, VIEWS, build, 0)

    def conv_x(field, v, k, target, row):
        def tile(j, carry):
            weights = [taps[v, TAPS - 1 - t if k else t] for t in range(TAPS)]
            sums = [None] * PX
            for a in range(WIDE_X):
                value = field[a, pl.ds(pl.multiple_of(8 * j, 8), 8), :]
                for i in range(PX):
                    if 0 <= a - i < TAPS:
                        term = weights[a - i] * value
                        sums[i] = term if sums[i] is None else sums[i] + term
            for i in range(PX):
                target[i, pl.ds(pl.multiple_of(row + 8 * j, 8), 8), :] = sums[i]
            return carry

        lax.fori_loop(0, PY // 8, tile, 0)

    def conv_y(field, v, k, planes=(0, PX)):
        blocks = []
        for p in range(*planes, 2):
            both = jnp.concatenate([field[p], field[p + 1]], axis=1)
            upper, lower = split(both)
            stacked = jnp.concatenate([upper, lower, upper], axis=0)
            both = jnp.dot(band_y[k, v], stacked, preferred_element_type=jnp.float32)
            blocks += [both[:, :CZ], both[:, CZ:]]
        return jnp.concatenate(blocks, axis=0)

    def conv_z(value, v, k):
        both = jnp.concatenate(split(value), axis=1)
        both = jnp.dot(both, band_z[k, v], preferred_element_type=jnp.float32)
        return both[:, :CZ] + both[:, CZ:]

    def store_aligned():
        aligned[vw] = own_aligned[piece(part), piece(core), :]

    aligned_start, aligned_wait, aligned_finish = spread(
        lambda r: own_aligned.at[piece(r // 2), piece(r % 2)], lambda s: aligned.at[s], store_aligned)

    def align():
        local_view.wait()
        for copy in raw_copies:
            copy.wait_recv()
        ox, oy, oz = off[0, 0, 0, 0], off[0, 0, 0, 1], off[0, 0, 0, 2]
        gy = by * CY + oy + lax.broadcasted_iota(jnp.int32, (CY, CZ), 0)
        gz = oz + lax.broadcasted_iota(jnp.int32, (CY, CZ), 1)
        inside = (gy >= 0) & (gy < nx * CY) & (gz >= 0) & (gz < CZ)
        turn = lax.rem(CZ - oz, CZ)

        def planes(n, carry):
            for i in range(8):
                p = 8 * n + i
                value = wide[SHIFT + ox + p, pl.ds(SHIFT + oy, CY), :]
                value = pltpu.roll(value, turn, 1)
                gx = bx * CX + ox + p
                ok = inside & (gx >= 0) & (gx < 2 * nz * CX)
                own_aligned[p] = jnp.where(ok, value, -1.0)
            return carry

        for n in range(2):
            planes(2 * n, 0)
            planes(2 * n + 1, 0)
            pl.when(core == 0)(functools.partial(aligned_start, (2 * n, 2 * n + 1), n == 1))

    weights = params[0, 4:8, :]
    total = jnp.sum(weights, axis=0, keepdims=True)

    shared = PX // 2
    own_target = out.at[piece(part), piece(core)]
    chip_mate = dev(zc, by, y, other)
    base = new_sem(4)
    mate_copy = remote(result, own_target, new_sem(), chip_mate)
    results = []
    for n in range(2):
        y_ = side + 2 * n
        for c in range(2):
            copy = remote(
                result.at[pl.ds(c * shared, shared)],
                out.at[pl.ds(part * PX + c * shared, shared), piece(core)],
                base + 2 * n + c, dev(zc, by, y_, c), base + 2 * part + core)
            results.append((y_ != y, copy))


    def begin_x(iteration, k, v, source):
        field = x_wide.at[iteration, k, v]
        field[HALF : HALF + PX] = source.reshape(PX, PY, CZ)
        return send_x(field)

    def begin_y(iteration, k, v, source):
        field = y_wide.at[iteration, k, v]
        field[:, PY : 2 * PY, :] = source.reshape(PX, PY, CZ)
        return send_y(field)

    def end_x(iteration, k, v, copies):
        field = x_wide.at[iteration, k, v]
        wait_x(field, copies)
        conv_x(field, v, k, value.at[v], 0)
        return value[v].reshape(PX * PY, CZ)

    def end_y(iteration, k, v, copies):
        for copy in copies:
            copy.wait_recv()
        return conv_y(y_wide.at[iteration, k, v], v, k)

    for iteration in range(ITERS):
        if iteration == 0:
            x_first, x_first_back = (True,) * VIEWS, (True, True, False, False)
            order, order_back = (0, 2, 1, 3), (2, 0, 3, 1)
            align()
        else:
            x_first, x_first_back = (True, True, False, False), (False, False, True, True)
            order, order_back = (2, 0, 1, 3), (0, 2, 1, 3)
        copies = {}
        for copy in current_copies[0]:
            copy.wait_recv()
        for v in range(VIEWS):
            if not x_first[v]:
                copies[v] = begin_x(iteration, 0, v, conv_y(raw_y.at[iteration], v, 0))
        wait_x(raw_x.at[iteration], current_copies[1])
        for v in range(VIEWS):
            if x_first[v]:
                field = y_wide.at[iteration, 0, v]
                conv_x(raw_x.at[iteration], v, 0, field, PY)
                copies[v] = send_y(field)
        if iteration == 0:
            pl.when(core == 1)(aligned_start)
        for v in order:
            blurred = (end_y if x_first[v] else end_x)(iteration, 0, v, copies[v])
            blurred = conv_z(blurred, v, 0)
            if iteration == 0:
                aligned_wait(v)
            recorded = aligned[v].reshape(PX * PY, CZ)
            ratio = jnp.where(recorded >= 0.0, recorded / blurred, 1.0)
            back = conv_z(ratio, v, 1)
            copies[v] = (begin_x if x_first_back[v] else begin_y)(iteration, 1, v, back)
        for v in order_back:
            if x_first_back[v]:
                wait_x(x_wide.at[iteration, 1, v], copies[v])
                field = y_wide.at[iteration, 1, v]
                conv_x(x_wide.at[iteration, 1, v], v, 1, field, PY)
                copies[v] = send_y(field)
            else:
                copies[v] = begin_x(iteration, 1, v, end_y(iteration, 1, v, copies[v]))
        last = order_back[-1] if iteration + 1 == ITERS else None
        for n, v in enumerate(order_back):
            if v == last:
                break
            back = (end_y if x_first_back[v] else end_x)(iteration, 1, v, copies[v])
            term = params[0, 4 + v : 5 + v, :] * jnp.log(back)
            summed[...] = term if n == 0 else summed[...] + term
        if last is None:
            update = jnp.exp(summed[...] / total).reshape(PX, PY, CZ)
            raw_x[iteration + 1, HALF : HALF + PX] = raw_x[iteration, HALF : HALF + PX] * update
            current_copies = send_current(iteration + 1)
            continue
        for copy in copies[last]:
            copy.wait_recv()
        for c in range(2):
            planes = (c * shared, (c + 1) * shared)
            back = conv_y(y_wide.at[iteration, 1, last], last, 1, planes)
            term = params[0, 4 + last : 5 + last, :] * jnp.log(back)
            log_sum = summed[planes[0] * PY : planes[1] * PY, :] + term
            update = jnp.exp(log_sum / total).reshape(shared, PY, CZ)
            result[planes[0] : planes[1]] = (
                raw_x[iteration, HALF + planes[0] : HALF + planes[1]] * update)
            for away, copy in results[c::2]:
                pl.when(away)(copy.start)

    @pl.when(stays)
    def _():
        mate_copy.start()
        own_target[...] = result[...]

    params_finish()
    aligned_finish()
    for copy in sent:
        copy.wait_send()
    for left, right in x_sent:
        pl.when(not_first)(left.wait_send)
        pl.when(not_last)(right.wait_send)

    base_mate = new_sem(4)
    forwards = []
    for s in (2, 3, 0, 1):
        away = chip_at(zc, 2 * y_lo + s // 2) != y
        got, missing = [
            out.at[pl.ds(s // 2 * PX + c * shared, shared), piece(s % 2)] for c in (core, other)
        ]
        arrival = remote(got, got, base + s, x_left)
        forward = remote(got, got, base_mate + s, chip_mate)
        missed = remote(missing, missing, base_mate + s, chip_mate)

        @pl.when(away)
        def _(arrival=arrival, forward=forward):
            arrival.wait_recv()
            forward.start()

        forwards.append((away, forward, missed))

    @pl.when(stays)
    def _():
        mate_copy.wait()

    for away, forward, missed in forwards:

        @pl.when(away)
        def _(forward=forward, missed=missed):
            missed.wait_recv()
            forward.wait_send()

    for away, copy in results:
        pl.when(away)(copy.wait_send)


def solution(mesh):
    nz, nx = mesh.shape["bx"] // 2, mesh.shape["by"]
    f32, bf16 = jnp.float32, jnp.bfloat16

    def shards(estimate, views_raw, psf_taps, offsets, view_weights):
        vmem = pl.BlockSpec(memory_space=pltpu.VMEM)
        hbm = pl.BlockSpec(memory_space=pltpu.HBM)
        return pl.pallas_call(
            functools.partial(kernel, (nz, nx)),
            out_shape=jax.ShapeDtypeStruct((CX, CY, CZ), f32),
            in_specs=[hbm] * 5,
            out_specs=vmem,
            scratch_shapes=[
                pltpu.VMEM((ITERS, WIDE_X, PY, CZ), f32),
                pltpu.VMEM((ITERS, PX, WIDE_Y, CZ), f32),
                pltpu.VMEM((ITERS, 2, VIEWS, WIDE_X, PY, CZ), f32),
                pltpu.VMEM((ITERS, 2, VIEWS, PX, WIDE_Y, CZ), f32),
                pltpu.VMEM((VIEWS, PX, PY, CZ), f32),
                pltpu.VMEM((PX * PY, CZ), f32),
                pltpu.VMEM((PX, PY, CZ), f32),
                pltpu.VMEM((3, 1, TAPS), f32),
                pltpu.SMEM((1, 1, 1, 3), jnp.int32),
                pltpu.SMEM((1, 1, VIEWS), jnp.int32),
                pltpu.VMEM((CX + 2 * SHIFT, CY + 2 * SHIFT, CZ), f32),
                pltpu.VMEM((CX, CY, CZ), f32),
                pltpu.VMEM((VIEWS, PX, PY, CZ), f32),
                pltpu.VMEM((8, 128), f32),
                pltpu.VMEM((VIEWS, 8, 128), f32),
                pltpu.VMEM((VIEWS, TAPS, 8, CZ), f32),
                pltpu.VMEM((2, VIEWS, PY, 3 * WIDE_Y), bf16),
                pltpu.VMEM((2, VIEWS, 2 * CZ, 2 * CZ), bf16),
                pltpu.SemaphoreType.DMA((N_SEMS,)),
                pltpu.SemaphoreType.DMA((N_SEMS,)),
                pltpu.SemaphoreType.DMA((5,)),
            ],
            compiler_params=pltpu.CompilerParams(
                collective_id=0, has_side_effects=True, vmem_limit_bytes=53 * 1024 * 1024
            ),
            cost_estimate=pl.CostEstimate(flops=10**9, bytes_accessed=2 * 10**6, transcendentals=10**6),
        )(
            estimate,
            views_raw,
            jnp.transpose(psf_taps, (1, 0, 2)),
            offsets,
            jnp.transpose(view_weights, (1, 2, 0)),
        )

    return jax.shard_map(
        shards,
        mesh=mesh,
        in_specs=(
            P("bx", "by", None),
            P("view", "bx", "by", None),
            P("view", None, None),
            P("view", "bx", "by", None),
            P(None, "bx", "by"),
        ),
        out_specs=P("bx", "by", None),
        check_vma=False,
    )
```
